1024 devices in a mesh: py: 16 (over y_lo, z), pz: 64 (over y_hi, x, core).
Axes of the slice: x: 8, y: 8 (y_hi: 4, y_lo: 2; y = y_hi * 2 + y_lo), z: 8, core: 2. Of those that a mesh axis runs over, the one named last changes fastest.
Arguments:
- velocity: float32 [3, 64, 512, 256], P(None, 'py', 'pz'), may hold values from -4 to 4
- cotangent: float32 [3, 64, 512, 256], P(None, 'py', 'pz'), may hold values from -15 to 15
Outputs:
- adjoint_velocity: float32 [3, 64, 512, 256], P(None, 'py', 'pz')
The draws below stay inside these ranges and needn't reach their ends.
All inputs are finite; a program needn't handle non-finite values.
Results may differ from the reference program's by a relative error of at most 0.0003.
Values sent between devices are 32-bit elements; how exact they have to be, the bound alone decides.
No kernel may reach another device: no remote copies, remote signals or barrier semaphores. Data moves between devices by JAX's collectives and lax.ppermute only.
A program may use at most 32 MiB of HBM per device.

```python
import math
import jax
import jax.numpy as jnp

NX = 256
ITERS = 2
NY = 64
NZ = 512


def binomial_filter(field, passes):
    for sweep_index in range(passes):
        for axis_number in (1, 2, 3):
            field = 0.25 * (jnp.roll(field, 1, axis_number) + 2.0 * field + jnp.roll(field, -1, axis_number))
    return field


def draw_cotangent(key, part):
    key = jax.random.fold_in(key, 7)
    smooth_key, rough_key, phase_key = jax.random.split(key, 3)
    shape = (3, NY, NZ, NX)
    ys = (jnp.arange(NY, dtype=jnp.float32) / NY).reshape(1, NY, 1, 1)
    zs = (jnp.arange(NZ, dtype=jnp.float32) / NZ).reshape(1, 1, NZ, 1)
    xs = (jnp.arange(NX, dtype=jnp.float32) / NX).reshape(1, 1, 1, NX)
    smooth_raw = jax.random.truncated_normal(smooth_key, -4.0, 4.0, shape, jnp.float32)
    rough_raw = jax.random.truncated_normal(rough_key, -4.0, 4.0, shape, jnp.float32)
    smooth = binomial_filter(smooth_raw, 2)
    rough_scale = 0.05 + 0.2 * ys
    phases = jax.random.uniform(phase_key, (3, 1, 1, 1), jnp.float32) * 2.0 * math.pi
    envelope = 1.0 + ys + zs
    amplitude = 3.0 - ys - zs
    wave = jnp.sin(2.0 * math.pi * xs + phases) * jnp.cos(2.0 * math.pi * ys + phases) * jnp.cos(2.0 * math.pi * zs)
    return (0.75 * envelope * smooth + rough_scale * rough_raw + amplitude * wave).astype(jnp.float32)


def shard_levels(rng, extent, shards, smallest, largest):
    def one(axis_at, blocks):
        heights = jax.random.uniform(jax.random.fold_in(jax.random.fold_in(rng, 6), axis_at), (blocks,), jnp.float32, smallest / len(shards), largest / len(shards))
        return jnp.repeat(jnp.exp(heights), extent[axis_at] // blocks).reshape((-1,) + (1,) * (len(extent) - axis_at - 1))

    loudness = one(*shards[0])
    for cut in shards[1:]:
        loudness = loudness * one(*cut)
    return loudness


def gaussian(own_key, shape, scale, reach, cuts=(), held_as=jnp.bfloat16):
    array = scale * jax.random.normal(own_key, shape, jnp.float32)
    if cuts:
        array = array * shard_levels(own_key, shape, cuts, -0.22, 0.18)
    return jnp.clip(array, -reach, reach).astype(held_as)


def setup_inputs(seed: int = 0) -> dict:
    keys = jax.random.split(jax.random.key(seed), 3)
    return {
        "velocity": gaussian(keys[0], (3, NY, NZ, NX), 1.0, 4.0, ((1, 16), (2, 64)), jnp.float32),
        "cotangent": draw_cotangent(jax.random.fold_in(keys[2], 71), 0),
    }


smag_coef = 0.1156
time_step = 0.2
strain_floor = 0.25

def along_x(f):
    return (0.5 * (jnp.roll(f, -1, -1) - jnp.roll(f, 1, -1)))[..., 1:-1, 1:-1, :]

def along_y(f):
    return 0.5 * (f[..., 2:, 1:-1, :] - f[..., :-2, 1:-1, :])

def along_z(f):
    return 0.5 * (f[..., 1:-1, 2:, :] - f[..., 1:-1, :-2, :])

def trimmed(f):
    return f[..., 1:-1, 1:-1, :]

def tendency(velocity):
    gradients = [[along_x(velocity[i]), along_y(velocity[i]), along_z(velocity[i])] for i in range(3)]
    strain = [[0.5 * (gradients[i][j] + gradients[j][i]) for j in range(3)] for i in range(3)]
    squares = strain[0][0] * strain[0][0]
    for i in range(3):
        for j in range(3):
            if i + j > 0:
                squares = squares + strain[i][j] * strain[i][j]
    viscosity = smag_coef * jnp.sqrt(2.0 * squares + strain_floor)
    centred = trimmed(velocity)
    pieces = []
    for i in range(3):
        advect = centred[0] * gradients[i][0] + centred[1] * gradients[i][1] + centred[2] * gradients[i][2]
        fluxes = [2.0 * viscosity * strain[i][j] for j in range(3)]
        diffuse = along_x(fluxes[0]) + along_y(fluxes[1]) + along_z(fluxes[2])
        pieces.append(time_step * (diffuse - trimmed(advect)))
    return jnp.stack(pieces)

def divergence(field):
    return along_x(field[0]) + along_y(field[1]) + along_z(field[2])

def gradient(scalar):
    return jnp.stack([along_x(scalar), along_y(scalar), along_z(scalar)])

def operate_padded(padded):
    centre = trimmed(padded)
    beside = jnp.roll(centre, 1, -1) + jnp.roll(centre, -1, -1)
    beside = beside + padded[2:, 1:-1, :] + padded[:-2, 1:-1, :]
    beside = beside + padded[1:-1, 2:, :] + padded[1:-1, :-2, :]
    return 6.0 * centre - beside

def periodic(field, width):
    pads = [(0, 0)] * (field.ndim - 3) + [(width, width), (width, width), (0, 0)]
    return jnp.pad(field, pads, mode='wrap')

def reference(velocity, cotangent):
    right_side = -divergence(periodic(cotangent, 1))
    pressure = jnp.zeros_like(right_side)
    residual = right_side
    direction = right_side
    norm_now = jnp.sum(residual * residual)
    for iteration in range(ITERS):
        image_field = operate_padded(periodic(direction, 1))
        step_size = norm_now / jnp.sum(direction * image_field)
        pressure = pressure + step_size * direction
        if iteration + 1 < ITERS:
            residual = residual - step_size * image_field
            norm_next = jnp.sum(residual * residual)
            direction = residual + norm_next / norm_now * direction
            norm_now = norm_next
    projected = cotangent - gradient(periodic(pressure, 1))

    def forward(field):
        return tendency(periodic(field, 2))
    outputs, pullback = jax.vjp(forward, velocity)
    adjoint_term = pullback(projected)[0]
    return projected + adjoint_term
```

```python
import functools

import jax
import jax.numpy as jnp
from jax import lax
from jax.experimental import pallas as pl
from jax.experimental.pallas import tpu as pltpu
from jax.sharding import PartitionSpec as P

smag_coef = 0.1156
time_step = 0.2
strain_floor = 0.25

ROWS = 4
TILE = 8
SIDE = 4
WIDE = TILE + 2 * SIDE
SENT = 9


def rolled(x, shift, axis):
    return pltpu.roll(x, shift % x.shape[axis], axis)


def dx(f):
    n = f.ndim - 1
    return 0.5 * (rolled(f, -1, n) - rolled(f, 1, n))


def dz(f):
    n = f.ndim - 2
    return 0.5 * (rolled(f, -1, n) - rolled(f, 1, n))


def sublane():
    return lax.broadcasted_iota(jnp.int32, (TILE, 256), 0)


def pack_z(cot_ref, vel_ref, prev_ref, next_ref):
    row = sublane()
    for c in range(3):
        for y in range(ROWS):
            cot, vel = cot_ref[c, y], vel_ref[c, y]
            prev_ref[c, y] = jnp.where(row < 5, cot, rolled(vel, 5, 0))
            next_ref[c, y] = jnp.where(row >= 3, cot, rolled(vel, 3, 0))


def side_cot(row, zn, zp):
    return jnp.where(row < SIDE, zn, zp)


def side_vel(row, zn, zp):
    return jnp.where(row < SIDE, rolled(zn, 3, 0), rolled(zp, 5, 0))


def pack_y(cot_ref, vel_ref, zn_ref, zp_ref, prev_ref, next_ref):
    row = sublane()
    for out, order in ((prev_ref, (0, 1, 2, 3)), (next_ref, (3, 2, 1, 0))):
        for c in range(3):
            side = [side_cot(row, zn_ref[c, y], zp_ref[c, y]) for y in order]
            near = side_vel(row, zn_ref[c, order[0]], zp_ref[c, order[0]])
            for d in range(4):
                out[c, d] = cot_ref[c, order[d]]
            out[c, 4] = side[0]
            far = jnp.where(row == 4, rolled(side[3], 5, 0), side[1])
            out[c, 5] = jnp.where(row == 3, rolled(side[3], 3, 0), far)
            mid = jnp.where(row == 5, rolled(near, 6, 0), side[2])
            out[c, 6] = jnp.where(row == 2, rolled(near, 2, 0), mid)
            out[c, 7] = vel_ref[c, order[0]]
            out[c, 8] = vel_ref[c, order[1]]


def joined(a, b):
    return jnp.concatenate([a, b], axis=0)


def cot_frame(refs, row, c, y):
    cot_ref, vel_ref, zn_ref, zp_ref, yn_ref, yp_ref = refs
    if 0 <= y < ROWS:
        return joined(cot_ref[c, y], side_cot(row, zn_ref[c, y], zp_ref[c, y]))
    got, d = (yn_ref, y - ROWS) if y >= ROWS else (yp_ref, -1 - y)
    if d < 3:
        return joined(got[c, d], got[c, 4 + d])
    tile = got[c, 5]
    return joined(got[c, 3], jnp.where(row < SIDE, rolled(tile, 5, 0), rolled(tile, 3, 0)))


def vel_frame(refs, row, c, y):
    cot_ref, vel_ref, zn_ref, zp_ref, yn_ref, yp_ref = refs
    if 0 <= y < ROWS:
        return joined(vel_ref[c, y], side_vel(row, zn_ref[c, y], zp_ref[c, y]))
    got, d = (yn_ref, y - ROWS) if y >= ROWS else (yp_ref, -1 - y)
    if d == 0:
        tile = got[c, 6]
        return joined(got[c, 7], jnp.where(row < SIDE, rolled(tile, 6, 0), rolled(tile, 2, 0)))
    return joined(got[c, 8], got[c, 8])


def along_z_cot(refs, row, frame, y):
    if not 0 <= y < ROWS:
        return dz(frame)
    zn_ref, zp_ref = refs[2], refs[3]
    ends = jnp.where(row < SIDE, zp_ref[2, y], zn_ref[2, y])
    wide = lax.broadcasted_iota(jnp.int32, (WIDE, 256), 0)
    both = joined(ends, ends)
    after = jnp.where(wide == TILE + 3, rolled(both, -1, 0), rolled(frame, -1, 0))
    before = jnp.where(wide == TILE + 4, rolled(both, 1, 0), rolled(frame, 1, 0))
    return 0.5 * (after - before)


def laplace(here, below, above):
    beside = rolled(here, 1, 1) + rolled(here, -1, 1)
    beside = beside + above + below
    beside = beside + rolled(here, 1, 0) + rolled(here, -1, 0)
    return 6.0 * here - beside


def ratio(top, bottom):
    safe = bottom > 0.0
    return jnp.where(safe, top / jnp.where(safe, bottom, 1.0), 0.0)


def total(x):
    return jnp.sum(jnp.sum(x, axis=0, keepdims=True), axis=1, keepdims=True)


def moments(peers, place_ref, cot_ref, vel_ref, zn_ref, zp_ref, yn_ref, yp_ref, out_ref, b_ref, w_ref):
    refs = (cot_ref, vel_ref, zn_ref, zp_ref, yn_ref, yp_ref)
    row = sublane()
    cot_y = {y: cot_frame(refs, row, 1, y) for y in range(-4, 8)}
    b = {}
    for y in range(-3, 7):
        flat = dx(cot_frame(refs, row, 0, y)) + along_z_cot(refs, row, cot_frame(refs, row, 2, y), y)
        b[y] = -(flat + 0.5 * (cot_y[y + 1] - cot_y[y - 1]))
        b_ref[y + 3] = b[y]
    w = {}
    for y in range(-2, 6):
        w[y] = laplace(b[y], b[y - 1], b[y + 1])
        w_ref[y + 2] = w[y]
    m0 = m1 = None
    for y in range(ROWS):
        bc, wc = b[y][:TILE], w[y][:TILE]
        m0 = bc * bc if m0 is None else m0 + bc * bc
        m1 = bc * wc if m1 is None else m1 + bc * wc
    m0, m1 = total(m0), total(m1)
    sigma = ratio(m1, m0)
    spread = third = cross = None
    for y in range(ROWS):
        bc, wc = b[y][:TILE], w[y][:TILE]
        x = laplace(w[y], w[y - 1], w[y + 1])[:TILE]
        v = wc - sigma * bc
        u = x - sigma * wc
        spread = v * v if spread is None else spread + v * v
        third = v * u if third is None else third + v * u
        cross = bc * u if cross is None else cross + bc * u
    spread, third, cross = total(spread), total(third), total(cross)
    line = lax.broadcasted_iota(jnp.int32, (TILE, 128), 0)
    tile = jnp.zeros((TILE, 128), jnp.float32)
    for k, value in enumerate((m0, m1, spread, third, cross)):
        tile = jnp.where(line == k, value, tile)
    place = place_ref[0]
    for j in range(peers):
        ahead = lax.rem(j - place + peers, peers)
        up = jnp.where(ahead < peers // 2, 1.0, 0.0)
        out_ref[j, :, :256] = jnp.where(up > 0.5, cot_ref[1, ROWS - 1], cot_ref[1, 0])
        out_ref[j, :, 256:] = tile


def merged(m0, m1, spread, third, cross):
    own = ratio(m1, m0)

    def over(x):
        return jnp.sum(x, axis=0, keepdims=True)

    all0, all1 = over(m0), over(m1)
    delta = ratio(all1, all0) - own
    all_spread = over(spread + delta * delta * m0)
    all_third = over(third - delta * (spread + cross) + delta * delta * m1)
    all_cross = over(cross - delta * m1)
    return all0, all1, all_spread, all_third, all_cross


def merge(got_ref, out_ref):
    parts = merged(*[got_ref[:, k, 256:] for k in range(5)])
    lane = lax.broadcasted_iota(jnp.int32, (1, 128), 1)
    line = jnp.zeros((1, 128), jnp.float32)
    for k, value in enumerate(parts):
        line = jnp.where(lane == k, value, line)
    for j in range(out_ref.shape[0]):
        out_ref[j] = line


def finish(peers, place_ref, cot_ref, vel_ref, zn_ref, zp_ref, yn_ref, yp_ref, far_ref, b_ref, w_ref, sums_ref, out_ref):
    refs = (cot_ref, vel_ref, zn_ref, zp_ref, yn_ref, yp_ref)
    row = sublane()
    sums = sums_ref[...].reshape(sums_ref.shape[0], 128)
    m0, m1, spread, third, _ = [x[:, :1] for x in merged(*[rolled(sums, -k, 1) for k in range(5)])]
    step0 = m0 / m1
    norm1 = step0 * step0 * spread
    beta = norm1 / m0
    bend = step0 * step0 * third - 2.0 * step0 * beta * spread + beta * beta * m1
    step1 = norm1 / bend
    coef_b = step0 + step1 * (1.0 + beta)
    coef_w = -(step1 * step0)

    place = place_ref[0]
    above = far_ref[lax.rem(place + 2, peers), :, :256]
    below = far_ref[lax.rem(place + peers - 2, peers), :, :256]
    above, below = joined(above, above), joined(below, below)
    cot = {(c, y): cot_frame(refs, row, c, y) for c in range(3) for y in range(-4, 8)}
    b = {y: b_ref[y + 3] for y in range(-3, 7)}
    b[-4] = -(dx(cot[0, -4]) + dz(cot[2, -4]) + 0.5 * (cot[1, -3] - below))
    b[7] = -(dx(cot[0, 7]) + dz(cot[2, 7]) + 0.5 * (above - cot[1, 6]))
    w = {y: w_ref[y + 2] for y in range(-2, 6)}
    w[-3] = laplace(b[-3], b[-4], b[-2])
    w[6] = laplace(b[6], b[5], b[7])
    p = {y: coef_b * b[y] + coef_w * w[y] for y in range(-3, 7)}
    lam = {}
    for y in range(-2, 6):
        lam[0, y] = cot[0, y] - dx(p[y])
        lam[1, y] = cot[1, y] - 0.5 * (p[y + 1] - p[y - 1])
        lam[2, y] = cot[2, y] - dz(p[y])
    vel = {(c, y): vel_frame(refs, row, c, y) for c in range(3) for y in range(-2, 6)}

    flat, upright = {}, {}
    for y in range(-1, 5):
        grad = [[dx(vel[i, y]), 0.5 * (vel[i, y + 1] - vel[i, y - 1]), dz(vel[i, y])] for i in range(3)]
        pull = [[dx(lam[i, y]), 0.5 * (lam[i, y + 1] - lam[i, y - 1]), dz(lam[i, y])] for i in range(3)]
        strain, ebb = {}, {}
        for i in range(3):
            for j in range(i + 1):
                strain[i, j] = grad[i][i] if i == j else 0.5 * (grad[i][j] + grad[j][i])
                ebb[i, j] = pull[i][i] if i == j else 0.5 * (pull[i][j] + pull[j][i])
        squares = strain[0, 0] * strain[0, 0] + strain[1, 1] * strain[1, 1] + strain[2, 2] * strain[2, 2]
        work = strain[0, 0] * ebb[0, 0] + strain[1, 1] * ebb[1, 1] + strain[2, 2] * ebb[2, 2]
        off = strain[1, 0] * strain[1, 0] + strain[2, 0] * strain[2, 0] + strain[2, 1] * strain[2, 1]
        off_work = strain[1, 0] * ebb[1, 0] + strain[2, 0] * ebb[2, 0] + strain[2, 1] * ebb[2, 1]
        inside = 2.0 * (squares + 2.0 * off) + strain_floor
        inverse = lax.rsqrt(inside)
        twice = (2.0 * smag_coef) * (inside * inverse)
        factor = (4.0 * smag_coef) * inverse * (work + 2.0 * off_work)
        stress = {key: twice * ebb[key] + factor * strain[key] for key in strain}

        def both(i, j):
            return stress[max(i, j), min(i, j)] + lam[i, y] * vel[j, y]

        for i in range(3):
            upright[i, y] = both(i, 1)[:TILE]
        if 0 <= y < ROWS:
            for i in range(3):
                carried = lam[0, y] * grad[0][i] + lam[1, y] * grad[1][i] + lam[2, y] * grad[2][i]
                level = dx(both(i, 0)) + dz(both(i, 2))
                flat[i, y] = (lam[i, y] + time_step * (level - carried))[:TILE]
    for i in range(3):
        for y in range(ROWS):
            out_ref[i, y] = flat[i, y] + (0.5 * time_step) * (upright[i, y + 1] - upright[i, y - 1])


def call(kernel, outs, scalars, arrays):
    vmem = pl.BlockSpec(memory_space=pltpu.VMEM)
    smem = pl.BlockSpec(memory_space=pltpu.SMEM)
    return pl.pallas_call(
        kernel,
        out_shape=[jax.ShapeDtypeStruct(s, jnp.float32) for s in outs],
        in_specs=[smem] * len(scalars) + [vmem] * len(arrays),
        out_specs=[vmem] * len(outs),
        compiler_params=pltpu.CompilerParams(vmem_limit_bytes=32 * 1024 * 1024),
    )(*scalars, *arrays)


def both_ways(to_prev, to_next, axis):
    n = lax.axis_size(axis)
    up = [(i, (i + 1) % n) for i in range(n)]
    down = [(j, i) for i, j in up]
    from_next = lax.ppermute(to_prev, axis, down)
    from_prev = lax.ppermute(to_next, axis, up)
    return from_next, from_prev


def body(velocity, cotangent):
    ny, nz = lax.axis_size("py"), lax.axis_size("pz")
    place = lax.axis_index("py").astype(jnp.int32).reshape(1)
    block = (3, ROWS, TILE, 256)
    to_prev, to_next = call(pack_z, [block, block], [], [cotangent, velocity])
    zn, zp = both_ways(to_prev, to_next, "pz")
    sent = (3, SENT, TILE, 256)
    to_prev, to_next = call(pack_y, [sent, sent], [], [cotangent, velocity, zn, zp])
    yn, yp = both_ways(to_prev, to_next, "py")
    held = [cotangent, velocity, zn, zp, yn, yp]
    chunks, b, w = call(
        functools.partial(moments, ny),
        [(ny, TILE, 384), (10, WIDE, 256), (8, WIDE, 256)],
        [place],
        held,
    )
    got = lax.all_to_all(chunks, "py", 0, 0)
    (lines,) = call(merge, [(nz, 1, 128)], [], [got])
    sums = lax.all_to_all(lines, "pz", 0, 0)
    (out,) = call(functools.partial(finish, ny), [block], [place], held + [got, b, w, sums])
    return out


def solution(mesh):
    placed = (P(None, "py", "pz", None), P(None, "py", "pz", None))
    return jax.shard_map(
        body, mesh=mesh, in_specs=placed, out_specs=P(None, "py", "pz", None), check_vma=False
    )
```

```python
import functools

import jax
import jax.numpy as jnp
from jax import lax
from jax.experimental import pallas as pl
from jax.experimental.pallas import tpu as pltpu
from jax.sharding import PartitionSpec as P

smag_coef = 0.1156
time_step = 0.2
strain_floor = 0.25

ROWS = 4
TILE = 8
SIDE = 4
WIDE = TILE + 2 * SIDE
SENT = 20


def rolled(x, shift, axis):
    return pltpu.roll(x, shift % x.shape[axis], axis)


def dx(f):
    n = f.ndim - 1
    return 0.5 * (rolled(f, -1, n) - rolled(f, 1, n))


def dz(f):
    n = f.ndim - 2
    return 0.5 * (rolled(f, -1, n) - rolled(f, 1, n))


def sublane():
    return lax.broadcasted_iota(jnp.int32, (TILE, 256), 0)


def pack_z(cot_hbm, vel_hbm, prev_ref, next_ref, cot_ref, vel_ref, sems):
    copies = [
        pltpu.make_async_copy(cot_hbm, cot_ref, sems.at[0]),
        pltpu.make_async_copy(vel_hbm, vel_ref, sems.at[1]),
    ]
    for copy in copies:
        copy.start()
    for copy in copies:
        copy.wait()
    row = sublane()
    for c in range(3):
        for y in range(ROWS):
            cot, vel = cot_ref[c, y], vel_ref[c, y]
            prev_ref[c, y] = jnp.where(row < 5, cot, rolled(vel, 5, 0))
            next_ref[c, y] = jnp.where(row >= 3, cot, rolled(vel, 3, 0))


def side_cot(row, zn, zp):
    return jnp.where(row < SIDE, zn, zp)


def side_vel(row, zn, zp):
    return jnp.where(row < SIDE, rolled(zn, 3, 0), rolled(zp, 5, 0))


def put(row, tile, k):
    return jnp.where(row < SIDE, rolled(tile, k, 0), rolled(tile, -k, 0))


def take(row, tile, k):
    return jnp.where(row < SIDE, rolled(tile, -k, 0), rolled(tile, k, 0))


def mixed(row, base, inner):
    for k, tile in inner:
        base = jnp.where((row == k) | (row == TILE - 1 - k), put(row, tile, k), base)
    return base


def joined(a, b):
    return jnp.concatenate([a, b], axis=0)


def pack_y(cot_ref, vel_ref, zn_ref, zp_ref, prev_ref, next_ref):
    refs = (cot_ref, vel_ref, zn_ref, zp_ref, None, None)
    row = sublane()
    cot = {(c, y): cot_frame(refs, row, c, y) for c in range(3) for y in range(ROWS)}
    flat = {y: -(dx(cot[0, y]) + along_z_cot(refs, row, cot[2, y], y)) for y in range(ROWS)}
    low = flat[0] - 0.5 * cot[1, 1]
    high = flat[3] + 0.5 * cot[1, 2]
    one = flat[1] - 0.5 * (cot[1, 2] - cot[1, 0])
    two = flat[2] - 0.5 * (cot[1, 3] - cot[1, 1])
    for out, part, (d1, d2) in (
        (prev_ref, (low, one, two, high), (0, 1)),
        (next_ref, (high, two, one, low), (3, 2)),
    ):
        for d in range(4):
            out[d] = part[d][:TILE]
        for c in range(3):
            out[4 + c] = cot_ref[c, d1]
            out[7 + c] = cot_ref[c, d2]
            out[10 + c] = vel_ref[c, d1]
            out[13 + c] = vel_ref[c, d2]
        vel = [side_vel(row, zn_ref[c, d1], zp_ref[c, d1]) for c in range(3)]
        out[16] = mixed(row, part[0][TILE:], [(3, part[2][TILE:])])
        out[17] = mixed(row, part[1][TILE:], [(2, cot[0, d1][TILE:]), (3, cot[2, d1][TILE:])])
        out[18] = mixed(row, vel[0], [(1, vel[1]), (2, vel[2])])
        out[19] = cot[1, d1][TILE:]


def cot_frame(refs, row, c, y):
    cot_ref, vel_ref, zn_ref, zp_ref, yn_ref, yp_ref = refs
    if 0 <= y < ROWS:
        return joined(cot_ref[c, y], side_cot(row, zn_ref[c, y], zp_ref[c, y]))
    got, d = (yn_ref, y - ROWS) if y >= ROWS else (yp_ref, -1 - y)
    if d == 1:
        return joined(got[7 + c], got[7 + c])
    return joined(got[4 + c], got[19] if c == 1 else take(row, got[17], 2 if c == 0 else 3))


def vel_frame(refs, row, c, y):
    cot_ref, vel_ref, zn_ref, zp_ref, yn_ref, yp_ref = refs
    if 0 <= y < ROWS:
        return joined(vel_ref[c, y], side_vel(row, zn_ref[c, y], zp_ref[c, y]))
    got, d = (yn_ref, y - ROWS) if y >= ROWS else (yp_ref, -1 - y)
    if d == 1:
        return joined(got[13 + c], got[13 + c])
    return joined(got[10 + c], take(row, got[18], c))


def part_frame(refs, row, y):
    got, d = (refs[4], y - ROWS) if y >= ROWS else (refs[5], -1 - y)
    if d == 0:
        return joined(got[0], got[16])
    if d == 1:
        return joined(got[1], got[17])
    if d == 2:
        return joined(got[2], take(row, got[16], 3))
    return joined(got[3], got[3])


def along_z_cot(refs, row, frame, y):
    if not 0 <= y < ROWS:
        return dz(frame)
    zn_ref, zp_ref = refs[2], refs[3]
    ends = jnp.where(row < SIDE, zp_ref[2, y], zn_ref[2, y])
    wide = lax.broadcasted_iota(jnp.int32, (WIDE, 256), 0)
    both = joined(ends, ends)
    after = jnp.where(wide == TILE + 3, rolled(both, -1, 0), rolled(frame, -1, 0))
    before = jnp.where(wide == TILE + 4, rolled(both, 1, 0), rolled(frame, 1, 0))
    return 0.5 * (after - before)


def laplace(here, below, above):
    beside = rolled(here, 1, 1) + rolled(here, -1, 1)
    beside = beside + above + below
    beside = beside + rolled(here, 1, 0) + rolled(here, -1, 0)
    return 6.0 * here - beside


def ratio(top, bottom):
    safe = bottom > 0.0
    return jnp.where(safe, top / jnp.where(safe, bottom, 1.0), 0.0)


def total(x):
    return jnp.sum(jnp.sum(x, axis=0, keepdims=True), axis=1, keepdims=True)


def moments(peers, place_ref, cot_ref, vel_ref, zn_ref, zp_ref, yn_ref, yp_ref, out_ref, b_ref, w_ref):
    refs = (cot_ref, vel_ref, zn_ref, zp_ref, yn_ref, yp_ref)
    row = sublane()
    cot_y = {y: cot_frame(refs, row, 1, y) for y in range(-1, 5)}
    b = {y: part_frame(refs, row, y) for y in (-3, -2, -1, 4, 5, 6)}
    b[-1] = b[-1] - 0.5 * cot_y[0]
    b[4] = b[4] + 0.5 * cot_y[3]
    for y in range(ROWS):
        flat = dx(cot_frame(refs, row, 0, y)) + along_z_cot(refs, row, cot_frame(refs, row, 2, y), y)
        b[y] = -(flat + 0.5 * (cot_y[y + 1] - cot_y[y - 1]))
    for y in range(-3, 7):
        b_ref[y + 3] = b[y]
    w = {}
    for y in range(-2, 6):
        w[y] = laplace(b[y], b[y - 1], b[y + 1])
        w_ref[y + 2] = w[y]
    m0 = m1 = None
    for y in range(ROWS):
        bc, wc = b[y][:TILE], w[y][:TILE]
        m0 = bc * bc if m0 is None else m0 + bc * bc
        m1 = bc * wc if m1 is None else m1 + bc * wc
    m0, m1 = total(m0), total(m1)
    sigma = ratio(m1, m0)
    spread = third = cross = None
    for y in range(ROWS):
        bc, wc = b[y][:TILE], w[y][:TILE]
        x = laplace(w[y], w[y - 1], w[y + 1])[:TILE]
        v = wc - sigma * bc
        u = x - sigma * wc
        spread = v * v if spread is None else spread + v * v
        third = v * u if third is None else third + v * u
        cross = bc * u if cross is None else cross + bc * u
    spread, third, cross = total(spread), total(third), total(cross)
    line = lax.broadcasted_iota(jnp.int32, (TILE, 128), 0)
    tile = jnp.zeros((TILE, 128), jnp.float32)
    for k, value in enumerate((m0, m1, spread, third, cross)):
        tile = jnp.where(line == k, value, tile)
    place = place_ref[0]
    for j in range(peers):
        ahead = lax.rem(j - place + peers, peers)
        up = jnp.where(ahead < peers // 2, 1.0, 0.0)
        out_ref[j, :, :256] = jnp.where(up > 0.5, cot_ref[1, ROWS - 1], cot_ref[1, 0])
        out_ref[j, :, 256:] = tile


def merged(m0, m1, spread, third, cross):
    own = ratio(m1, m0)

    def over(x):
        return jnp.sum(x, axis=0, keepdims=True)

    all0, all1 = over(m0), over(m1)
    delta = ratio(all1, all0) - own
    all_spread = over(spread + delta * delta * m0)
    all_third = over(third - delta * (spread + cross) + delta * delta * m1)
    all_cross = over(cross - delta * m1)
    return all0, all1, all_spread, all_third, all_cross


def merge(got_ref, out_ref):
    parts = merged(*[got_ref[:, k, 256:] for k in range(5)])
    lane = lax.broadcasted_iota(jnp.int32, (1, 128), 1)
    line = jnp.zeros((1, 128), jnp.float32)
    for k, value in enumerate(parts):
        line = jnp.where(lane == k, value, line)
    for j in range(out_ref.shape[0]):
        out_ref[j] = line


def finish(peers, place_ref, cot_ref, vel_ref, zn_ref, zp_ref, yn_ref, yp_ref, far_ref, b_ref, w_ref, sums_ref, out_ref):
    refs = (cot_ref, vel_ref, zn_ref, zp_ref, yn_ref, yp_ref)
    row = sublane()
    sums = sums_ref[...].reshape(sums_ref.shape[0], 128)
    m0, m1, spread, third, _ = [x[:, :1] for x in merged(*[rolled(sums, -k, 1) for k in range(5)])]
    step0 = m0 / m1
    norm1 = step0 * step0 * spread
    beta = norm1 / m0
    bend = step0 * step0 * third - 2.0 * step0 * beta * spread + beta * beta * m1
    step1 = norm1 / bend
    coef_b = step0 + step1 * (1.0 + beta)
    coef_w = -(step1 * step0)

    place = place_ref[0]
    above = far_ref[lax.rem(place + 2, peers), :, :256]
    below = far_ref[lax.rem(place + peers - 2, peers), :, :256]
    above, below = joined(above, above), joined(below, below)
    cot = {(c, y): cot_frame(refs, row, c, y) for c in range(3) for y in range(-2, 6)}
    b = {y: b_ref[y + 3] for y in range(-3, 7)}
    b[-4] = part_frame(refs, row, -4) + 0.5 * below
    b[7] = part_frame(refs, row, 7) - 0.5 * above
    w = {y: w_ref[y + 2] for y in range(-2, 6)}
    w[-3] = laplace(b[-3], b[-4], b[-2])
    w[6] = laplace(b[6], b[5], b[7])
    p = {y: coef_b * b[y] + coef_w * w[y] for y in range(-3, 7)}
    lam = {}
    for y in range(-2, 6):
        lam[0, y] = cot[0, y] - dx(p[y])
        lam[1, y] = cot[1, y] - 0.5 * (p[y + 1] - p[y - 1])
        lam[2, y] = cot[2, y] - dz(p[y])
    vel = {(c, y): vel_frame(refs, row, c, y) for c in range(3) for y in range(-2, 6)}

    flat, upright = {}, {}
    for y in range(-1, 5):
        grad = [[dx(vel[i, y]), 0.5 * (vel[i, y + 1] - vel[i, y - 1]), dz(vel[i, y])] for i in range(3)]
        pull = [[dx(lam[i, y]), 0.5 * (lam[i, y + 1] - lam[i, y - 1]), dz(lam[i, y])] for i in range(3)]
        strain, ebb = {}, {}
        for i in range(3):
            for j in range(i + 1):
                strain[i, j] = grad[i][i] if i == j else 0.5 * (grad[i][j] + grad[j][i])
                ebb[i, j] = pull[i][i] if i == j else 0.5 * (pull[i][j] + pull[j][i])
        squares = strain[0, 0] * strain[0, 0] + strain[1, 1] * strain[1, 1] + strain[2, 2] * strain[2, 2]
        work = strain[0, 0] * ebb[0, 0] + strain[1, 1] * ebb[1, 1] + strain[2, 2] * ebb[2, 2]
        off = strain[1, 0] * strain[1, 0] + strain[2, 0] * strain[2, 0] + strain[2, 1] * strain[2, 1]
        off_work = strain[1, 0] * ebb[1, 0] + strain[2, 0] * ebb[2, 0] + strain[2, 1] * ebb[2, 1]
        inside = 2.0 * (squares + 2.0 * off) + strain_floor
        inverse = lax.rsqrt(inside)
        twice = (2.0 * smag_coef) * (inside * inverse)
        factor = (4.0 * smag_coef) * inverse * (work + 2.0 * off_work)
        stress = {key: twice * ebb[key] + factor * strain[key] for key in strain}

        def both(i, j):
            return stress[max(i, j), min(i, j)] + lam[i, y] * vel[j, y]

        for i in range(3):
            upright[i, y] = both(i, 1)[:TILE]
        if 0 <= y < ROWS:
            for i in range(3):
                carried = lam[0, y] * grad[0][i] + lam[1, y] * grad[1][i] + lam[2, y] * grad[2][i]
                level = dx(both(i, 0)) + dz(both(i, 2))
                flat[i, y] = (lam[i, y] + time_step * (level - carried))[:TILE]
    for i in range(3):
        for y in range(ROWS):
            out_ref[i, y] = flat[i, y] + (0.5 * time_step) * (upright[i, y + 1] - upright[i, y - 1])


def call(kernel, outs, scalars, arrays, place=pltpu.VMEM, scratch=()):
    vmem = pl.BlockSpec(memory_space=pltpu.VMEM)
    given = pl.BlockSpec(memory_space=place)
    smem = pl.BlockSpec(memory_space=pltpu.SMEM)
    return pl.pallas_call(
        kernel,
        out_shape=[jax.ShapeDtypeStruct(s, jnp.float32) for s in outs],
        in_specs=[smem] * len(scalars) + [given] * len(arrays),
        out_specs=[vmem] * len(outs),
        scratch_shapes=list(scratch),
        compiler_params=pltpu.CompilerParams(vmem_limit_bytes=32 * 1024 * 1024),
    )(*scalars, *arrays)


def both_ways(to_prev, to_next, axis):
    n = lax.axis_size(axis)
    up = [(i, (i + 1) % n) for i in range(n)]
    down = [(j, i) for i, j in up]
    from_next = lax.ppermute(to_prev, axis, down)
    from_prev = lax.ppermute(to_next, axis, up)
    return from_next, from_prev


def body(velocity, cotangent):
    ny, nz = lax.axis_size("py"), lax.axis_size("pz")
    place = lax.axis_index("py").astype(jnp.int32).reshape(1)
    block = (3, ROWS, TILE, 256)
    dmas = [pltpu.SemaphoreType.DMA((2,))]
    to_prev, to_next, cotangent, velocity = call(
        pack_z, [block] * 4, [], [cotangent, velocity], pl.ANY, dmas
    )
    zn, zp = both_ways(to_prev, to_next, "pz")
    sent = (SENT, TILE, 256)
    to_prev, to_next = call(pack_y, [sent, sent], [], [cotangent, velocity, zn, zp])
    yn, yp = both_ways(to_prev, to_next, "py")
    held = [cotangent, velocity, zn, zp, yn, yp]
    chunks, b, w = call(
        functools.partial(moments, ny),
        [(ny, TILE, 384), (10, WIDE, 256), (8, WIDE, 256)],
        [place],
        held,
    )
    got = lax.all_to_all(chunks, "py", 0, 0)
    (lines,) = call(merge, [(nz, 1, 128)], [], [got])
    sums = lax.all_to_all(lines, "pz", 0, 0)
    (out,) = call(functools.partial(finish, ny), [block], [place], held + [got, b, w, sums])
    return out


def solution(mesh):
    placed = (P(None, "py", "pz", None), P(None, "py", "pz", None))
    return jax.shard_map(
        body, mesh=mesh, in_specs=placed, out_specs=P(None, "py", "pz", None), check_vma=False
    )
```

```python
import functools

import jax
import jax.numpy as jnp
from jax import lax
from jax.experimental import pallas as pl
from jax.experimental.pallas import tpu as pltpu
from jax.sharding import PartitionSpec as P

smag_coef = 0.1156
time_step = 0.2
strain_floor = 0.25

ROWS = 4
TILE = 8
SIDE = 4
WIDE = TILE + 2 * SIDE
SENT = 20


def rolled(x, shift, axis):
    return pltpu.roll(x, shift % x.shape[axis], axis)


def dx(f):
    n = f.ndim - 1
    return 0.5 * (rolled(f, -1, n) - rolled(f, 1, n))


def dz(f):
    n = f.ndim - 2
    return 0.5 * (rolled(f, -1, n) - rolled(f, 1, n))


def sublane():
    return lax.broadcasted_iota(jnp.int32, (TILE, 256), 0)


def pack_z(odd_ref, cot_hbm, vel_hbm, cross_ref, core_ref, cot_ref, vel_ref, sems):
    copies = [
        pltpu.make_async_copy(cot_hbm, cot_ref, sems.at[0]),
        pltpu.make_async_copy(vel_hbm, vel_ref, sems.at[1]),
    ]
    for copy in copies:
        copy.start()
    for copy in copies:
        copy.wait()
    row = sublane()
    even = odd_ref[0] == 0
    for c in range(3):
        for y in range(ROWS):
            cot, vel = cot_ref[c, y], vel_ref[c, y]
            to_prev = jnp.where(row < 5, cot, rolled(vel, 5, 0))
            to_next = jnp.where(row >= 3, cot, rolled(vel, 3, 0))
            cross_ref[c, y] = jnp.where(even, to_prev, to_next)
            core_ref[c, y] = jnp.where(even, to_next, to_prev)


def side_cot(row, zn, zp):
    return jnp.where(row < SIDE, zn, zp)


def side_vel(row, zn, zp):
    return jnp.where(row < SIDE, rolled(zn, 3, 0), rolled(zp, 5, 0))


def put(row, tile, k):
    return jnp.where(row < SIDE, rolled(tile, k, 0), rolled(tile, -k, 0))


def take(row, tile, k):
    return jnp.where(row < SIDE, rolled(tile, -k, 0), rolled(tile, k, 0))


def mixed(row, base, inner):
    for k, tile in inner:
        base = jnp.where((row == k) | (row == TILE - 1 - k), put(row, tile, k), base)
    return base


def joined(a, b):
    return jnp.concatenate([a, b], axis=0)


def pack_y(odd_ref, cot_ref, vel_ref, cross_ref, core_ref, prev_ref, next_ref, zn_ref, zp_ref):
    even = odd_ref[0] == 0
    for c in range(3):
        for y in range(ROWS):
            cross, core = cross_ref[c, y], core_ref[c, y]
            zn_ref[c, y] = jnp.where(even, core, cross)
            zp_ref[c, y] = jnp.where(even, cross, core)
    refs = (cot_ref, vel_ref, zn_ref, zp_ref, None, None)
    row = sublane()
    cot = {(c, y): cot_frame(refs, row, c, y) for c in range(3) for y in range(ROWS)}
    flat = {y: -(dx(cot[0, y]) + along_z_cot(refs, row, cot[2, y], y)) for y in range(ROWS)}
    low = flat[0] - 0.5 * cot[1, 1]
    high = flat[3] + 0.5 * cot[1, 2]
    one = flat[1] - 0.5 * (cot[1, 2] - cot[1, 0])
    two = flat[2] - 0.5 * (cot[1, 3] - cot[1, 1])
    for out, part, (d1, d2) in (
        (prev_ref, (low, one, two, high), (0, 1)),
        (next_ref, (high, two, one, low), (3, 2)),
    ):
        for d in range(4):
            out[d] = part[d][:TILE]
        for c in range(3):
            out[4 + c] = cot_ref[c, d1]
            out[7 + c] = cot_ref[c, d2]
            out[10 + c] = vel_ref[c, d1]
            out[13 + c] = vel_ref[c, d2]
        vel = [side_vel(row, zn_ref[c, d1], zp_ref[c, d1]) for c in range(3)]
        out[16] = mixed(row, part[0][TILE:], [(3, part[2][TILE:])])
        out[17] = mixed(row, part[1][TILE:], [(2, cot[0, d1][TILE:]), (3, cot[2, d1][TILE:])])
        out[18] = mixed(row, vel[0], [(1, vel[1]), (2, vel[2])])
        out[19] = cot[1, d1][TILE:]


def cot_frame(refs, row, c, y):
    cot_ref, vel_ref, zn_ref, zp_ref, yn_ref, yp_ref = refs
    if 0 <= y < ROWS:
        return joined(cot_ref[c, y], side_cot(row, zn_ref[c, y], zp_ref[c, y]))
    got, d = (yn_ref, y - ROWS) if y >= ROWS else (yp_ref, -1 - y)
    if d == 1:
        return joined(got[7 + c], got[7 + c])
    return joined(got[4 + c], got[19] if c == 1 else take(row, got[17], 2 if c == 0 else 3))


def vel_frame(refs, row, c, y):
    cot_ref, vel_ref, zn_ref, zp_ref, yn_ref, yp_ref = refs
    if 0 <= y < ROWS:
        return joined(vel_ref[c, y], side_vel(row, zn_ref[c, y], zp_ref[c, y]))
    got, d = (yn_ref, y - ROWS) if y >= ROWS else (yp_ref, -1 - y)
    if d == 1:
        return joined(got[13 + c], got[13 + c])
    return joined(got[10 + c], take(row, got[18], c))


def part_frame(refs, row, y):
    got, d = (refs[4], y - ROWS) if y >= ROWS else (refs[5], -1 - y)
    if d == 0:
        return joined(got[0], got[16])
    if d == 1:
        return joined(got[1], got[17])
    if d == 2:
        return joined(got[2], take(row, got[16], 3))
    return joined(got[3], got[3])


def along_z_cot(refs, row, frame, y):
    if not 0 <= y < ROWS:
        return dz(frame)
    zn_ref, zp_ref = refs[2], refs[3]
    ends = jnp.where(row < SIDE, zp_ref[2, y], zn_ref[2, y])
    wide = lax.broadcasted_iota(jnp.int32, (WIDE, 256), 0)
    both = joined(ends, ends)
    after = jnp.where(wide == TILE + 3, rolled(both, -1, 0), rolled(frame, -1, 0))
    before = jnp.where(wide == TILE + 4, rolled(both, 1, 0), rolled(frame, 1, 0))
    return 0.5 * (after - before)


def laplace(here, below, above):
    beside = rolled(here, 1, 1) + rolled(here, -1, 1)
    beside = beside + above + below
    beside = beside + rolled(here, 1, 0) + rolled(here, -1, 0)
    return 6.0 * here - beside


def ratio(top, bottom):
    safe = bottom > 0.0
    return jnp.where(safe, top / jnp.where(safe, bottom, 1.0), 0.0)


def total(x):
    return jnp.sum(jnp.sum(x, axis=0, keepdims=True), axis=1, keepdims=True)


def moments(peers, place_ref, cot_ref, vel_ref, zn_ref, zp_ref, yn_ref, yp_ref, out_ref, b_ref, w_ref):
    refs = (cot_ref, vel_ref, zn_ref, zp_ref, yn_ref, yp_ref)
    row = sublane()
    cot_y = {y: cot_frame(refs, row, 1, y) for y in range(-1, 5)}
    b = {y: part_frame(refs, row, y) for y in (-3, -2, -1, 4, 5, 6)}
    b[-1] = b[-1] - 0.5 * cot_y[0]
    b[4] = b[4] + 0.5 * cot_y[3]
    for y in range(ROWS):
        flat = dx(cot_frame(refs, row, 0, y)) + along_z_cot(refs, row, cot_frame(refs, row, 2, y), y)
        b[y] = -(flat + 0.5 * (cot_y[y + 1] - cot_y[y - 1]))
    for y in range(-3, 7):
        b_ref[y + 3] = b[y]
    w = {}
    for y in range(-2, 6):
        w[y] = laplace(b[y], b[y - 1], b[y + 1])
        w_ref[y + 2] = w[y]
    m0 = m1 = None
    for y in range(ROWS):
        bc, wc = b[y][:TILE], w[y][:TILE]
        m0 = bc * bc if m0 is None else m0 + bc * bc
        m1 = bc * wc if m1 is None else m1 + bc * wc
    m0, m1 = total(m0), total(m1)
    sigma = ratio(m1, m0)
    spread = third = cross = None
    for y in range(ROWS):
        bc, wc = b[y][:TILE], w[y][:TILE]
        x = laplace(w[y], w[y - 1], w[y + 1])[:TILE]
        v = wc - sigma * bc
        u = x - sigma * wc
        spread = v * v if spread is None else spread + v * v
        third = v * u if third is None else third + v * u
        cross = bc * u if cross is None else cross + bc * u
    spread, third, cross = total(spread), total(third), total(cross)
    line = lax.broadcasted_iota(jnp.int32, (TILE, 128), 0)
    tile = jnp.zeros((TILE, 128), jnp.float32)
    for k, value in enumerate((m0, m1, spread, third, cross)):
        tile = jnp.where(line == k, value, tile)
    place = place_ref[0]
    for j in range(peers):
        ahead = lax.rem(j - place + peers, peers)
        up = jnp.where(ahead < peers // 2, 1.0, 0.0)
        out_ref[j, :, :256] = jnp.where(up > 0.5, cot_ref[1, ROWS - 1], cot_ref[1, 0])
        out_ref[j, :, 256:] = tile


def merged(m0, m1, spread, third, cross):
    own = ratio(m1, m0)

    def over(x):
        return jnp.sum(x, axis=0, keepdims=True)

    all0, all1 = over(m0), over(m1)
    delta = ratio(all1, all0) - own
    all_spread = over(spread + delta * delta * m0)
    all_third = over(third - delta * (spread + cross) + delta * delta * m1)
    all_cross = over(cross - delta * m1)
    return all0, all1, all_spread, all_third, all_cross


def merge(got_ref, out_ref):
    parts = merged(*[got_ref[:, k, 256:] for k in range(5)])
    lane = lax.broadcasted_iota(jnp.int32, (1, 128), 1)
    line = jnp.zeros((1, 128), jnp.float32)
    for k, value in enumerate(parts):
        line = jnp.where(lane == k, value, line)
    for j in range(out_ref.shape[0]):
        out_ref[j] = line


def finish(peers, place_ref, cot_ref, vel_ref, zn_ref, zp_ref, yn_ref, yp_ref, far_ref, b_ref, w_ref, sums_ref, out_ref):
    refs = (cot_ref, vel_ref, zn_ref, zp_ref, yn_ref, yp_ref)
    row = sublane()
    sums = sums_ref[...].reshape(sums_ref.shape[0], 128)
    m0, m1, spread, third, _ = [x[:, :1] for x in merged(*[rolled(sums, -k, 1) for k in range(5)])]
    step0 = m0 / m1
    norm1 = step0 * step0 * spread
    beta = norm1 / m0
    bend = step0 * step0 * third - 2.0 * step0 * beta * spread + beta * beta * m1
    step1 = norm1 / bend
    coef_b = step0 + step1 * (1.0 + beta)
    coef_w = -(step1 * step0)

    place = place_ref[0]
    above = far_ref[lax.rem(place + 2, peers), :, :256]
    below = far_ref[lax.rem(place + peers - 2, peers), :, :256]
    above, below = joined(above, above), joined(below, below)
    cot = {(c, y): cot_frame(refs, row, c, y) for c in range(3) for y in range(-2, 6)}
    b = {y: b_ref[y + 3] for y in range(-3, 7)}
    b[-4] = part_frame(refs, row, -4) + 0.5 * below
    b[7] = part_frame(refs, row, 7) - 0.5 * above
    w = {y: w_ref[y + 2] for y in range(-2, 6)}
    w[-3] = laplace(b[-3], b[-4], b[-2])
    w[6] = laplace(b[6], b[5], b[7])
    p = {y: coef_b * b[y] + coef_w * w[y] for y in range(-3, 7)}
    lam = {}
    for y in range(-2, 6):
        lam[0, y] = cot[0, y] - dx(p[y])
        lam[1, y] = cot[1, y] - 0.5 * (p[y + 1] - p[y - 1])
        lam[2, y] = cot[2, y] - dz(p[y])
    vel = {(c, y): vel_frame(refs, row, c, y) for c in range(3) for y in range(-2, 6)}

    flat, upright = {}, {}
    for y in range(-1, 5):
        grad = [[dx(vel[i, y]), 0.5 * (vel[i, y + 1] - vel[i, y - 1]), dz(vel[i, y])] for i in range(3)]
        pull = [[dx(lam[i, y]), 0.5 * (lam[i, y + 1] - lam[i, y - 1]), dz(lam[i, y])] for i in range(3)]
        strain, ebb = {}, {}
        for i in range(3):
            for j in range(i + 1):
                strain[i, j] = grad[i][i] if i == j else 0.5 * (grad[i][j] + grad[j][i])
                ebb[i, j] = pull[i][i] if i == j else 0.5 * (pull[i][j] + pull[j][i])
        squares = strain[0, 0] * strain[0, 0] + strain[1, 1] * strain[1, 1] + strain[2, 2] * strain[2, 2]
        work = strain[0, 0] * ebb[0, 0] + strain[1, 1] * ebb[1, 1] + strain[2, 2] * ebb[2, 2]
        off = strain[1, 0] * strain[1, 0] + strain[2, 0] * strain[2, 0] + strain[2, 1] * strain[2, 1]
        off_work = strain[1, 0] * ebb[1, 0] + strain[2, 0] * ebb[2, 0] + strain[2, 1] * ebb[2, 1]
        inside = 2.0 * (squares + 2.0 * off) + strain_floor
        inverse = lax.rsqrt(inside)
        twice = (2.0 * smag_coef) * (inside * inverse)
        factor = (4.0 * smag_coef) * inverse * (work + 2.0 * off_work)
        stress = {key: twice * ebb[key] + factor * strain[key] for key in strain}

        def both(i, j):
            return stress[max(i, j), min(i, j)] + lam[i, y] * vel[j, y]

        for i in range(3):
            upright[i, y] = both(i, 1)[:TILE]
        if 0 <= y < ROWS:
            for i in range(3):
                carried = lam[0, y] * grad[0][i] + lam[1, y] * grad[1][i] + lam[2, y] * grad[2][i]
                level = dx(both(i, 0)) + dz(both(i, 2))
                flat[i, y] = (lam[i, y] + time_step * (level - carried))[:TILE]
    for i in range(3):
        for y in range(ROWS):
            out_ref[i, y] = flat[i, y] + (0.5 * time_step) * (upright[i, y + 1] - upright[i, y - 1])


def call(kernel, outs, scalars, arrays, place=pltpu.VMEM, scratch=()):
    vmem = pl.BlockSpec(memory_space=pltpu.VMEM)
    given = pl.BlockSpec(memory_space=place)
    smem = pl.BlockSpec(memory_space=pltpu.SMEM)
    return pl.pallas_call(
        kernel,
        out_shape=[jax.ShapeDtypeStruct(s, jnp.float32) for s in outs],
        in_specs=[smem] * len(scalars) + [given] * len(arrays),
        out_specs=[vmem] * len(outs),
        scratch_shapes=list(scratch),
        compiler_params=pltpu.CompilerParams(vmem_limit_bytes=32 * 1024 * 1024),
    )(*scalars, *arrays)


def both_ways(to_prev, to_next, axis):
    n = lax.axis_size(axis)
    up = [(i, (i + 1) % n) for i in range(n)]
    down = [(j, i) for i, j in up]
    from_next = lax.ppermute(to_prev, axis, down)
    from_prev = lax.ppermute(to_next, axis, up)
    return from_next, from_prev


def body(velocity, cotangent):
    ny, nz = lax.axis_size("py"), lax.axis_size("pz")
    place = lax.axis_index("py").astype(jnp.int32).reshape(1)
    block = (3, ROWS, TILE, 256)
    dmas = [pltpu.SemaphoreType.DMA((2,))]
    odd = lax.rem(lax.axis_index("pz"), 2).astype(jnp.int32).reshape(1)
    cross, core, cotangent, velocity = call(
        pack_z, [block] * 4, [odd], [cotangent, velocity], pltpu.HBM, dmas
    )
    cross = lax.ppermute(cross, "pz", [(i, (i + 1 if i % 2 else i - 1) % nz) for i in range(nz)])
    core = lax.ppermute(core, "pz", [(i, i ^ 1) for i in range(nz)])
    sent = (SENT, TILE, 256)
    to_prev, to_next, zn, zp = call(
        pack_y, [sent, sent, block, block], [odd], [cotangent, velocity, cross, core]
    )
    yn, yp = both_ways(to_prev, to_next, "py")
    held = [cotangent, velocity, zn, zp, yn, yp]
    chunks, b, w = call(
        functools.partial(moments, ny),
        [(ny, TILE, 384), (10, WIDE, 256), (8, WIDE, 256)],
        [place],
        held,
    )
    got = lax.all_to_all(chunks, "py", 0, 0)
    (lines,) = call(merge, [(nz, 1, 128)], [], [got])
    sums = lax.all_to_all(lines, "pz", 0, 0)
    (out,) = call(functools.partial(finish, ny), [block], [place], held + [got, b, w, sums])
    return out


def solution(mesh):
    placed = (P(None, "py", "pz", None), P(None, "py", "pz", None))
    return jax.shard_map(
        body, mesh=mesh, in_specs=placed, out_specs=P(None, "py", "pz", None), check_vma=False
    )
```

```python
import functools

import jax
import jax.numpy as jnp
from jax import lax
from jax.experimental import pallas as pl
from jax.experimental.pallas import tpu as pltpu
from jax.sharding import PartitionSpec as P

smag_coef = 0.1156
time_step = 0.2
strain_floor = 0.25

ROWS = 4
TILE = 8
SIDE = 4
WIDE = TILE + 2 * SIDE
SENT = 20


def rolled(x, shift, axis):
    return pltpu.roll(x, shift % x.shape[axis], axis)


def dx(f):
    n = f.ndim - 1
    return 0.5 * (rolled(f, -1, n) - rolled(f, 1, n))


def dz(f):
    n = f.ndim - 2
    return 0.5 * (rolled(f, -1, n) - rolled(f, 1, n))


def sublane():
    return lax.broadcasted_iota(jnp.int32, (TILE, 256), 0)


def pack_z(odd_ref, cot_hbm, vel_hbm, cross_ref, core_ref, cot_ref, vel_ref, sems):
    copies = [
        pltpu.make_async_copy(cot_hbm, cot_ref, sems.at[0]),
        pltpu.make_async_copy(vel_hbm, vel_ref, sems.at[1]),
    ]
    for copy in copies:
        copy.start()
    for copy in copies:
        copy.wait()
    row = sublane()
    even = odd_ref[0] == 0
    for c in range(3):
        for y in range(ROWS):
            cot, vel = cot_ref[c, y], vel_ref[c, y]
            to_prev = jnp.where(row < 5, cot, rolled(vel, 5, 0))
            to_next = jnp.where(row >= 3, cot, rolled(vel, 3, 0))
            cross_ref[c, y] = jnp.where(even, to_prev, to_next)
            core_ref[c, y] = jnp.where(even, to_next, to_prev)


def side_cot(row, zn, zp):
    return jnp.where(row < SIDE, zn, zp)


def side_vel(row, zn, zp):
    return jnp.where(row < SIDE, rolled(zn, 3, 0), rolled(zp, 5, 0))


def put(row, tile, k):
    return jnp.where(row < SIDE, rolled(tile, k, 0), rolled(tile, -k, 0))


def take(row, tile, k):
    return jnp.where(row < SIDE, rolled(tile, -k, 0), rolled(tile, k, 0))


def mixed(row, base, inner):
    for k, tile in inner:
        base = jnp.where((row == k) | (row == TILE - 1 - k), put(row, tile, k), base)
    return base


def joined(a, b):
    return jnp.concatenate([a, b], axis=0)


def pack_y(odd_ref, place_ref, cot_ref, vel_ref, cross_ref, core_ref, first_ref, second_ref, zn_ref, zp_ref):
    even = odd_ref[0] == 0
    for c in range(3):
        for y in range(ROWS):
            cross, core = cross_ref[c, y], core_ref[c, y]
            zn_ref[c, y] = jnp.where(even, core, cross)
            zp_ref[c, y] = jnp.where(even, cross, core)
    refs = (cot_ref, vel_ref, zn_ref, zp_ref, None, None)
    row = sublane()
    cot = {(c, y): cot_frame(refs, row, c, y) for c in range(3) for y in range(ROWS)}
    flat = {y: -(dx(cot[0, y]) + along_z_cot(refs, row, cot[2, y], y)) for y in range(ROWS)}
    low = flat[0] - 0.5 * cot[1, 1]
    high = flat[3] + 0.5 * cot[1, 2]
    one = flat[1] - 0.5 * (cot[1, 2] - cot[1, 0])
    two = flat[2] - 0.5 * (cot[1, 3] - cot[1, 1])
    to_prev, to_next = {}, {}
    for out, part, (d1, d2) in (
        (to_prev, (low, one, two, high), (0, 1)),
        (to_next, (high, two, one, low), (3, 2)),
    ):
        for d in range(4):
            out[d] = part[d][:TILE]
        for c in range(3):
            out[4 + c] = cot_ref[c, d1]
            out[7 + c] = cot_ref[c, d2]
            out[10 + c] = vel_ref[c, d1]
            out[13 + c] = vel_ref[c, d2]
        vel = [side_vel(row, zn_ref[c, d1], zp_ref[c, d1]) for c in range(3)]
        out[16] = mixed(row, part[0][TILE:], [(3, part[2][TILE:])])
        out[17] = mixed(row, part[1][TILE:], [(2, cot[0, d1][TILE:]), (3, cot[2, d1][TILE:])])
        out[18] = mixed(row, vel[0], [(1, vel[1]), (2, vel[2])])
        out[19] = cot[1, d1][TILE:]
    level = lax.rem(place_ref[0], 2) == 0
    for k in range(SENT):
        first_ref[k] = jnp.where(level, to_prev[k], to_next[k])
        second_ref[k] = jnp.where(level, to_next[k], to_prev[k])


def cot_frame(refs, row, c, y):
    cot_ref, vel_ref, zn_ref, zp_ref, yn_ref, yp_ref = refs
    if 0 <= y < ROWS:
        return joined(cot_ref[c, y], side_cot(row, zn_ref[c, y], zp_ref[c, y]))
    got, d = (yn_ref, y - ROWS) if y >= ROWS else (yp_ref, -1 - y)
    if d == 1:
        return joined(got[7 + c], got[7 + c])
    return joined(got[4 + c], got[19] if c == 1 else take(row, got[17], 2 if c == 0 else 3))


def vel_frame(refs, row, c, y):
    cot_ref, vel_ref, zn_ref, zp_ref, yn_ref, yp_ref = refs
    if 0 <= y < ROWS:
        return joined(vel_ref[c, y], side_vel(row, zn_ref[c, y], zp_ref[c, y]))
    got, d = (yn_ref, y - ROWS) if y >= ROWS else (yp_ref, -1 - y)
    if d == 1:
        return joined(got[13 + c], got[13 + c])
    return joined(got[10 + c], take(row, got[18], c))


def part_frame(refs, row, y):
    got, d = (refs[4], y - ROWS) if y >= ROWS else (refs[5], -1 - y)
    if d == 0:
        return joined(got[0], got[16])
    if d == 1:
        return joined(got[1], got[17])
    if d == 2:
        return joined(got[2], take(row, got[16], 3))
    return joined(got[3], got[3])


def along_z_cot(refs, row, frame, y):
    if not 0 <= y < ROWS:
        return dz(frame)
    zn_ref, zp_ref = refs[2], refs[3]
    ends = jnp.where(row < SIDE, zp_ref[2, y], zn_ref[2, y])
    wide = lax.broadcasted_iota(jnp.int32, (WIDE, 256), 0)
    both = joined(ends, ends)
    after = jnp.where(wide == TILE + 3, rolled(both, -1, 0), rolled(frame, -1, 0))
    before = jnp.where(wide == TILE + 4, rolled(both, 1, 0), rolled(frame, 1, 0))
    return 0.5 * (after - before)


def laplace(here, below, above):
    beside = rolled(here, 1, 1) + rolled(here, -1, 1)
    beside = beside + above + below
    beside = beside + rolled(here, 1, 0) + rolled(here, -1, 0)
    return 6.0 * here - beside


def ratio(top, bottom):
    safe = bottom > 0.0
    return jnp.where(safe, top / jnp.where(safe, bottom, 1.0), 0.0)


def total(x):
    return jnp.sum(jnp.sum(x, axis=0, keepdims=True), axis=1, keepdims=True)


def moments(
    peers, place_ref, cot_ref, vel_ref, zn_ref, zp_ref, first_ref, second_ref, out_ref, b_ref, w_ref, yn_ref, yp_ref
):
    level = lax.rem(place_ref[0], 2) == 0
    for k in range(SENT):
        first, second = first_ref[k], second_ref[k]
        yn_ref[k] = jnp.where(level, second, first)
        yp_ref[k] = jnp.where(level, first, second)
    refs = (cot_ref, vel_ref, zn_ref, zp_ref, yn_ref, yp_ref)
    row = sublane()
    cot_y = {y: cot_frame(refs, row, 1, y) for y in range(-1, 5)}
    b = {y: part_frame(refs, row, y) for y in (-3, -2, -1, 4, 5, 6)}
    b[-1] = b[-1] - 0.5 * cot_y[0]
    b[4] = b[4] + 0.5 * cot_y[3]
    for y in range(ROWS):
        flat = dx(cot_frame(refs, row, 0, y)) + along_z_cot(refs, row, cot_frame(refs, row, 2, y), y)
        b[y] = -(flat + 0.5 * (cot_y[y + 1] - cot_y[y - 1]))
    for y in range(-3, 7):
        b_ref[y + 3] = b[y]
    w = {}
    for y in range(-2, 6):
        w[y] = laplace(b[y], b[y - 1], b[y + 1])
        w_ref[y + 2] = w[y]
    m0 = m1 = None
    for y in range(ROWS):
        bc, wc = b[y][:TILE], w[y][:TILE]
        m0 = bc * bc if m0 is None else m0 + bc * bc
        m1 = bc * wc if m1 is None else m1 + bc * wc
    m0, m1 = total(m0), total(m1)
    sigma = ratio(m1, m0)
    spread = third = cross = None
    for y in range(ROWS):
        bc, wc = b[y][:TILE], w[y][:TILE]
        x = laplace(w[y], w[y - 1], w[y + 1])[:TILE]
        v = wc - sigma * bc
        u = x - sigma * wc
        spread = v * v if spread is None else spread + v * v
        third = v * u if third is None else third + v * u
        cross = bc * u if cross is None else cross + bc * u
    spread, third, cross = total(spread), total(third), total(cross)
    line = lax.broadcasted_iota(jnp.int32, (TILE, 128), 0)
    tile = jnp.zeros((TILE, 128), jnp.float32)
    for k, value in enumerate((m0, m1, spread, third, cross)):
        tile = jnp.where(line == k, value, tile)
    place = place_ref[0]
    for j in range(peers):
        ahead = lax.rem(j - place + peers, peers)
        up = jnp.where(ahead < peers // 2, 1.0, 0.0)
        out_ref[j, :, :256] = jnp.where(up > 0.5, cot_ref[1, ROWS - 1], cot_ref[1, 0])
        out_ref[j, :, 256:] = tile


def merged(m0, m1, spread, third, cross):
    own = ratio(m1, m0)

    def over(x):
        return jnp.sum(x, axis=0, keepdims=True)

    all0, all1 = over(m0), over(m1)
    delta = ratio(all1, all0) - own
    all_spread = over(spread + delta * delta * m0)
    all_third = over(third - delta * (spread + cross) + delta * delta * m1)
    all_cross = over(cross - delta * m1)
    return all0, all1, all_spread, all_third, all_cross


def merge(got_ref, out_ref):
    parts = merged(*[got_ref[:, k, 256:] for k in range(5)])
    lane = lax.broadcasted_iota(jnp.int32, (1, 128), 1)
    line = jnp.zeros((1, 128), jnp.float32)
    for k, value in enumerate(parts):
        line = jnp.where(lane == k, value, line)
    for j in range(out_ref.shape[0]):
        out_ref[j] = line


def finish(peers, place_ref, cot_ref, vel_ref, zn_ref, zp_ref, yn_ref, yp_ref, far_ref, b_ref, w_ref, sums_ref, out_ref):
    refs = (cot_ref, vel_ref, zn_ref, zp_ref, yn_ref, yp_ref)
    row = sublane()
    sums = sums_ref[...].reshape(sums_ref.shape[0], 128)
    m0, m1, spread, third, _ = [x[:, :1] for x in merged(*[rolled(sums, -k, 1) for k in range(5)])]
    step0 = m0 / m1
    norm1 = step0 * step0 * spread
    beta = norm1 / m0
    bend = step0 * step0 * third - 2.0 * step0 * beta * spread + beta * beta * m1
    step1 = norm1 / bend
    coef_b = step0 + step1 * (1.0 + beta)
    coef_w = -(step1 * step0)

    place = place_ref[0]
    above = far_ref[lax.rem(place + 2, peers), :, :256]
    below = far_ref[lax.rem(place + peers - 2, peers), :, :256]
    above, below = joined(above, above), joined(below, below)
    cot = {(c, y): cot_frame(refs, row, c, y) for c in range(3) for y in range(-2, 6)}
    b = {y: b_ref[y + 3] for y in range(-3, 7)}
    b[-4] = part_frame(refs, row, -4) + 0.5 * below
    b[7] = part_frame(refs, row, 7) - 0.5 * above
    w = {y: w_ref[y + 2] for y in range(-2, 6)}
    w[-3] = laplace(b[-3], b[-4], b[-2])
    w[6] = laplace(b[6], b[5], b[7])
    p = {y: coef_b * b[y] + coef_w * w[y] for y in range(-3, 7)}
    lam = {}
    for y in range(-2, 6):
        lam[0, y] = cot[0, y] - dx(p[y])
        lam[1, y] = cot[1, y] - 0.5 * (p[y + 1] - p[y - 1])
        lam[2, y] = cot[2, y] - dz(p[y])
    vel = {(c, y): vel_frame(refs, row, c, y) for c in range(3) for y in range(-2, 6)}

    flat, upright = {}, {}
    for y in range(-1, 5):
        grad = [[dx(vel[i, y]), 0.5 * (vel[i, y + 1] - vel[i, y - 1]), dz(vel[i, y])] for i in range(3)]
        pull = [[dx(lam[i, y]), 0.5 * (lam[i, y + 1] - lam[i, y - 1]), dz(lam[i, y])] for i in range(3)]
        strain, ebb = {}, {}
        for i in range(3):
            for j in range(i + 1):
                strain[i, j] = grad[i][i] if i == j else 0.5 * (grad[i][j] + grad[j][i])
                ebb[i, j] = pull[i][i] if i == j else 0.5 * (pull[i][j] + pull[j][i])
        squares = strain[0, 0] * strain[0, 0] + strain[1, 1] * strain[1, 1] + strain[2, 2] * strain[2, 2]
        work = strain[0, 0] * ebb[0, 0] + strain[1, 1] * ebb[1, 1] + strain[2, 2] * ebb[2, 2]
        off = strain[1, 0] * strain[1, 0] + strain[2, 0] * strain[2, 0] + strain[2, 1] * strain[2, 1]
        off_work = strain[1, 0] * ebb[1, 0] + strain[2, 0] * ebb[2, 0] + strain[2, 1] * ebb[2, 1]
        inside = 2.0 * (squares + 2.0 * off) + strain_floor
        inverse = lax.rsqrt(inside)
        twice = (2.0 * smag_coef) * (inside * inverse)
        factor = (4.0 * smag_coef) * inverse * (work + 2.0 * off_work)
        stress = {key: twice * ebb[key] + factor * strain[key] for key in strain}

        def both(i, j):
            return stress[max(i, j), min(i, j)] + lam[i, y] * vel[j, y]

        for i in range(3):
            upright[i, y] = both(i, 1)[:TILE]
        if 0 <= y < ROWS:
            for i in range(3):
                carried = lam[0, y] * grad[0][i] + lam[1, y] * grad[1][i] + lam[2, y] * grad[2][i]
                level = dx(both(i, 0)) + dz(both(i, 2))
                flat[i, y] = (lam[i, y] + time_step * (level - carried))[:TILE]
    for i in range(3):
        for y in range(ROWS):
            out_ref[i, y] = flat[i, y] + (0.5 * time_step) * (upright[i, y + 1] - upright[i, y - 1])


def call(kernel, outs, scalars, arrays, place=pltpu.VMEM, scratch=()):
    vmem = pl.BlockSpec(memory_space=pltpu.VMEM)
    given = pl.BlockSpec(memory_space=place)
    smem = pl.BlockSpec(memory_space=pltpu.SMEM)
    return pl.pallas_call(
        kernel,
        out_shape=[jax.ShapeDtypeStruct(s, jnp.float32) for s in outs],
        in_specs=[smem] * len(scalars) + [given] * len(arrays),
        out_specs=[vmem] * len(outs),
        scratch_shapes=list(scratch),
        compiler_params=pltpu.CompilerParams(vmem_limit_bytes=32 * 1024 * 1024),
    )(*scalars, *arrays)


def swap_across(x, axis):
    n = lax.axis_size(axis)
    return lax.ppermute(x, axis, [(i, (i + 1 if i % 2 else i - 1) % n) for i in range(n)])


def swap_within(x, axis):
    return lax.ppermute(x, axis, [(i, i ^ 1) for i in range(lax.axis_size(axis))])


def body(velocity, cotangent):
    ny, nz = lax.axis_size("py"), lax.axis_size("pz")
    place = lax.axis_index("py").astype(jnp.int32).reshape(1)
    block = (3, ROWS, TILE, 256)
    dmas = [pltpu.SemaphoreType.DMA((2,))]
    odd = lax.rem(lax.axis_index("pz"), 2).astype(jnp.int32).reshape(1)
    cross, core, cotangent, velocity = call(
        pack_z, [block] * 4, [odd], [cotangent, velocity], pltpu.HBM, dmas
    )
    cross = swap_across(cross, "pz")
    core = swap_within(core, "pz")
    sent = (SENT, TILE, 256)
    first, second, zn, zp = call(
        pack_y, [sent, sent, block, block], [odd, place], [cotangent, velocity, cross, core]
    )
    first = swap_across(first, "py")
    second = swap_within(second, "py")
    chunks, b, w, yn, yp = call(
        functools.partial(moments, ny),
        [(ny, TILE, 384), (10, WIDE, 256), (8, WIDE, 256), sent, sent],
        [place],
        [cotangent, velocity, zn, zp, first, second],
    )
    held = [cotangent, velocity, zn, zp, yn, yp]
    got = lax.all_to_all(chunks, "py", 0, 0)
    (lines,) = call(merge, [(nz, 1, 128)], [], [got])
    sums = lax.all_to_all(lines, "pz", 0, 0)
    (out,) = call(functools.partial(finish, ny), [block], [place], held + [got, b, w, sums])
    return out


def solution(mesh):
    placed = (P(None, "py", "pz", None), P(None, "py", "pz", None))
    return jax.shard_map(
        body, mesh=mesh, in_specs=placed, out_specs=P(None, "py", "pz", None), check_vma=False
    )
```

```python
import math

import jax
import jax.numpy as jnp
from jax import lax
from jax.experimental import pallas as pl
from jax.experimental.pallas import tpu as pltpu
from jax.sharding import PartitionSpec as P

smag_coef = 0.1156
time_step = 0.2
strain_floor = 0.25

ROWS = 4
TILE = 8
SIDE = 4
WIDE = TILE + 2 * SIDE
SENT = 20


def rolled(x, shift, axis):
    return pltpu.roll(x, shift % x.shape[axis], axis)


def dx(f):
    n = f.ndim - 1
    return 0.5 * (rolled(f, -1, n) - rolled(f, 1, n))


def dz(f):
    n = f.ndim - 2
    return 0.5 * (rolled(f, -1, n) - rolled(f, 1, n))


def sublane():
    return lax.broadcasted_iota(jnp.int32, (TILE, 256), 0)


def pack_z(odd_ref, both_ref, cross_ref, core_ref, cot_ref, vel_ref):
    row = sublane()
    even = odd_ref[0] == 0
    for c in range(3):
        for y in range(ROWS):
            cot, vel = both_ref[c, y], both_ref[3 + c, y]
            cot_ref[c, y], vel_ref[c, y] = cot, vel
            to_prev = jnp.where(row < 5, cot, rolled(vel, 5, 0))
            to_next = jnp.where(row >= 3, cot, rolled(vel, 3, 0))
            cross_ref[c, y] = jnp.where(even, to_prev, to_next)
            core_ref[c, y] = jnp.where(even, to_next, to_prev)


def side_cot(row, zn, zp):
    return jnp.where(row < SIDE, zn, zp)


def side_vel(row, zn, zp):
    return jnp.where(row < SIDE, rolled(zn, 3, 0), rolled(zp, 5, 0))


def put(row, tile, k):
    return jnp.where(row < SIDE, rolled(tile, k, 0), rolled(tile, -k, 0))


def take(row, tile, k):
    return jnp.where(row < SIDE, rolled(tile, -k, 0), rolled(tile, k, 0))


def mixed(row, base, inner):
    for k, tile in inner:
        base = jnp.where((row == k) | (row == TILE - 1 - k), put(row, tile, k), base)
    return base


def joined(a, b):
    return jnp.concatenate([a, b], axis=0)


def pack_y(odd_ref, place_ref, cot_ref, vel_ref, cross_ref, core_ref, first_ref, second_ref, zn_ref, zp_ref, far1_ref, far2_ref):
    even = odd_ref[0] == 0
    for c in range(3):
        for y in range(ROWS):
            cross, core = cross_ref[c, y], core_ref[c, y]
            zn_ref[c, y] = jnp.where(even, core, cross)
            zp_ref[c, y] = jnp.where(even, cross, core)
    refs = (cot_ref, vel_ref, zn_ref, zp_ref, None, None)
    row = sublane()
    cot = {(c, y): cot_frame(refs, row, c, y) for c in range(3) for y in range(ROWS)}
    flat = {y: -(dx(cot[0, y]) + along_z_cot(refs, row, cot[2, y], y)) for y in range(ROWS)}
    low = flat[0] - 0.5 * cot[1, 1]
    high = flat[3] + 0.5 * cot[1, 2]
    one = flat[1] - 0.5 * (cot[1, 2] - cot[1, 0])
    two = flat[2] - 0.5 * (cot[1, 3] - cot[1, 1])
    to_prev, to_next = {}, {}
    for out, part, (d1, d2) in (
        (to_prev, (low, one, two, high), (0, 1)),
        (to_next, (high, two, one, low), (3, 2)),
    ):
        for d in range(4):
            out[d] = part[d][:TILE]
        for c in range(3):
            out[4 + c] = cot_ref[c, d1]
            out[7 + c] = cot_ref[c, d2]
            out[10 + c] = vel_ref[c, d1]
            out[13 + c] = vel_ref[c, d2]
        vel = [side_vel(row, zn_ref[c, d1], zp_ref[c, d1]) for c in range(3)]
        out[16] = mixed(row, part[0][TILE:], [(3, part[2][TILE:])])
        out[17] = mixed(row, part[1][TILE:], [(2, cot[0, d1][TILE:]), (3, cot[2, d1][TILE:])])
        out[18] = mixed(row, vel[0], [(1, vel[1]), (2, vel[2])])
        out[19] = cot[1, d1][TILE:]
    level = lax.rem(place_ref[0], 2) == 0
    for k in range(SENT):
        first_ref[k] = jnp.where(level, to_prev[k], to_next[k])
        second_ref[k] = jnp.where(level, to_next[k], to_prev[k])
    lower = lax.rem(place_ref[0], 4) < 2
    far1_ref[...] = jnp.where(lower, cot_ref[1, 0], cot_ref[1, ROWS - 1])
    far2_ref[...] = jnp.where(lower, cot_ref[1, ROWS - 1], cot_ref[1, 0])


def cot_frame(refs, row, c, y):
    cot_ref, vel_ref, zn_ref, zp_ref, yn_ref, yp_ref = refs
    if 0 <= y < ROWS:
        return joined(cot_ref[c, y], side_cot(row, zn_ref[c, y], zp_ref[c, y]))
    got, d = (yn_ref, y - ROWS) if y >= ROWS else (yp_ref, -1 - y)
    if d == 1:
        return joined(got[7 + c], got[7 + c])
    return joined(got[4 + c], got[19] if c == 1 else take(row, got[17], 2 if c == 0 else 3))


def vel_frame(refs, row, c, y):
    cot_ref, vel_ref, zn_ref, zp_ref, yn_ref, yp_ref = refs
    if 0 <= y < ROWS:
        return joined(vel_ref[c, y], side_vel(row, zn_ref[c, y], zp_ref[c, y]))
    got, d = (yn_ref, y - ROWS) if y >= ROWS else (yp_ref, -1 - y)
    if d == 1:
        return joined(got[13 + c], got[13 + c])
    return joined(got[10 + c], take(row, got[18], c))


def part_frame(refs, row, y):
    got, d = (refs[4], y - ROWS) if y >= ROWS else (refs[5], -1 - y)
    if d == 0:
        return joined(got[0], got[16])
    if d == 1:
        return joined(got[1], got[17])
    if d == 2:
        return joined(got[2], take(row, got[16], 3))
    return joined(got[3], got[3])


def along_z_cot(refs, row, frame, y):
    if not 0 <= y < ROWS:
        return dz(frame)
    zn_ref, zp_ref = refs[2], refs[3]
    ends = jnp.where(row < SIDE, zp_ref[2, y], zn_ref[2, y])
    wide = lax.broadcasted_iota(jnp.int32, (WIDE, 256), 0)
    both = joined(ends, ends)
    after = jnp.where(wide == TILE + 3, rolled(both, -1, 0), rolled(frame, -1, 0))
    before = jnp.where(wide == TILE + 4, rolled(both, 1, 0), rolled(frame, 1, 0))
    return 0.5 * (after - before)


def laplace(here, below, above):
    beside = rolled(here, 1, 1) + rolled(here, -1, 1)
    beside = beside + above + below
    beside = beside + rolled(here, 1, 0) + rolled(here, -1, 0)
    return 6.0 * here - beside


def ratio(top, bottom):
    safe = bottom > 0.0
    return jnp.where(safe, top / jnp.where(safe, bottom, 1.0), 0.0)


def total(x):
    return jnp.sum(jnp.sum(x, axis=0, keepdims=True), axis=1, keepdims=True)


def moments(
    place_ref, cot_ref, vel_ref, zn_ref, zp_ref, first_ref, second_ref, out_ref, b_ref, w_ref, yn_ref, yp_ref
):
    level = lax.rem(place_ref[0], 2) == 0
    for k in range(SENT):
        first, second = first_ref[k], second_ref[k]
        yn_ref[k] = jnp.where(level, second, first)
        yp_ref[k] = jnp.where(level, first, second)
    refs = (cot_ref, vel_ref, zn_ref, zp_ref, yn_ref, yp_ref)
    row = sublane()
    cot_y = {y: cot_frame(refs, row, 1, y) for y in range(-1, 5)}
    b = {y: part_frame(refs, row, y) for y in (-3, -2, -1, 4, 5, 6)}
    b[-1] = b[-1] - 0.5 * cot_y[0]
    b[4] = b[4] + 0.5 * cot_y[3]
    for y in range(ROWS):
        flat = dx(cot_frame(refs, row, 0, y)) + along_z_cot(refs, row, cot_frame(refs, row, 2, y), y)
        b[y] = -(flat + 0.5 * (cot_y[y + 1] - cot_y[y - 1]))
    for y in range(-3, 7):
        b_ref[y + 3] = b[y]
    w = {}
    for y in range(-2, 6):
        w[y] = laplace(b[y], b[y - 1], b[y + 1])
        w_ref[y + 2] = w[y]
    m0 = m1 = None
    for y in range(ROWS):
        bc, wc = b[y][:TILE], w[y][:TILE]
        m0 = bc * bc if m0 is None else m0 + bc * bc
        m1 = bc * wc if m1 is None else m1 + bc * wc
    m0, m1 = total(m0), total(m1)
    sigma = ratio(m1, m0)
    spread = third = cross = None
    for y in range(ROWS):
        bc, wc = b[y][:TILE], w[y][:TILE]
        x = laplace(w[y], w[y - 1], w[y + 1])[:TILE]
        v = wc - sigma * bc
        u = x - sigma * wc
        spread = v * v if spread is None else spread + v * v
        third = v * u if third is None else third + v * u
        cross = bc * u if cross is None else cross + bc * u
    spread, third, cross = total(spread), total(third), total(cross)
    spread_out((m0, m1, spread, third, cross), out_ref)


def spread_out(parts, out_ref):
    lane = lax.broadcasted_iota(jnp.int32, (1, 128), 1)
    line = jnp.zeros((1, 128), jnp.float32)
    for k, value in enumerate(parts):
        line = jnp.where(lane == k, value, line)
    for j in range(out_ref.shape[0]):
        out_ref[j] = line


def gathered(got_ref):
    lines = got_ref[...].reshape(got_ref.shape[0], 128)
    return [x[:, :1] for x in merged(*[rolled(lines, -k, 1) for k in range(5)])]


def merged(m0, m1, spread, third, cross):
    own = ratio(m1, m0)

    def over(x):
        return jnp.sum(x, axis=0, keepdims=True)

    all0, all1 = over(m0), over(m1)
    delta = ratio(all1, all0) - own
    all_spread = over(spread + delta * delta * m0)
    all_third = over(third - delta * (spread + cross) + delta * delta * m1)
    all_cross = over(cross - delta * m1)
    return all0, all1, all_spread, all_third, all_cross


def merge(got_ref, out_ref):
    spread_out(gathered(got_ref), out_ref)


def finish(
    place_ref, cot_ref, vel_ref, zn_ref, zp_ref, yn_ref, yp_ref, far1_ref, far2_ref, b_ref, w_ref, sums_ref, out_ref
):
    refs = (cot_ref, vel_ref, zn_ref, zp_ref, yn_ref, yp_ref)
    row = sublane()
    m0, m1, spread, third, _ = gathered(sums_ref)
    step0 = m0 / m1
    norm1 = step0 * step0 * spread
    beta = norm1 / m0
    bend = step0 * step0 * third - 2.0 * step0 * beta * spread + beta * beta * m1
    step1 = norm1 / bend
    coef_b = step0 + step1 * (1.0 + beta)
    coef_w = -(step1 * step0)

    lower = lax.rem(place_ref[0], 4) < 2
    above = jnp.where(lower, far2_ref[...], far1_ref[...])
    below = jnp.where(lower, far1_ref[...], far2_ref[...])
    above, below = joined(above, above), joined(below, below)
    cot = {(c, y): cot_frame(refs, row, c, y) for c in range(3) for y in range(-2, 6)}
    b = {y: b_ref[y + 3] for y in range(-3, 7)}
    b[-4] = part_frame(refs, row, -4) + 0.5 * below
    b[7] = part_frame(refs, row, 7) - 0.5 * above
    w = {y: w_ref[y + 2] for y in range(-2, 6)}
    w[-3] = laplace(b[-3], b[-4], b[-2])
    w[6] = laplace(b[6], b[5], b[7])
    p = {y: coef_b * b[y] + coef_w * w[y] for y in range(-3, 7)}
    lam = {}
    for y in range(-2, 6):
        lam[0, y] = cot[0, y] - dx(p[y])
        lam[1, y] = cot[1, y] - 0.5 * (p[y + 1] - p[y - 1])
        lam[2, y] = cot[2, y] - dz(p[y])
    vel = {(c, y): vel_frame(refs, row, c, y) for c in range(3) for y in range(-2, 6)}

    flat, upright = {}, {}
    for y in range(-1, 5):
        grad = [[dx(vel[i, y]), 0.5 * (vel[i, y + 1] - vel[i, y - 1]), dz(vel[i, y])] for i in range(3)]
        pull = [[dx(lam[i, y]), 0.5 * (lam[i, y + 1] - lam[i, y - 1]), dz(lam[i, y])] for i in range(3)]
        strain, ebb = {}, {}
        for i in range(3):
            for j in range(i + 1):
                strain[i, j] = grad[i][i] if i == j else 0.5 * (grad[i][j] + grad[j][i])
                ebb[i, j] = pull[i][i] if i == j else 0.5 * (pull[i][j] + pull[j][i])
        squares = strain[0, 0] * strain[0, 0] + strain[1, 1] * strain[1, 1] + strain[2, 2] * strain[2, 2]
        work = strain[0, 0] * ebb[0, 0] + strain[1, 1] * ebb[1, 1] + strain[2, 2] * ebb[2, 2]
        off = strain[1, 0] * strain[1, 0] + strain[2, 0] * strain[2, 0] + strain[2, 1] * strain[2, 1]
        off_work = strain[1, 0] * ebb[1, 0] + strain[2, 0] * ebb[2, 0] + strain[2, 1] * ebb[2, 1]
        inside = 2.0 * (squares + 2.0 * off) + strain_floor
        inverse = lax.rsqrt(inside)
        twice = (2.0 * smag_coef) * (inside * inverse)
        factor = (4.0 * smag_coef) * inverse * (work + 2.0 * off_work)
        stress = {key: twice * ebb[key] + factor * strain[key] for key in strain}

        def both(i, j):
            return stress[max(i, j), min(i, j)] + lam[i, y] * vel[j, y]

        for i in range(3):
            upright[i, y] = both(i, 1)[:TILE]
        if 0 <= y < ROWS:
            for i in range(3):
                carried = lam[0, y] * grad[0][i] + lam[1, y] * grad[1][i] + lam[2, y] * grad[2][i]
                level = dx(both(i, 0)) + dz(both(i, 2))
                flat[i, y] = (lam[i, y] + time_step * (level - carried))[:TILE]
    for i in range(3):
        for y in range(ROWS):
            out_ref[i, y] = flat[i, y] + (0.5 * time_step) * (upright[i, y + 1] - upright[i, y - 1])


def call(kernel, outs, scalars, arrays):
    vmem = pl.BlockSpec(memory_space=pltpu.VMEM)
    smem = pl.BlockSpec(memory_space=pltpu.SMEM)
    return pl.pallas_call(
        kernel,
        out_shape=[jax.ShapeDtypeStruct(s, jnp.float32) for s in outs],
        in_specs=[smem] * len(scalars) + [vmem] * len(arrays),
        out_specs=[vmem] * len(outs),
        compiler_params=pltpu.CompilerParams(vmem_limit_bytes=32 * 1024 * 1024),
    )(*scalars, *arrays)


PY = ("y_low", "z")
PZ = ("y_high", "x", "core")
STEPS = (("z", "core"), ("y_high", "y_low", "x"))


def size(axes):
    return math.prod(lax.axis_size(axis) for axis in axes)


def swap_across(x, axes, reach=1):
    n = size(axes)
    return lax.ppermute(x, axes, [(i, (i + (reach if i // reach % 2 else -reach)) % n) for i in range(n)])


def swap_within(x, axes, reach=1):
    return lax.ppermute(x, axes, [(i, i ^ reach) for i in range(size(axes))])


def body(velocity, cotangent):
    place = lax.axis_index(PY).astype(jnp.int32).reshape(1)
    odd = lax.axis_index("core").astype(jnp.int32).reshape(1)
    block = (3, ROWS, TILE, 256)
    cross, core, cotangent, velocity = call(
        pack_z, [block] * 4, [odd], [jnp.concatenate([cotangent, velocity], axis=0)]
    )
    cross = swap_across(cross, PZ)
    core = swap_within(core, PZ)
    sent = (SENT, TILE, 256)
    far = (TILE, 256)
    first, second, zn, zp, far1, far2 = call(
        pack_y,
        [sent, sent, block, block, far, far],
        [odd, place],
        [cotangent, velocity, cross, core],
    )
    first = swap_across(first, PY)
    second = swap_within(second, PY)
    far1 = swap_across(far1, PY, 2)
    far2 = swap_within(far2, PY, 2)
    lines, b, w, yn, yp = call(
        moments,
        [(size(STEPS[0]), 1, 128), (10, WIDE, 256), (8, WIDE, 256), sent, sent],
        [place],
        [cotangent, velocity, zn, zp, first, second],
    )
    got = lax.all_to_all(lines, STEPS[0], 0, 0)
    (lines,) = call(merge, [(size(STEPS[1]), 1, 128)], [], [got])
    sums = lax.all_to_all(lines, STEPS[1], 0, 0)
    held = [cotangent, velocity, zn, zp, yn, yp, far1, far2]
    (out,) = call(finish, [block], [place], held + [b, w, sums])
    return out


def solution(mesh):
    ny, nz = mesh.shape["py"], mesh.shape["pz"]
    x = min(8, nz // 2)
    shape = (2, ny // 2, nz // (2 * x), x, 2)
    names = ("y_low", "z", "y_high", "x", "core")
    fine = jax.sharding.Mesh(mesh.devices.reshape(shape), names)
    placed = P(None, PY, PZ, None)
    return jax.shard_map(body, mesh=fine, in_specs=(placed, placed), out_specs=placed, check_vma=False)
```

```python
import math

import jax
import jax.numpy as jnp
from jax import lax
from jax.experimental import pallas as pl
from jax.experimental.pallas import tpu as pltpu
from jax.sharding import PartitionSpec as P

smag_coef = 0.1156
time_step = 0.2
strain_floor = 0.25

ROWS = 4
TILE = 8
SIDE = 4
WIDE = TILE + 2 * SIDE
SOON = 6
LATE = 14


def rolled(x, shift, axis):
    return pltpu.roll(x, shift % x.shape[axis], axis)


def dx(f):
    n = f.ndim - 1
    return 0.5 * (rolled(f, -1, n) - rolled(f, 1, n))


def dz(f):
    n = f.ndim - 2
    return 0.5 * (rolled(f, -1, n) - rolled(f, 1, n))


def sublane():
    return lax.broadcasted_iota(jnp.int32, (TILE, 256), 0)


def pack_z(odd_ref, both_ref, cross_ref, core_ref, cot_ref, vel_ref):
    row = sublane()
    even = odd_ref[0] == 0
    for c in range(3):
        for y in range(ROWS):
            cot, vel = both_ref[c, y], both_ref[3 + c, y]
            cot_ref[c, y], vel_ref[c, y] = cot, vel
            to_prev = jnp.where(row < 5, cot, rolled(vel, 5, 0))
            to_next = jnp.where(row >= 3, cot, rolled(vel, 3, 0))
            cross_ref[c, y] = jnp.where(even, to_prev, to_next)
            core_ref[c, y] = jnp.where(even, to_next, to_prev)


def side_cot(row, zn, zp):
    return jnp.where(row < SIDE, zn, zp)


def side_vel(row, zn, zp):
    return jnp.where(row < SIDE, rolled(zn, 3, 0), rolled(zp, 5, 0))


def put(row, tile, k):
    return jnp.where(row < SIDE, rolled(tile, k, 0), rolled(tile, -k, 0))


def take(row, tile, k):
    return jnp.where(row < SIDE, rolled(tile, -k, 0), rolled(tile, k, 0))


def mixed(row, base, inner):
    for k, tile in inner:
        base = jnp.where((row == k) | (row == TILE - 1 - k), put(row, tile, k), base)
    return base


def joined(a, b):
    return jnp.concatenate([a, b], axis=0)


def own_parts(refs, row):
    flat, cot_y = {}, {}
    for y in range(ROWS):
        flat[y] = -(dx(cot_frame(refs, row, 0, y)) + along_z_cot(refs, row, cot_frame(refs, row, 2, y), y))
        cot_y[y] = cot_frame(refs, row, 1, y)
    return flat, cot_y


def paired(place_ref, to_prev, to_next, first_ref, second_ref):
    even = lax.rem(place_ref[0], 2) == 0
    for k in range(first_ref.shape[0]):
        first_ref[k] = jnp.where(even, to_prev[k], to_next[k])
        second_ref[k] = jnp.where(even, to_next[k], to_prev[k])


def unpaired(place_ref, first_ref, second_ref):
    even = lax.rem(place_ref[0], 2) == 0
    tiles = range(first_ref.shape[0])
    after = [jnp.where(even, second_ref[k], first_ref[k]) for k in tiles]
    before = [jnp.where(even, first_ref[k], second_ref[k]) for k in tiles]
    return after, before


def pack_y(odd_ref, place_ref, cot_ref, vel_ref, cross_ref, core_ref, first_ref, second_ref, zn_ref, zp_ref):
    even = odd_ref[0] == 0
    for c in range(3):
        for y in range(ROWS):
            cross, core = cross_ref[c, y], core_ref[c, y]
            zn_ref[c, y] = jnp.where(even, core, cross)
            zp_ref[c, y] = jnp.where(even, cross, core)
    refs = (cot_ref, vel_ref, zn_ref, zp_ref)
    row = sublane()
    flat, cot_y = own_parts(refs, row)
    low = flat[0] - 0.5 * cot_y[1]
    high = flat[3] + 0.5 * cot_y[2]
    one = flat[1] - 0.5 * (cot_y[2] - cot_y[0])
    two = flat[2] - 0.5 * (cot_y[3] - cot_y[1])
    to_prev, to_next = [], []
    for out, part, edge in ((to_prev, (low, one, two), 0), (to_next, (high, two, one), 3)):
        side_x = side_cot(row, zn_ref[0, edge], zp_ref[0, edge])
        side_z = side_cot(row, zn_ref[2, edge], zp_ref[2, edge])
        out.append(part[0][:TILE])
        out.append(part[1][:TILE])
        out.append(cot_y[edge][:TILE])
        out.append(mixed(row, part[0][TILE:], [(3, part[2][TILE:])]))
        out.append(mixed(row, part[1][TILE:], [(2, side_x), (3, side_z)]))
        out.append(cot_y[edge][TILE:])
    paired(place_ref, to_prev, to_next, first_ref, second_ref)


def pack_late(place_ref, refs, row, b, first_ref, second_ref):
    cot_ref, vel_ref, zn_ref, zp_ref = refs
    to_prev, to_next = [], []
    for out, d1, d2, d3, d4 in ((to_prev, 0, 1, 2, 3), (to_next, 3, 2, 1, 0)):
        out += [b[d3][:TILE], b[d4][:TILE], cot_ref[0, d1], cot_ref[2, d1]]
        out += [cot_ref[c, d2] for c in range(3)]
        out += [vel_ref[c, d1] for c in range(3)]
        out += [vel_ref[c, d2] for c in range(3)]
        vel = [side_vel(row, zn_ref[c, d1], zp_ref[c, d1]) for c in range(3)]
        out.append(mixed(row, vel[0], [(1, vel[1]), (2, vel[2])]))
    paired(place_ref, to_prev, to_next, first_ref, second_ref)


def cot_frame(refs, row, c, y):
    cot_ref, _, zn_ref, zp_ref = refs
    return joined(cot_ref[c, y], side_cot(row, zn_ref[c, y], zp_ref[c, y]))


def vel_frame(refs, row, c, y):
    _, vel_ref, zn_ref, zp_ref = refs
    return joined(vel_ref[c, y], side_vel(row, zn_ref[c, y], zp_ref[c, y]))


def along_z_cot(refs, row, frame, y):
    if not 0 <= y < ROWS:
        return dz(frame)
    zn_ref, zp_ref = refs[2], refs[3]
    ends = jnp.where(row < SIDE, zp_ref[2, y], zn_ref[2, y])
    wide = lax.broadcasted_iota(jnp.int32, (WIDE, 256), 0)
    both = joined(ends, ends)
    after = jnp.where(wide == TILE + 3, rolled(both, -1, 0), rolled(frame, -1, 0))
    before = jnp.where(wide == TILE + 4, rolled(both, 1, 0), rolled(frame, 1, 0))
    return 0.5 * (after - before)


def laplace(here, below, above):
    beside = rolled(here, 1, 1) + rolled(here, -1, 1)
    beside = beside + above + below
    beside = beside + rolled(here, 1, 0) + rolled(here, -1, 0)
    return 6.0 * here - beside


def ratio(top, bottom):
    safe = bottom > 0.0
    return jnp.where(safe, top / jnp.where(safe, bottom, 1.0), 0.0)


def total(x):
    return jnp.sum(jnp.sum(x, axis=0, keepdims=True), axis=1, keepdims=True)


def moments(
    place_ref,
    cot_ref,
    vel_ref,
    zn_ref,
    zp_ref,
    first_ref,
    second_ref,
    out_ref,
    b_ref,
    w_ref,
):
    refs = (cot_ref, vel_ref, zn_ref, zp_ref)
    row = sublane()
    after, before = unpaired(place_ref, first_ref, second_ref)
    flat, cot_y = own_parts(refs, row)
    cot_y[-1], cot_y[4] = joined(before[2], before[5]), joined(after[2], after[5])
    b = {y: flat[y] - 0.5 * (cot_y[y + 1] - cot_y[y - 1]) for y in range(ROWS)}
    b[-1] = joined(before[0], before[3]) - 0.5 * cot_y[0]
    b[4] = joined(after[0], after[3]) + 0.5 * cot_y[3]
    b[-2] = joined(before[1], before[4])
    b[5] = joined(after[1], after[4])
    w = {y: laplace(b[y], b[y - 1], b[y + 1]) for y in range(-1, 5)}
    m0 = m1 = None
    for y in range(ROWS):
        bc, wc = b[y][:TILE], w[y][:TILE]
        m0 = bc * bc if m0 is None else m0 + bc * bc
        m1 = bc * wc if m1 is None else m1 + bc * wc
    m0, m1 = total(m0), total(m1)
    sigma = ratio(m1, m0)
    spread = third = cross = None
    for y in range(ROWS):
        bc, wc = b[y][:TILE], w[y][:TILE]
        x = laplace(w[y], w[y - 1], w[y + 1])[:TILE]
        v = wc - sigma * bc
        u = x - sigma * wc
        spread = v * v if spread is None else spread + v * v
        third = v * u if third is None else third + v * u
        cross = bc * u if cross is None else cross + bc * u
    spread, third, cross = total(spread), total(third), total(cross)
    spread_out((m0, m1, spread, third, cross), out_ref)
    for y in range(-2, 6):
        b_ref[y + 2] = b[y]
    for y in range(-1, 5):
        w_ref[y + 1] = w[y]


def spread_out(parts, out_ref):
    lane = lax.broadcasted_iota(jnp.int32, (1, 128), 1)
    line = jnp.zeros((1, 128), jnp.float32)
    for k, value in enumerate(parts):
        line = jnp.where(lane == k, value, line)
    for j in range(out_ref.shape[0]):
        out_ref[j] = line


def gathered(got_ref):
    lines = got_ref[...].reshape(got_ref.shape[0], 128)
    return [x[:, :1] for x in merged(*[rolled(lines, -k, 1) for k in range(5)])]


def merged(m0, m1, spread, third, cross):
    own = ratio(m1, m0)

    def over(x):
        return jnp.sum(x, axis=0, keepdims=True)

    all0, all1 = over(m0), over(m1)
    delta = ratio(all1, all0) - own
    all_spread = over(spread + delta * delta * m0)
    all_third = over(third - delta * (spread + cross) + delta * delta * m1)
    all_cross = over(cross - delta * m1)
    return all0, all1, all_spread, all_third, all_cross


def merge(place_ref, got_ref, cot_ref, vel_ref, zn_ref, zp_ref, b_ref, out_ref, late1_ref, late2_ref):
    spread_out(gathered(got_ref), out_ref)
    b = {y: b_ref[y + 2] for y in range(ROWS)}
    pack_late(place_ref, (cot_ref, vel_ref, zn_ref, zp_ref), sublane(), b, late1_ref, late2_ref)


def slope(vel, y, grad_ref, inverse_ref, at):
    grad = [[dx(vel[i, y]), 0.5 * (vel[i, y + 1] - vel[i, y - 1]), dz(vel[i, y])] for i in range(3)]
    inside = None
    for i in range(3):
        for j in range(3):
            grad_ref[at, 3 * i + j] = grad[i][j]
        for j in range(i + 1):
            strain = grad[i][i] if i == j else 0.5 * (grad[i][j] + grad[j][i])
            square = (1.0 if i == j else 2.0) * (strain * strain)
            inside = square if inside is None else inside + square
    inverse_ref[at] = lax.rsqrt(2.0 * inside + strain_floor)


INNER = (1, 2)
OUTER = (-1, 0, 3, 4)


def inner_slopes(cot_ref, vel_ref, zn_ref, zp_ref, lines_ref, grad_ref, inverse_ref):
    refs = (cot_ref, vel_ref, zn_ref, zp_ref)
    row = sublane()
    vel = {(c, y): vel_frame(refs, row, c, y) for c in range(3) for y in range(ROWS)}
    for at, y in enumerate(INNER):
        slope(vel, y, grad_ref, inverse_ref, at)


def outer_slopes(place_ref, cot_ref, vel_ref, zn_ref, zp_ref, late1_ref, late2_ref, grad_ref, inverse_ref):
    refs = (cot_ref, vel_ref, zn_ref, zp_ref)
    row = sublane()
    vel = {(c, y): vel_frame(refs, row, c, y) for c in range(3) for y in range(ROWS)}
    late = unpaired(place_ref, late1_ref, late2_ref)
    for got, edge, step in ((late[0], ROWS - 1, 1), (late[1], 0, -1)):
        for c in range(3):
            vel[c, edge + step] = joined(got[7 + c], take(row, got[13], c))
            vel[c, edge + 2 * step] = joined(got[10 + c], got[10 + c])
    for at, y in enumerate(OUTER):
        slope(vel, y, grad_ref, inverse_ref, at)


def finish(
    place_ref,
    cot_ref,
    vel_ref,
    zn_ref,
    zp_ref,
    first_ref,
    second_ref,
    late1_ref,
    late2_ref,
    b_ref,
    w_ref,
    inner_grad_ref,
    inner_inverse_ref,
    outer_grad_ref,
    outer_inverse_ref,
    sums_ref,
    out_ref,
):
    refs = (cot_ref, vel_ref, zn_ref, zp_ref)
    row = sublane()
    m0, m1, spread, third, _ = gathered(sums_ref)
    step0 = m0 / m1
    norm1 = step0 * step0 * spread
    beta = norm1 / m0
    bend = step0 * step0 * third - 2.0 * step0 * beta * spread + beta * beta * m1
    step1 = norm1 / bend
    coef_b = step0 + step1 * (1.0 + beta)
    coef_w = -(step1 * step0)

    b = {y: b_ref[y + 2] for y in range(-2, 6)}
    w = {y: w_ref[y + 1] for y in range(-1, 5)}
    cot = {(c, y): cot_frame(refs, row, c, y) for c in range(3) for y in range(ROWS)}
    vel = {(c, y): vel_frame(refs, row, c, y) for c in range(3) for y in range(ROWS)}
    soon = unpaired(place_ref, first_ref, second_ref)
    late = unpaired(place_ref, late1_ref, late2_ref)
    for side, edge, step in ((0, ROWS - 1, 1), (1, 0, -1)):
        near, got = soon[side], late[side]
        y1, y2, y3, y4 = [edge + step * d for d in range(1, 5)]
        b[y3] = joined(got[0], take(row, near[3], 3))
        b[y4] = joined(got[1], got[1])
        cot[0, y1] = joined(got[2], take(row, near[4], 2))
        cot[1, y1] = joined(near[2], near[5])
        cot[2, y1] = joined(got[3], take(row, near[4], 3))
        for c in range(3):
            cot[c, y2] = joined(got[4 + c], got[4 + c])
            vel[c, y1] = joined(got[7 + c], take(row, got[13], c))
            vel[c, y2] = joined(got[10 + c], got[10 + c])
    for y in (-3, -2, 5, 6):
        w[y] = laplace(b[y], b[y - 1], b[y + 1])
    p = {y: coef_b * b[y] + coef_w * w[y] for y in range(-3, 7)}
    lam = {}
    for y in range(-2, 6):
        lam[0, y] = cot[0, y] - dx(p[y])
        lam[1, y] = cot[1, y] - 0.5 * (p[y + 1] - p[y - 1])
        lam[2, y] = cot[2, y] - dz(p[y])

    flat, upright = {}, {}
    for y in range(-1, 5):
        grad_ref, inverse_ref, rows = (
            (inner_grad_ref, inner_inverse_ref, INNER)
            if y in INNER
            else (outer_grad_ref, outer_inverse_ref, OUTER)
        )
        at = rows.index(y)
        grad = [[grad_ref[at, 3 * i + j] for j in range(3)] for i in range(3)]
        pull = [[dx(lam[i, y]), 0.5 * (lam[i, y + 1] - lam[i, y - 1]), dz(lam[i, y])] for i in range(3)]
        strain, ebb = {}, {}
        for i in range(3):
            for j in range(i + 1):
                strain[i, j] = grad[i][i] if i == j else 0.5 * (grad[i][j] + grad[j][i])
                ebb[i, j] = pull[i][i] if i == j else 0.5 * (pull[i][j] + pull[j][i])
        work = strain[0, 0] * ebb[0, 0] + strain[1, 1] * ebb[1, 1] + strain[2, 2] * ebb[2, 2]
        off_work = strain[1, 0] * ebb[1, 0] + strain[2, 0] * ebb[2, 0] + strain[2, 1] * ebb[2, 1]
        inverse = inverse_ref[at]
        twice = (2.0 * smag_coef) / inverse
        factor = (4.0 * smag_coef) * inverse * (work + 2.0 * off_work)
        stress = {key: twice * ebb[key] + factor * strain[key] for key in strain}

        def both(i, j):
            return stress[max(i, j), min(i, j)] + lam[i, y] * vel[j, y]

        for i in range(3):
            upright[i, y] = both(i, 1)[:TILE]
        if 0 <= y < ROWS:
            for i in range(3):
                carried = lam[0, y] * grad[0][i] + lam[1, y] * grad[1][i] + lam[2, y] * grad[2][i]
                level = dx(both(i, 0)) + dz(both(i, 2))
                flat[i, y] = (lam[i, y] + time_step * (level - carried))[:TILE]
    for i in range(3):
        for y in range(ROWS):
            out_ref[i, y] = flat[i, y] + (0.5 * time_step) * (upright[i, y + 1] - upright[i, y - 1])


def call(kernel, outs, scalars, arrays, cost=None):
    vmem = pl.BlockSpec(memory_space=pltpu.VMEM)
    smem = pl.BlockSpec(memory_space=pltpu.SMEM)
    return pl.pallas_call(
        kernel,
        out_shape=[jax.ShapeDtypeStruct(s, jnp.float32) for s in outs],
        in_specs=[smem] * len(scalars) + [vmem] * len(arrays),
        out_specs=[vmem] * len(outs),
        cost_estimate=cost and pl.CostEstimate(flops=cost, bytes_accessed=2_000_000, transcendentals=100_000),
        compiler_params=pltpu.CompilerParams(vmem_limit_bytes=32 * 1024 * 1024),
    )(*scalars, *arrays)


PY = ("y_low", "z")
PZ = ("y_high", "x", "core")
STEPS = (("z", "core"), ("y_high", "y_low", "x"))


def size(axes):
    return math.prod(lax.axis_size(axis) for axis in axes)


def swap_across(x, axes):
    n = size(axes)
    return lax.ppermute(x, axes, [(i, (i + 1 if i % 2 else i - 1) % n) for i in range(n)])


def swap_within(x, axes):
    return lax.ppermute(x, axes, [(i, i ^ 1) for i in range(size(axes))])


def body(velocity, cotangent):
    place = lax.axis_index(PY).astype(jnp.int32).reshape(1)
    odd = lax.axis_index("core").astype(jnp.int32).reshape(1)
    block = (3, ROWS, TILE, 256)
    cross, core, cotangent, velocity = call(
        pack_z, [block] * 4, [odd], [jnp.concatenate([cotangent, velocity], axis=0)]
    )
    cross = swap_across(cross, PZ)
    core = swap_within(core, PZ)
    soon, later = (SOON, TILE, 256), (LATE, TILE, 256)
    first, second, zn, zp = call(
        pack_y, [soon, soon, block, block], [odd, place], [cotangent, velocity, cross, core]
    )
    held = [cotangent, velocity, zn, zp, swap_across(first, PY), swap_within(second, PY)]
    lines, b, w = call(
        moments,
        [(size(STEPS[0]), 1, 128), (8, WIDE, 256), (6, WIDE, 256)],
        [place],
        held,
    )
    got = lax.all_to_all(lines, STEPS[0], 0, 0)
    lines, late1, late2 = call(
        merge, [(size(STEPS[1]), 1, 128), later, later], [place], [got] + held[:4] + [b]
    )
    sums = lax.all_to_all(lines, STEPS[1], 0, 0)
    late = [swap_across(late1, PY), swap_within(late2, PY)]
    inner = call(inner_slopes, [(2, 9, WIDE, 256), (2, WIDE, 256)], [], held[:4] + [lines], 4_000_000_000)
    outer = call(outer_slopes, [(4, 9, WIDE, 256), (4, WIDE, 256)], [place], held[:4] + late, 4_000_000)
    (out,) = call(finish, [block], [place], held + late + [b, w, *inner, *outer, sums])
    return out


def solution(mesh):
    ny, nz = mesh.shape["py"], mesh.shape["pz"]
    x = min(8, nz // 2)
    shape = (2, ny // 2, nz // (2 * x), x, 2)
    names = ("y_low", "z", "y_high", "x", "core")
    fine = jax.sharding.Mesh(mesh.devices.reshape(shape), names)
    placed = P(None, PY, PZ, None)
    return jax.shard_map(body, mesh=fine, in_specs=(placed, placed), out_specs=placed, check_vma=False)
```

```python
import math

import jax
import jax.numpy as jnp
from jax import lax
from jax.experimental import pallas as pl
from jax.experimental.pallas import tpu as pltpu
from jax.sharding import PartitionSpec as P

smag_coef = 0.1156
time_step = 0.2
strain_floor = 0.25

ROWS = 4
TILE = 8
SIDE = 4
WIDE = TILE + 2 * SIDE
SOON = 6
LATE = 14


def rolled(x, shift, axis):
    return pltpu.roll(x, shift % x.shape[axis], axis)


def dx(f):
    n = f.ndim - 1
    return 0.5 * (rolled(f, -1, n) - rolled(f, 1, n))


def dz(f):
    n = f.ndim - 2
    return 0.5 * (rolled(f, -1, n) - rolled(f, 1, n))


def sublane():
    return lax.broadcasted_iota(jnp.int32, (TILE, 256), 0)


def pack_z(odd_ref, both_ref, cross_ref, core_ref, cot_ref, vel_ref):
    row = sublane()
    even = odd_ref[0] == 0
    for c in range(3):
        for y in range(ROWS):
            cot, vel = both_ref[c, y], both_ref[3 + c, y]
            cot_ref[c, y], vel_ref[c, y] = cot, vel
            to_prev = jnp.where(row < 5, cot, rolled(vel, 5, 0))
            to_next = jnp.where(row >= 3, cot, rolled(vel, 3, 0))
            cross_ref[c, y] = jnp.where(even, to_prev, to_next)
            core_ref[c, y] = jnp.where(even, to_next, to_prev)


def side_cot(row, zn, zp):
    return jnp.where(row < SIDE, zn, zp)


def side_vel(row, zn, zp):
    return jnp.where(row < SIDE, rolled(zn, 3, 0), rolled(zp, 5, 0))


def put(row, tile, k):
    return jnp.where(row < SIDE, rolled(tile, k, 0), rolled(tile, -k, 0))


def take(row, tile, k):
    return jnp.where(row < SIDE, rolled(tile, -k, 0), rolled(tile, k, 0))


def mixed(row, base, inner):
    for k, tile in inner:
        base = jnp.where((row == k) | (row == TILE - 1 - k), put(row, tile, k), base)
    return base


def joined(a, b):
    return jnp.concatenate([a, b], axis=0)


def own_parts(refs, row):
    flat, cot_y = {}, {}
    for y in range(ROWS):
        flat[y] = -(dx(cot_frame(refs, row, 0, y)) + along_z_cot(refs, row, cot_frame(refs, row, 2, y), y))
        cot_y[y] = cot_frame(refs, row, 1, y)
    return flat, cot_y


def paired(place_ref, to_prev, to_next, first_ref, second_ref):
    even = lax.rem(place_ref[0], 2) == 0
    for k in range(first_ref.shape[0]):
        first_ref[k] = jnp.where(even, to_prev[k], to_next[k])
        second_ref[k] = jnp.where(even, to_next[k], to_prev[k])


def unpaired(place_ref, first_ref, second_ref):
    even = lax.rem(place_ref[0], 2) == 0
    tiles = range(first_ref.shape[0])
    after = [jnp.where(even, second_ref[k], first_ref[k]) for k in tiles]
    before = [jnp.where(even, first_ref[k], second_ref[k]) for k in tiles]
    return after, before


def pack_y(odd_ref, place_ref, cot_ref, vel_ref, cross_ref, core_ref, first_ref, second_ref, zn_ref, zp_ref):
    even = odd_ref[0] == 0
    for c in range(3):
        for y in range(ROWS):
            cross, core = cross_ref[c, y], core_ref[c, y]
            zn_ref[c, y] = jnp.where(even, core, cross)
            zp_ref[c, y] = jnp.where(even, cross, core)
    refs = (cot_ref, vel_ref, zn_ref, zp_ref)
    row = sublane()
    flat, cot_y = own_parts(refs, row)
    low = flat[0] - 0.5 * cot_y[1]
    high = flat[3] + 0.5 * cot_y[2]
    one = flat[1] - 0.5 * (cot_y[2] - cot_y[0])
    two = flat[2] - 0.5 * (cot_y[3] - cot_y[1])
    to_prev, to_next = [], []
    for out, part, edge in ((to_prev, (low, one, two), 0), (to_next, (high, two, one), 3)):
        side_x = side_cot(row, zn_ref[0, edge], zp_ref[0, edge])
        side_z = side_cot(row, zn_ref[2, edge], zp_ref[2, edge])
        out.append(part[0][:TILE])
        out.append(part[1][:TILE])
        out.append(cot_y[edge][:TILE])
        out.append(mixed(row, part[0][TILE:], [(3, part[2][TILE:])]))
        out.append(mixed(row, part[1][TILE:], [(2, side_x), (3, side_z)]))
        out.append(cot_y[edge][TILE:])
    paired(place_ref, to_prev, to_next, first_ref, second_ref)


def pack_late(place_ref, refs, row, b, first_ref, second_ref):
    cot_ref, vel_ref, zn_ref, zp_ref = refs
    to_prev, to_next = [], []
    for out, d1, d2, d3, d4 in ((to_prev, 0, 1, 2, 3), (to_next, 3, 2, 1, 0)):
        out += [b[d3][:TILE], b[d4][:TILE], cot_ref[0, d1], cot_ref[2, d1]]
        out += [cot_ref[c, d2] for c in range(3)]
        out += [vel_ref[c, d1] for c in range(3)]
        out += [vel_ref[c, d2] for c in range(3)]
        vel = [side_vel(row, zn_ref[c, d1], zp_ref[c, d1]) for c in range(3)]
        out.append(mixed(row, vel[0], [(1, vel[1]), (2, vel[2])]))
    paired(place_ref, to_prev, to_next, first_ref, second_ref)


def cot_frame(refs, row, c, y):
    cot_ref, _, zn_ref, zp_ref = refs
    return joined(cot_ref[c, y], side_cot(row, zn_ref[c, y], zp_ref[c, y]))


def vel_frame(refs, row, c, y):
    _, vel_ref, zn_ref, zp_ref = refs
    return joined(vel_ref[c, y], side_vel(row, zn_ref[c, y], zp_ref[c, y]))


def along_z_cot(refs, row, frame, y):
    if not 0 <= y < ROWS:
        return dz(frame)
    zn_ref, zp_ref = refs[2], refs[3]
    ends = jnp.where(row < SIDE, zp_ref[2, y], zn_ref[2, y])
    wide = lax.broadcasted_iota(jnp.int32, (WIDE, 256), 0)
    both = joined(ends, ends)
    after = jnp.where(wide == TILE + 3, rolled(both, -1, 0), rolled(frame, -1, 0))
    before = jnp.where(wide == TILE + 4, rolled(both, 1, 0), rolled(frame, 1, 0))
    return 0.5 * (after - before)


def laplace(here, below, above):
    beside = rolled(here, 1, 1) + rolled(here, -1, 1)
    beside = beside + above + below
    beside = beside + rolled(here, 1, 0) + rolled(here, -1, 0)
    return 6.0 * here - beside


def ratio(top, bottom):
    safe = bottom > 0.0
    return jnp.where(safe, top / jnp.where(safe, bottom, 1.0), 0.0)


def total(x):
    return jnp.sum(jnp.sum(x, axis=0, keepdims=True), axis=1, keepdims=True)


def moments(
    place_ref,
    cot_ref,
    vel_ref,
    zn_ref,
    zp_ref,
    first_ref,
    second_ref,
    out_ref,
    b_ref,
    w_ref,
    late1_ref,
    late2_ref,
):
    refs = (cot_ref, vel_ref, zn_ref, zp_ref)
    row = sublane()
    after, before = unpaired(place_ref, first_ref, second_ref)
    flat, cot_y = own_parts(refs, row)
    cot_y[-1], cot_y[4] = joined(before[2], before[5]), joined(after[2], after[5])
    b = {y: flat[y] - 0.5 * (cot_y[y + 1] - cot_y[y - 1]) for y in range(ROWS)}
    b[-1] = joined(before[0], before[3]) - 0.5 * cot_y[0]
    b[4] = joined(after[0], after[3]) + 0.5 * cot_y[3]
    b[-2] = joined(before[1], before[4])
    b[5] = joined(after[1], after[4])
    w = {y: laplace(b[y], b[y - 1], b[y + 1]) for y in range(-1, 5)}
    m0 = m1 = None
    for y in range(ROWS):
        bc, wc = b[y][:TILE], w[y][:TILE]
        m0 = bc * bc if m0 is None else m0 + bc * bc
        m1 = bc * wc if m1 is None else m1 + bc * wc
    m0, m1 = total(m0), total(m1)
    sigma = ratio(m1, m0)
    spread = third = cross = None
    for y in range(ROWS):
        bc, wc = b[y][:TILE], w[y][:TILE]
        x = laplace(w[y], w[y - 1], w[y + 1])[:TILE]
        v = wc - sigma * bc
        u = x - sigma * wc
        spread = v * v if spread is None else spread + v * v
        third = v * u if third is None else third + v * u
        cross = bc * u if cross is None else cross + bc * u
    spread, third, cross = total(spread), total(third), total(cross)
    spread_out((m0, m1, spread, third, cross), out_ref)
    for y in range(-2, 6):
        b_ref[y + 2] = b[y]
    for y in range(-1, 5):
        w_ref[y + 1] = w[y]
    pack_late(place_ref, refs, row, b, late1_ref, late2_ref)


def spread_out(parts, out_ref):
    lane = lax.broadcasted_iota(jnp.int32, (1, 128), 1)
    line = jnp.zeros((1, 128), jnp.float32)
    for k, value in enumerate(parts):
        line = jnp.where(lane == k, value, line)
    for j in range(out_ref.shape[0]):
        out_ref[j] = line


def gathered(got_ref):
    lines = got_ref[...].reshape(got_ref.shape[0], 128)
    return [x[:, :1] for x in merged(*[rolled(lines, -k, 1) for k in range(5)])]


def merged(m0, m1, spread, third, cross):
    own = ratio(m1, m0)

    def over(x):
        return jnp.sum(x, axis=0, keepdims=True)

    all0, all1 = over(m0), over(m1)
    delta = ratio(all1, all0) - own
    all_spread = over(spread + delta * delta * m0)
    all_third = over(third - delta * (spread + cross) + delta * delta * m1)
    all_cross = over(cross - delta * m1)
    return all0, all1, all_spread, all_third, all_cross


def merge(got_ref, out_ref):
    spread_out(gathered(got_ref), out_ref)


def slope(vel, y, grad_ref, inverse_ref, at):
    grad = [[dx(vel[i, y]), 0.5 * (vel[i, y + 1] - vel[i, y - 1]), dz(vel[i, y])] for i in range(3)]
    inside = None
    for i in range(3):
        for j in range(3):
            grad_ref[at, 3 * i + j] = grad[i][j]
        for j in range(i + 1):
            strain = grad[i][i] if i == j else 0.5 * (grad[i][j] + grad[j][i])
            square = (1.0 if i == j else 2.0) * (strain * strain)
            inside = square if inside is None else inside + square
    inverse_ref[at] = lax.rsqrt(2.0 * inside + strain_floor)


INNER = (1, 2)
OUTER = (-1, 0, 3, 4)


def inner_slopes(cot_ref, vel_ref, zn_ref, zp_ref, lines_ref, grad_ref, inverse_ref):
    refs = (cot_ref, vel_ref, zn_ref, zp_ref)
    row = sublane()
    vel = {(c, y): vel_frame(refs, row, c, y) for c in range(3) for y in range(ROWS)}
    for at, y in enumerate(INNER):
        slope(vel, y, grad_ref, inverse_ref, at)


def outer_slopes(place_ref, cot_ref, vel_ref, zn_ref, zp_ref, late1_ref, late2_ref, grad_ref, inverse_ref):
    refs = (cot_ref, vel_ref, zn_ref, zp_ref)
    row = sublane()
    vel = {(c, y): vel_frame(refs, row, c, y) for c in range(3) for y in range(ROWS)}
    late = unpaired(place_ref, late1_ref, late2_ref)
    for got, edge, step in ((late[0], ROWS - 1, 1), (late[1], 0, -1)):
        for c in range(3):
            vel[c, edge + step] = joined(got[7 + c], take(row, got[13], c))
            vel[c, edge + 2 * step] = joined(got[10 + c], got[10 + c])
    for at, y in enumerate(OUTER):
        slope(vel, y, grad_ref, inverse_ref, at)


def finish(
    place_ref,
    cot_ref,
    vel_ref,
    zn_ref,
    zp_ref,
    first_ref,
    second_ref,
    late1_ref,
    late2_ref,
    b_ref,
    w_ref,
    inner_grad_ref,
    inner_inverse_ref,
    outer_grad_ref,
    outer_inverse_ref,
    sums_ref,
    out_ref,
):
    refs = (cot_ref, vel_ref, zn_ref, zp_ref)
    row = sublane()
    m0, m1, spread, third, _ = gathered(sums_ref)
    step0 = m0 / m1
    norm1 = step0 * step0 * spread
    beta = norm1 / m0
    bend = step0 * step0 * third - 2.0 * step0 * beta * spread + beta * beta * m1
    step1 = norm1 / bend
    coef_b = step0 + step1 * (1.0 + beta)
    coef_w = -(step1 * step0)

    b = {y: b_ref[y + 2] for y in range(-2, 6)}
    w = {y: w_ref[y + 1] for y in range(-1, 5)}
    cot = {(c, y): cot_frame(refs, row, c, y) for c in range(3) for y in range(ROWS)}
    vel = {(c, y): vel_frame(refs, row, c, y) for c in range(3) for y in range(ROWS)}
    soon = unpaired(place_ref, first_ref, second_ref)
    late = unpaired(place_ref, late1_ref, late2_ref)
    for side, edge, step in ((0, ROWS - 1, 1), (1, 0, -1)):
        near, got = soon[side], late[side]
        y1, y2, y3, y4 = [edge + step * d for d in range(1, 5)]
        b[y3] = joined(got[0], take(row, near[3], 3))
        b[y4] = joined(got[1], got[1])
        cot[0, y1] = joined(got[2], take(row, near[4], 2))
        cot[1, y1] = joined(near[2], near[5])
        cot[2, y1] = joined(got[3], take(row, near[4], 3))
        for c in range(3):
            cot[c, y2] = joined(got[4 + c], got[4 + c])
            vel[c, y1] = joined(got[7 + c], take(row, got[13], c))
            vel[c, y2] = joined(got[10 + c], got[10 + c])
    for y in (-3, -2, 5, 6):
        w[y] = laplace(b[y], b[y - 1], b[y + 1])
    p = {y: coef_b * b[y] + coef_w * w[y] for y in range(-3, 7)}
    lam = {}
    for y in range(-2, 6):
        lam[0, y] = cot[0, y] - dx(p[y])
        lam[1, y] = cot[1, y] - 0.5 * (p[y + 1] - p[y - 1])
        lam[2, y] = cot[2, y] - dz(p[y])

    flat, upright = {}, {}
    for y in range(-1, 5):
        grad_ref, inverse_ref, rows = (
            (inner_grad_ref, inner_inverse_ref, INNER)
            if y in INNER
            else (outer_grad_ref, outer_inverse_ref, OUTER)
        )
        at = rows.index(y)
        grad = [[grad_ref[at, 3 * i + j] for j in range(3)] for i in range(3)]
        pull = [[dx(lam[i, y]), 0.5 * (lam[i, y + 1] - lam[i, y - 1]), dz(lam[i, y])] for i in range(3)]
        strain, ebb = {}, {}
        for i in range(3):
            for j in range(i + 1):
                strain[i, j] = grad[i][i] if i == j else 0.5 * (grad[i][j] + grad[j][i])
                ebb[i, j] = pull[i][i] if i == j else 0.5 * (pull[i][j] + pull[j][i])
        work = strain[0, 0] * ebb[0, 0] + strain[1, 1] * ebb[1, 1] + strain[2, 2] * ebb[2, 2]
        off_work = strain[1, 0] * ebb[1, 0] + strain[2, 0] * ebb[2, 0] + strain[2, 1] * ebb[2, 1]
        inverse = inverse_ref[at]
        twice = (2.0 * smag_coef) / inverse
        factor = (4.0 * smag_coef) * inverse * (work + 2.0 * off_work)
        stress = {key: twice * ebb[key] + factor * strain[key] for key in strain}

        def both(i, j):
            return stress[max(i, j), min(i, j)] + lam[i, y] * vel[j, y]

        for i in range(3):
            upright[i, y] = both(i, 1)[:TILE]
        if 0 <= y < ROWS:
            for i in range(3):
                carried = lam[0, y] * grad[0][i] + lam[1, y] * grad[1][i] + lam[2, y] * grad[2][i]
                level = dx(both(i, 0)) + dz(both(i, 2))
                flat[i, y] = (lam[i, y] + time_step * (level - carried))[:TILE]
    for i in range(3):
        for y in range(ROWS):
            out_ref[i, y] = flat[i, y] + (0.5 * time_step) * (upright[i, y + 1] - upright[i, y - 1])


def call(kernel, outs, scalars, arrays, cost=None):
    vmem = pl.BlockSpec(memory_space=pltpu.VMEM)
    smem = pl.BlockSpec(memory_space=pltpu.SMEM)
    return pl.pallas_call(
        kernel,
        out_shape=[jax.ShapeDtypeStruct(s, jnp.float32) for s in outs],
        in_specs=[smem] * len(scalars) + [vmem] * len(arrays),
        out_specs=[vmem] * len(outs),
        cost_estimate=cost and pl.CostEstimate(flops=cost, bytes_accessed=2_000_000, transcendentals=100_000),
        compiler_params=pltpu.CompilerParams(vmem_limit_bytes=32 * 1024 * 1024),
    )(*scalars, *arrays)


PY = ("y_low", "z")
PZ = ("y_high", "x", "core")
STEPS = (("y_high", "y_low", "x"), ("z", "core"))


def size(axes):
    return math.prod(lax.axis_size(axis) for axis in axes)


def swap_across(x, axes):
    n = size(axes)
    return lax.ppermute(x, axes, [(i, (i + 1 if i % 2 else i - 1) % n) for i in range(n)])


def swap_within(x, axes):
    return lax.ppermute(x, axes, [(i, i ^ 1) for i in range(size(axes))])


def body(velocity, cotangent):
    place = lax.axis_index(PY).astype(jnp.int32).reshape(1)
    odd = lax.axis_index("core").astype(jnp.int32).reshape(1)
    block = (3, ROWS, TILE, 256)
    cross, core, cotangent, velocity = call(
        pack_z, [block] * 4, [odd], [jnp.concatenate([cotangent, velocity], axis=0)]
    )
    cross = swap_across(cross, PZ)
    core = swap_within(core, PZ)
    soon, later = (SOON, TILE, 256), (LATE, TILE, 256)
    first, second, zn, zp = call(
        pack_y, [soon, soon, block, block], [odd, place], [cotangent, velocity, cross, core]
    )
    held = [cotangent, velocity, zn, zp, swap_across(first, PY), swap_within(second, PY)]
    lines, b, w, late1, late2 = call(
        moments,
        [(size(STEPS[0]), 1, 128), (8, WIDE, 256), (6, WIDE, 256), later, later],
        [place],
        held,
    )
    got = lax.all_to_all(lines, STEPS[0], 0, 0)
    late = [swap_across(late1, PY), swap_within(late2, PY)]
    inner = call(inner_slopes, [(2, 9, WIDE, 256), (2, WIDE, 256)], [], held[:4] + [lines], 4_000_000_000)
    outer = call(outer_slopes, [(4, 9, WIDE, 256), (4, WIDE, 256)], [place], held[:4] + late, 4_000_000)
    (lines,) = call(merge, [(size(STEPS[1]), 1, 128)], [], [got])
    sums = lax.all_to_all(lines, STEPS[1], 0, 0)
    (out,) = call(finish, [block], [place], held + late + [b, w, *inner, *outer, sums])
    return out


def solution(mesh):
    ny, nz = mesh.shape["py"], mesh.shape["pz"]
    x = min(8, nz // 2)
    shape = (2, ny // 2, nz // (2 * x), x, 2)
    names = ("y_low", "z", "y_high", "x", "core")
    fine = jax.sharding.Mesh(mesh.devices.reshape(shape), names)
    placed = P(None, PY, PZ, None)
    return jax.shard_map(body, mesh=fine, in_specs=(placed, placed), out_specs=placed, check_vma=False)
```

```python
import math

import jax
import jax.numpy as jnp
from jax import lax
from jax.experimental import pallas as pl
from jax.experimental.pallas import tpu as pltpu
from jax.sharding import PartitionSpec as P

smag_coef = 0.1156
time_step = 0.2
strain_floor = 0.25

ROWS = 4
TILE = 8
SIDE = 4
WIDE = TILE + 2 * SIDE
SOON = 6
LATE = 14


def rolled(x, shift, axis):
    return pltpu.roll(x, shift % x.shape[axis], axis)


def dx(f):
    n = f.ndim - 1
    return 0.5 * (rolled(f, -1, n) - rolled(f, 1, n))


def dz(f):
    n = f.ndim - 2
    return 0.5 * (rolled(f, -1, n) - rolled(f, 1, n))


def sublane():
    return lax.broadcasted_iota(jnp.int32, (TILE, 256), 0)


def pack_z(odd_ref, both_ref, cross_ref, core_ref, cot_ref, vel_ref):
    row = sublane()
    even = odd_ref[0] == 0
    for c in range(3):
        for y in range(ROWS):
            cot, vel = both_ref[c, y], both_ref[3 + c, y]
            cot_ref[c, y], vel_ref[c, y] = cot, vel
            to_prev = jnp.where(row < 5, cot, rolled(vel, 5, 0))
            to_next = jnp.where(row >= 3, cot, rolled(vel, 3, 0))
            cross_ref[c, y] = jnp.where(even, to_prev, to_next)
            core_ref[c, y] = jnp.where(even, to_next, to_prev)


def side_cot(row, zn, zp):
    return jnp.where(row < SIDE, zn, zp)


def side_vel(row, zn, zp):
    return jnp.where(row < SIDE, rolled(zn, 3, 0), rolled(zp, 5, 0))


def put(row, tile, k):
    return jnp.where(row < SIDE, rolled(tile, k, 0), rolled(tile, -k, 0))


def take(row, tile, k):
    return jnp.where(row < SIDE, rolled(tile, -k, 0), rolled(tile, k, 0))


def mixed(row, base, inner):
    for k, tile in inner:
        base = jnp.where((row == k) | (row == TILE - 1 - k), put(row, tile, k), base)
    return base


def joined(a, b):
    return jnp.concatenate([a, b], axis=0)


def own_parts(refs, row):
    flat, cot_y = {}, {}
    for y in range(ROWS):
        flat[y] = -(dx(cot_frame(refs, row, 0, y)) + along_z_cot(refs, row, cot_frame(refs, row, 2, y), y))
        cot_y[y] = cot_frame(refs, row, 1, y)
    return flat, cot_y


def paired(place_ref, to_prev, to_next, first_ref, second_ref):
    even = lax.rem(place_ref[0], 2) == 0
    for k in range(first_ref.shape[0]):
        first_ref[k] = jnp.where(even, to_prev[k], to_next[k])
        second_ref[k] = jnp.where(even, to_next[k], to_prev[k])


def unpaired(place_ref, first_ref, second_ref):
    even = lax.rem(place_ref[0], 2) == 0
    tiles = range(first_ref.shape[0])
    after = [jnp.where(even, second_ref[k], first_ref[k]) for k in tiles]
    before = [jnp.where(even, first_ref[k], second_ref[k]) for k in tiles]
    return after, before


def pack_y(odd_ref, place_ref, cot_ref, vel_ref, cross_ref, core_ref, first_ref, second_ref, zn_ref, zp_ref):
    even = odd_ref[0] == 0
    for c in range(3):
        for y in range(ROWS):
            cross, core = cross_ref[c, y], core_ref[c, y]
            zn_ref[c, y] = jnp.where(even, core, cross)
            zp_ref[c, y] = jnp.where(even, cross, core)
    refs = (cot_ref, vel_ref, zn_ref, zp_ref)
    row = sublane()
    flat, cot_y = own_parts(refs, row)
    low = flat[0] - 0.5 * cot_y[1]
    high = flat[3] + 0.5 * cot_y[2]
    one = flat[1] - 0.5 * (cot_y[2] - cot_y[0])
    two = flat[2] - 0.5 * (cot_y[3] - cot_y[1])
    to_prev, to_next = [], []
    for out, part, edge in ((to_prev, (low, one, two), 0), (to_next, (high, two, one), 3)):
        side_x = side_cot(row, zn_ref[0, edge], zp_ref[0, edge])
        side_z = side_cot(row, zn_ref[2, edge], zp_ref[2, edge])
        out.append(part[0][:TILE])
        out.append(part[1][:TILE])
        out.append(cot_y[edge][:TILE])
        out.append(mixed(row, part[0][TILE:], [(3, part[2][TILE:])]))
        out.append(mixed(row, part[1][TILE:], [(2, side_x), (3, side_z)]))
        out.append(cot_y[edge][TILE:])
    paired(place_ref, to_prev, to_next, first_ref, second_ref)


def pack_late(place_ref, refs, row, b, first_ref, second_ref):
    cot_ref, vel_ref, zn_ref, zp_ref = refs
    to_prev, to_next = [], []
    for out, d1, d2, d3, d4 in ((to_prev, 0, 1, 2, 3), (to_next, 3, 2, 1, 0)):
        out += [b[d3][:TILE], b[d4][:TILE], cot_ref[0, d1], cot_ref[2, d1]]
        out += [cot_ref[c, d2] for c in range(3)]
        out += [vel_ref[c, d1] for c in range(3)]
        out += [vel_ref[c, d2] for c in range(3)]
        vel = [side_vel(row, zn_ref[c, d1], zp_ref[c, d1]) for c in range(3)]
        out.append(mixed(row, vel[0], [(1, vel[1]), (2, vel[2])]))
    paired(place_ref, to_prev, to_next, first_ref, second_ref)


def cot_frame(refs, row, c, y):
    cot_ref, _, zn_ref, zp_ref = refs
    return joined(cot_ref[c, y], side_cot(row, zn_ref[c, y], zp_ref[c, y]))


def vel_frame(refs, row, c, y):
    _, vel_ref, zn_ref, zp_ref = refs
    return joined(vel_ref[c, y], side_vel(row, zn_ref[c, y], zp_ref[c, y]))


def along_z_cot(refs, row, frame, y):
    if not 0 <= y < ROWS:
        return dz(frame)
    zn_ref, zp_ref = refs[2], refs[3]
    ends = jnp.where(row < SIDE, zp_ref[2, y], zn_ref[2, y])
    wide = lax.broadcasted_iota(jnp.int32, (WIDE, 256), 0)
    both = joined(ends, ends)
    after = jnp.where(wide == TILE + 3, rolled(both, -1, 0), rolled(frame, -1, 0))
    before = jnp.where(wide == TILE + 4, rolled(both, 1, 0), rolled(frame, 1, 0))
    return 0.5 * (after - before)


def laplace(here, below, above):
    beside = rolled(here, 1, 1) + rolled(here, -1, 1)
    beside = beside + above + below
    beside = beside + rolled(here, 1, 0) + rolled(here, -1, 0)
    return 6.0 * here - beside


def ratio(top, bottom):
    safe = bottom > 0.0
    return jnp.where(safe, top / jnp.where(safe, bottom, 1.0), 0.0)


def total(x):
    return jnp.sum(jnp.sum(x, axis=0, keepdims=True), axis=1, keepdims=True)


def moments(
    place_ref,
    cot_ref,
    vel_ref,
    zn_ref,
    zp_ref,
    first_ref,
    second_ref,
    out_ref,
    b_ref,
    w_ref,
):
    refs = (cot_ref, vel_ref, zn_ref, zp_ref)
    row = sublane()
    after, before = unpaired(place_ref, first_ref, second_ref)
    flat, cot_y = own_parts(refs, row)
    cot_y[-1], cot_y[4] = joined(before[2], before[5]), joined(after[2], after[5])
    b = {y: flat[y] - 0.5 * (cot_y[y + 1] - cot_y[y - 1]) for y in range(ROWS)}
    b[-1] = joined(before[0], before[3]) - 0.5 * cot_y[0]
    b[4] = joined(after[0], after[3]) + 0.5 * cot_y[3]
    b[-2] = joined(before[1], before[4])
    b[5] = joined(after[1], after[4])
    w = {y: laplace(b[y], b[y - 1], b[y + 1]) for y in range(-1, 5)}
    m0 = m1 = None
    for y in range(ROWS):
        bc, wc = b[y][:TILE], w[y][:TILE]
        m0 = bc * bc if m0 is None else m0 + bc * bc
        m1 = bc * wc if m1 is None else m1 + bc * wc
    m0, m1 = total(m0), total(m1)
    sigma = ratio(m1, m0)
    spread = third = cross = None
    for y in range(ROWS):
        bc, wc = b[y][:TILE], w[y][:TILE]
        x = laplace(w[y], w[y - 1], w[y + 1])[:TILE]
        v = wc - sigma * bc
        u = x - sigma * wc
        spread = v * v if spread is None else spread + v * v
        third = v * u if third is None else third + v * u
        cross = bc * u if cross is None else cross + bc * u
    spread, third, cross = total(spread), total(third), total(cross)
    spread_out((m0, m1, spread, third, cross), out_ref)
    for y in range(-2, 6):
        b_ref[y + 2] = b[y]
    for y in range(-1, 5):
        w_ref[y + 1] = w[y]


def spread_out(parts, out_ref):
    lane = lax.broadcasted_iota(jnp.int32, (1, 128), 1)
    line = jnp.zeros((1, 128), jnp.float32)
    for k, value in enumerate(parts):
        line = jnp.where(lane == k, value, line)
    for j in range(out_ref.shape[0]):
        out_ref[j] = line


def gathered(got_ref):
    lines = got_ref[...].reshape(got_ref.shape[0], 128)
    return [x[:, :1] for x in merged(*[rolled(lines, -k, 1) for k in range(5)])]


def merged(m0, m1, spread, third, cross):
    own = ratio(m1, m0)

    def over(x):
        return jnp.sum(x, axis=0, keepdims=True)

    all0, all1 = over(m0), over(m1)
    delta = ratio(all1, all0) - own
    all_spread = over(spread + delta * delta * m0)
    all_third = over(third - delta * (spread + cross) + delta * delta * m1)
    all_cross = over(cross - delta * m1)
    return all0, all1, all_spread, all_third, all_cross


def merge(place_ref, got_ref, cot_ref, vel_ref, zn_ref, zp_ref, b_ref, out_ref, late1_ref, late2_ref):
    spread_out(gathered(got_ref), out_ref)
    b = {y: b_ref[y + 2] for y in range(ROWS)}
    pack_late(place_ref, (cot_ref, vel_ref, zn_ref, zp_ref), sublane(), b, late1_ref, late2_ref)


def slope(vel, y, grad_ref, inverse_ref, at):
    grad = [[dx(vel[i, y]), 0.5 * (vel[i, y + 1] - vel[i, y - 1]), dz(vel[i, y])] for i in range(3)]
    inside = None
    for i in range(3):
        for j in range(3):
            grad_ref[at, 3 * i + j] = grad[i][j]
        for j in range(i + 1):
            strain = grad[i][i] if i == j else 0.5 * (grad[i][j] + grad[j][i])
            square = (1.0 if i == j else 2.0) * (strain * strain)
            inside = square if inside is None else inside + square
    inverse_ref[at] = lax.rsqrt(2.0 * inside + strain_floor)


INNER = (1, 2)
OUTER = (-1, 0, 3, 4)


def inner_slopes(cot_ref, vel_ref, zn_ref, zp_ref, lines_ref, grad_ref, inverse_ref):
    refs = (cot_ref, vel_ref, zn_ref, zp_ref)
    row = sublane()
    vel = {(c, y): vel_frame(refs, row, c, y) for c in range(3) for y in range(ROWS)}
    for at, y in enumerate(INNER):
        slope(vel, y, grad_ref, inverse_ref, at)


def outer_slopes(place_ref, cot_ref, vel_ref, zn_ref, zp_ref, late1_ref, late2_ref, grad_ref, inverse_ref):
    refs = (cot_ref, vel_ref, zn_ref, zp_ref)
    row = sublane()
    vel = {(c, y): vel_frame(refs, row, c, y) for c in range(3) for y in range(ROWS)}
    late = unpaired(place_ref, late1_ref, late2_ref)
    for got, edge, step in ((late[0], ROWS - 1, 1), (late[1], 0, -1)):
        for c in range(3):
            vel[c, edge + step] = joined(got[7 + c], take(row, got[13], c))
            vel[c, edge + 2 * step] = joined(got[10 + c], got[10 + c])
    for at, y in enumerate(OUTER):
        slope(vel, y, grad_ref, inverse_ref, at)


def finish(
    place_ref,
    cot_ref,
    vel_ref,
    zn_ref,
    zp_ref,
    first_ref,
    second_ref,
    late1_ref,
    late2_ref,
    b_ref,
    w_ref,
    inner_grad_ref,
    inner_inverse_ref,
    outer_grad_ref,
    outer_inverse_ref,
    sums_ref,
    out_ref,
):
    refs = (cot_ref, vel_ref, zn_ref, zp_ref)
    row = sublane()
    m0, m1, spread, third, _ = gathered(sums_ref)
    step0 = m0 / m1
    norm1 = step0 * step0 * spread
    beta = norm1 / m0
    bend = step0 * step0 * third - 2.0 * step0 * beta * spread + beta * beta * m1
    step1 = norm1 / bend
    coef_b = step0 + step1 * (1.0 + beta)
    coef_w = -(step1 * step0)

    b = {y: b_ref[y + 2] for y in range(-2, 6)}
    w = {y: w_ref[y + 1] for y in range(-1, 5)}
    cot = {(c, y): cot_frame(refs, row, c, y) for c in range(3) for y in range(ROWS)}
    vel = {(c, y): vel_frame(refs, row, c, y) for c in range(3) for y in range(ROWS)}
    soon = unpaired(place_ref, first_ref, second_ref)
    late = unpaired(place_ref, late1_ref, late2_ref)
    for side, edge, step in ((0, ROWS - 1, 1), (1, 0, -1)):
        near, got = soon[side], late[side]
        y1, y2, y3, y4 = [edge + step * d for d in range(1, 5)]
        b[y3] = joined(got[0], take(row, near[3], 3))
        b[y4] = joined(got[1], got[1])
        cot[0, y1] = joined(got[2], take(row, near[4], 2))
        cot[1, y1] = joined(near[2], near[5])
        cot[2, y1] = joined(got[3], take(row, near[4], 3))
        for c in range(3):
            cot[c, y2] = joined(got[4 + c], got[4 + c])
            vel[c, y1] = joined(got[7 + c], take(row, got[13], c))
            vel[c, y2] = joined(got[10 + c], got[10 + c])
    for y in (-3, -2, 5, 6):
        w[y] = laplace(b[y], b[y - 1], b[y + 1])
    p = {y: coef_b * b[y] + coef_w * w[y] for y in range(-3, 7)}
    lam = {}
    for y in range(-2, 6):
        lam[0, y] = cot[0, y] - dx(p[y])
        lam[1, y] = cot[1, y] - 0.5 * (p[y + 1] - p[y - 1])
        lam[2, y] = cot[2, y] - dz(p[y])

    flat, upright = {}, {}
    for y in range(-1, 5):
        grad_ref, inverse_ref, rows = (
            (inner_grad_ref, inner_inverse_ref, INNER)
            if y in INNER
            else (outer_grad_ref, outer_inverse_ref, OUTER)
        )
        at = rows.index(y)
        grad = [[grad_ref[at, 3 * i + j] for j in range(3)] for i in range(3)]
        pull = [[dx(lam[i, y]), 0.5 * (lam[i, y + 1] - lam[i, y - 1]), dz(lam[i, y])] for i in range(3)]
        strain, ebb = {}, {}
        for i in range(3):
            for j in range(i + 1):
                strain[i, j] = grad[i][i] if i == j else 0.5 * (grad[i][j] + grad[j][i])
                ebb[i, j] = pull[i][i] if i == j else 0.5 * (pull[i][j] + pull[j][i])
        work = strain[0, 0] * ebb[0, 0] + strain[1, 1] * ebb[1, 1] + strain[2, 2] * ebb[2, 2]
        off_work = strain[1, 0] * ebb[1, 0] + strain[2, 0] * ebb[2, 0] + strain[2, 1] * ebb[2, 1]
        inverse = inverse_ref[at]
        twice = (2.0 * smag_coef) / inverse
        factor = (4.0 * smag_coef) * inverse * (work + 2.0 * off_work)
        stress = {key: twice * ebb[key] + factor * strain[key] for key in strain}

        def both(i, j):
            return stress[max(i, j), min(i, j)] + lam[i, y] * vel[j, y]

        for i in range(3):
            upright[i, y] = both(i, 1)[:TILE]
        if 0 <= y < ROWS:
            for i in range(3):
                carried = lam[0, y] * grad[0][i] + lam[1, y] * grad[1][i] + lam[2, y] * grad[2][i]
                level = dx(both(i, 0)) + dz(both(i, 2))
                flat[i, y] = (lam[i, y] + time_step * (level - carried))[:TILE]
    for i in range(3):
        for y in range(ROWS):
            out_ref[i, y] = flat[i, y] + (0.5 * time_step) * (upright[i, y + 1] - upright[i, y - 1])


def call(kernel, outs, scalars, arrays, cost=None):
    vmem = pl.BlockSpec(memory_space=pltpu.VMEM)
    smem = pl.BlockSpec(memory_space=pltpu.SMEM)
    return pl.pallas_call(
        kernel,
        out_shape=[jax.ShapeDtypeStruct(s, jnp.float32) for s in outs],
        in_specs=[smem] * len(scalars) + [vmem] * len(arrays),
        out_specs=[vmem] * len(outs),
        cost_estimate=cost and pl.CostEstimate(flops=cost, bytes_accessed=2_000_000, transcendentals=100_000),
        compiler_params=pltpu.CompilerParams(vmem_limit_bytes=32 * 1024 * 1024),
    )(*scalars, *arrays)


PY = ("y_low", "z")
PZ = ("y_high", "x", "core")
STEPS = (("z", "core"), ("y_high", "y_low", "x"))


def to_all(rows, axes):
    sizes = [lax.axis_size(axis) for axis in axes]
    order = [0]
    for n in sizes:
        middle = n // 2 if n > 2 else 0
        order = [i * n + (k + middle) % n for i in order for k in range(n)]
    return lax.all_to_all(rows, axes, 0, 0, axis_index_groups=[order])


def size(axes):
    return math.prod(lax.axis_size(axis) for axis in axes)


def swap_across(x, axes):
    n = size(axes)
    return lax.ppermute(x, axes, [(i, (i + 1 if i % 2 else i - 1) % n) for i in range(n)])


def swap_within(x, axes):
    return lax.ppermute(x, axes, [(i, i ^ 1) for i in range(size(axes))])


def body(velocity, cotangent):
    place = lax.axis_index(PY).astype(jnp.int32).reshape(1)
    odd = lax.axis_index("core").astype(jnp.int32).reshape(1)
    block = (3, ROWS, TILE, 256)
    cross, core, cotangent, velocity = call(
        pack_z, [block] * 4, [odd], [jnp.concatenate([cotangent, velocity], axis=0)]
    )
    cross = swap_across(cross, PZ)
    core = swap_within(core, PZ)
    soon, later = (SOON, TILE, 256), (LATE, TILE, 256)
    first, second, zn, zp = call(
        pack_y, [soon, soon, block, block], [odd, place], [cotangent, velocity, cross, core]
    )
    held = [cotangent, velocity, zn, zp, swap_across(first, PY), swap_within(second, PY)]
    lines, b, w = call(
        moments,
        [(size(STEPS[0]), 1, 128), (8, WIDE, 256), (6, WIDE, 256)],
        [place],
        held,
    )
    got = to_all(lines, STEPS[0])
    lines, late1, late2 = call(
        merge, [(size(STEPS[1]), 1, 128), later, later], [place], [got] + held[:4] + [b]
    )
    sums = to_all(lines, STEPS[1])
    late = [swap_across(late1, PY), swap_within(late2, PY)]
    inner = call(inner_slopes, [(2, 9, WIDE, 256), (2, WIDE, 256)], [], held[:4] + [lines], 4_000_000_000)
    outer = call(outer_slopes, [(4, 9, WIDE, 256), (4, WIDE, 256)], [place], held[:4] + late, 4_000_000)
    (out,) = call(finish, [block], [place], held + late + [b, w, *inner, *outer, sums])
    return out


def solution(mesh):
    ny, nz = mesh.shape["py"], mesh.shape["pz"]
    x = min(8, nz // 2)
    shape = (2, ny // 2, nz // (2 * x), x, 2)
    names = ("y_low", "z", "y_high", "x", "core")
    fine = jax.sharding.Mesh(mesh.devices.reshape(shape), names)
    placed = P(None, PY, PZ, None)
    return jax.shard_map(body, mesh=fine, in_specs=(placed, placed), out_specs=placed, check_vma=False)
```

```python
import math

import jax
import jax.numpy as jnp
from jax import lax
from jax.experimental import pallas as pl
from jax.experimental.pallas import tpu as pltpu
from jax.sharding import PartitionSpec as P

smag_coef = 0.1156
time_step = 0.2
strain_floor = 0.25

ROWS = 4
TILE = 8
SIDE = 4
WIDE = TILE + 2 * SIDE
SOON = 6
LATE = 14


def rolled(x, shift, axis):
    return pltpu.roll(x, shift % x.shape[axis], axis)


def dx(f):
    n = f.ndim - 1
    return 0.5 * (rolled(f, -1, n) - rolled(f, 1, n))


def dz(f):
    n = f.ndim - 2
    return 0.5 * (rolled(f, -1, n) - rolled(f, 1, n))


def sublane():
    return lax.broadcasted_iota(jnp.int32, (TILE, 256), 0)


def pack_z(odd_ref, both_ref, cross_ref, core_ref, cot_ref, vel_ref):
    row = sublane()
    even = odd_ref[0] == 0
    for c in range(3):
        for y in range(ROWS):
            cot, vel = both_ref[c, y], both_ref[3 + c, y]
            cot_ref[c, y], vel_ref[c, y] = cot, vel
            to_prev = jnp.where(row < 5, cot, rolled(vel, 5, 0))
            to_next = jnp.where(row >= 3, cot, rolled(vel, 3, 0))
            cross_ref[c, y] = jnp.where(even, to_prev, to_next)
            core_ref[c, y] = jnp.where(even, to_next, to_prev)


def side_cot(row, zn, zp):
    return jnp.where(row < SIDE, zn, zp)


def side_vel(row, zn, zp):
    return jnp.where(row < SIDE, rolled(zn, 3, 0), rolled(zp, 5, 0))


def put(row, tile, k):
    return jnp.where(row < SIDE, rolled(tile, k, 0), rolled(tile, -k, 0))


def take(row, tile, k):
    return jnp.where(row < SIDE, rolled(tile, -k, 0), rolled(tile, k, 0))


def mixed(row, base, inner):
    for k, tile in inner:
        base = jnp.where((row == k) | (row == TILE - 1 - k), put(row, tile, k), base)
    return base


def joined(a, b):
    return jnp.concatenate([a, b], axis=0)


def own_parts(refs, row):
    flat, cot_y = {}, {}
    for y in range(ROWS):
        flat[y] = -(dx(cot_frame(refs, row, 0, y)) + along_z_cot(refs, row, cot_frame(refs, row, 2, y), y))
        cot_y[y] = cot_frame(refs, row, 1, y)
    return flat, cot_y


def paired(place_ref, to_prev, to_next, first_ref, second_ref):
    even = lax.rem(place_ref[0], 2) == 0
    for k in range(first_ref.shape[0]):
        first_ref[k] = jnp.where(even, to_prev[k], to_next[k])
        second_ref[k] = jnp.where(even, to_next[k], to_prev[k])


def unpaired(place_ref, first_ref, second_ref):
    even = lax.rem(place_ref[0], 2) == 0
    tiles = range(first_ref.shape[0])
    after = [jnp.where(even, second_ref[k], first_ref[k]) for k in tiles]
    before = [jnp.where(even, first_ref[k], second_ref[k]) for k in tiles]
    return after, before


def pack_y(odd_ref, place_ref, cot_ref, vel_ref, cross_ref, core_ref, first_ref, second_ref, zn_ref, zp_ref):
    even = odd_ref[0] == 0
    for c in range(3):
        for y in range(ROWS):
            cross, core = cross_ref[c, y], core_ref[c, y]
            zn_ref[c, y] = jnp.where(even, core, cross)
            zp_ref[c, y] = jnp.where(even, cross, core)
    refs = (cot_ref, vel_ref, zn_ref, zp_ref)
    row = sublane()
    flat, cot_y = own_parts(refs, row)
    low = flat[0] - 0.5 * cot_y[1]
    high = flat[3] + 0.5 * cot_y[2]
    one = flat[1] - 0.5 * (cot_y[2] - cot_y[0])
    two = flat[2] - 0.5 * (cot_y[3] - cot_y[1])
    to_prev, to_next = [], []
    for out, part, edge in ((to_prev, (low, one, two), 0), (to_next, (high, two, one), 3)):
        side_x = side_cot(row, zn_ref[0, edge], zp_ref[0, edge])
        side_z = side_cot(row, zn_ref[2, edge], zp_ref[2, edge])
        out.append(part[0][:TILE])
        out.append(part[1][:TILE])
        out.append(cot_y[edge][:TILE])
        out.append(mixed(row, part[0][TILE:], [(3, part[2][TILE:])]))
        out.append(mixed(row, part[1][TILE:], [(2, side_x), (3, side_z)]))
        out.append(cot_y[edge][TILE:])
    paired(place_ref, to_prev, to_next, first_ref, second_ref)


def pack_late(place_ref, refs, row, b, first_ref, second_ref):
    cot_ref, vel_ref, zn_ref, zp_ref = refs
    to_prev, to_next = [], []
    for out, d1, d2, d3, d4 in ((to_prev, 0, 1, 2, 3), (to_next, 3, 2, 1, 0)):
        out += [b[d3][:TILE], b[d4][:TILE], cot_ref[0, d1], cot_ref[2, d1]]
        out += [cot_ref[c, d2] for c in range(3)]
        out += [vel_ref[c, d1] for c in range(3)]
        out += [vel_ref[c, d2] for c in range(3)]
        vel = [side_vel(row, zn_ref[c, d1], zp_ref[c, d1]) for c in range(3)]
        out.append(mixed(row, vel[0], [(1, vel[1]), (2, vel[2])]))
    paired(place_ref, to_prev, to_next, first_ref, second_ref)


def cot_frame(refs, row, c, y):
    cot_ref, _, zn_ref, zp_ref = refs
    return joined(cot_ref[c, y], side_cot(row, zn_ref[c, y], zp_ref[c, y]))


def vel_frame(refs, row, c, y):
    _, vel_ref, zn_ref, zp_ref = refs
    return joined(vel_ref[c, y], side_vel(row, zn_ref[c, y], zp_ref[c, y]))


def along_z_cot(refs, row, frame, y):
    if not 0 <= y < ROWS:
        return dz(frame)
    zn_ref, zp_ref = refs[2], refs[3]
    ends = jnp.where(row < SIDE, zp_ref[2, y], zn_ref[2, y])
    wide = lax.broadcasted_iota(jnp.int32, (WIDE, 256), 0)
    both = joined(ends, ends)
    after = jnp.where(wide == TILE + 3, rolled(both, -1, 0), rolled(frame, -1, 0))
    before = jnp.where(wide == TILE + 4, rolled(both, 1, 0), rolled(frame, 1, 0))
    return 0.5 * (after - before)


def laplace(here, below, above):
    beside = rolled(here, 1, 1) + rolled(here, -1, 1)
    beside = beside + above + below
    beside = beside + rolled(here, 1, 0) + rolled(here, -1, 0)
    return 6.0 * here - beside


def ratio(top, bottom):
    safe = bottom > 0.0
    return jnp.where(safe, top / jnp.where(safe, bottom, 1.0), 0.0)


def total(x):
    return jnp.sum(jnp.sum(x, axis=0, keepdims=True), axis=1, keepdims=True)


def moments(
    place_ref,
    cot_ref,
    vel_ref,
    zn_ref,
    zp_ref,
    first_ref,
    second_ref,
    out_ref,
    b_ref,
    w_ref,
    late1_ref,
    late2_ref,
):
    refs = (cot_ref, vel_ref, zn_ref, zp_ref)
    row = sublane()
    after, before = unpaired(place_ref, first_ref, second_ref)
    flat, cot_y = own_parts(refs, row)
    cot_y[-1], cot_y[4] = joined(before[2], before[5]), joined(after[2], after[5])
    b = {y: flat[y] - 0.5 * (cot_y[y + 1] - cot_y[y - 1]) for y in range(ROWS)}
    b[-1] = joined(before[0], before[3]) - 0.5 * cot_y[0]
    b[4] = joined(after[0], after[3]) + 0.5 * cot_y[3]
    b[-2] = joined(before[1], before[4])
    b[5] = joined(after[1], after[4])
    w = {y: laplace(b[y], b[y - 1], b[y + 1]) for y in range(-1, 5)}
    m0 = m1 = None
    for y in range(ROWS):
        bc, wc = b[y][:TILE], w[y][:TILE]
        m0 = bc * bc if m0 is None else m0 + bc * bc
        m1 = bc * wc if m1 is None else m1 + bc * wc
    m0, m1 = total(m0), total(m1)
    sigma = ratio(m1, m0)
    spread = third = cross = None
    for y in range(ROWS):
        bc, wc = b[y][:TILE], w[y][:TILE]
        x = laplace(w[y], w[y - 1], w[y + 1])[:TILE]
        v = wc - sigma * bc
        u = x - sigma * wc
        spread = v * v if spread is None else spread + v * v
        third = v * u if third is None else third + v * u
        cross = bc * u if cross is None else cross + bc * u
    spread, third, cross = total(spread), total(third), total(cross)
    spread_out((m0, m1, spread, third, cross), out_ref)
    for y in range(-2, 6):
        b_ref[y + 2] = b[y]
    for y in range(-1, 5):
        w_ref[y + 1] = w[y]
    pack_late(place_ref, refs, row, b, late1_ref, late2_ref)


def spread_out(parts, out_ref):
    lane = lax.broadcasted_iota(jnp.int32, (1, 128), 1)
    line = jnp.zeros((1, 128), jnp.float32)
    for k, value in enumerate(parts):
        line = jnp.where(lane == k, value, line)
    for j in range(out_ref.shape[0]):
        out_ref[j] = line


def gathered(got_ref):
    lines = got_ref[...].reshape(got_ref.shape[0], 128)
    return [x[:, :1] for x in merged(*[rolled(lines, -k, 1) for k in range(5)])]


def merged(m0, m1, spread, third, cross):
    own = ratio(m1, m0)

    def over(x):
        return jnp.sum(x, axis=0, keepdims=True)

    all0, all1 = over(m0), over(m1)
    delta = ratio(all1, all0) - own
    all_spread = over(spread + delta * delta * m0)
    all_third = over(third - delta * (spread + cross) + delta * delta * m1)
    all_cross = over(cross - delta * m1)
    return all0, all1, all_spread, all_third, all_cross


def merge(got_ref, out_ref):
    spread_out(gathered(got_ref), out_ref)


def slope(vel, y, grad_ref, inverse_ref, at):
    grad = [[dx(vel[i, y]), 0.5 * (vel[i, y + 1] - vel[i, y - 1]), dz(vel[i, y])] for i in range(3)]
    inside = None
    for i in range(3):
        for j in range(3):
            grad_ref[at, 3 * i + j] = grad[i][j]
        for j in range(i + 1):
            strain = grad[i][i] if i == j else 0.5 * (grad[i][j] + grad[j][i])
            square = (1.0 if i == j else 2.0) * (strain * strain)
            inside = square if inside is None else inside + square
    inverse_ref[at] = lax.rsqrt(2.0 * inside + strain_floor)


INNER = (1, 2)
OUTER = (-1, 0, 3, 4)


def inner_slopes(cot_ref, vel_ref, zn_ref, zp_ref, lines_ref, grad_ref, inverse_ref):
    refs = (cot_ref, vel_ref, zn_ref, zp_ref)
    row = sublane()
    vel = {(c, y): vel_frame(refs, row, c, y) for c in range(3) for y in range(ROWS)}
    for at, y in enumerate(INNER):
        slope(vel, y, grad_ref, inverse_ref, at)


def outer_slopes(place_ref, cot_ref, vel_ref, zn_ref, zp_ref, late1_ref, late2_ref, grad_ref, inverse_ref):
    refs = (cot_ref, vel_ref, zn_ref, zp_ref)
    row = sublane()
    vel = {(c, y): vel_frame(refs, row, c, y) for c in range(3) for y in range(ROWS)}
    late = unpaired(place_ref, late1_ref, late2_ref)
    for got, edge, step in ((late[0], ROWS - 1, 1), (late[1], 0, -1)):
        for c in range(3):
            vel[c, edge + step] = joined(got[7 + c], take(row, got[13], c))
            vel[c, edge + 2 * step] = joined(got[10 + c], got[10 + c])
    for at, y in enumerate(OUTER):
        slope(vel, y, grad_ref, inverse_ref, at)


def finish(
    place_ref,
    cot_ref,
    vel_ref,
    zn_ref,
    zp_ref,
    first_ref,
    second_ref,
    late1_ref,
    late2_ref,
    b_ref,
    w_ref,
    inner_grad_ref,
    inner_inverse_ref,
    outer_grad_ref,
    outer_inverse_ref,
    sums_ref,
    out_ref,
):
    refs = (cot_ref, vel_ref, zn_ref, zp_ref)
    row = sublane()
    m0, m1, spread, third, _ = gathered(sums_ref)
    step0 = m0 / m1
    norm1 = step0 * step0 * spread
    beta = norm1 / m0
    bend = step0 * step0 * third - 2.0 * step0 * beta * spread + beta * beta * m1
    step1 = norm1 / bend
    coef_b = step0 + step1 * (1.0 + beta)
    coef_w = -(step1 * step0)

    b = {y: b_ref[y + 2] for y in range(-2, 6)}
    w = {y: w_ref[y + 1] for y in range(-1, 5)}
    cot = {(c, y): cot_frame(refs, row, c, y) for c in range(3) for y in range(ROWS)}
    vel = {(c, y): vel_frame(refs, row, c, y) for c in range(3) for y in range(ROWS)}
    soon = unpaired(place_ref, first_ref, second_ref)
    late = unpaired(place_ref, late1_ref, late2_ref)
    for side, edge, step in ((0, ROWS - 1, 1), (1, 0, -1)):
        near, got = soon[side], late[side]
        y1, y2, y3, y4 = [edge + step * d for d in range(1, 5)]
        b[y3] = joined(got[0], take(row, near[3], 3))
        b[y4] = joined(got[1], got[1])
        cot[0, y1] = joined(got[2], take(row, near[4], 2))
        cot[1, y1] = joined(near[2], near[5])
        cot[2, y1] = joined(got[3], take(row, near[4], 3))
        for c in range(3):
            cot[c, y2] = joined(got[4 + c], got[4 + c])
            vel[c, y1] = joined(got[7 + c], take(row, got[13], c))
            vel[c, y2] = joined(got[10 + c], got[10 + c])
    for y in (-3, -2, 5, 6):
        w[y] = laplace(b[y], b[y - 1], b[y + 1])
    p = {y: coef_b * b[y] + coef_w * w[y] for y in range(-3, 7)}
    lam = {}
    for y in range(-2, 6):
        lam[0, y] = cot[0, y] - dx(p[y])
        lam[1, y] = cot[1, y] - 0.5 * (p[y + 1] - p[y - 1])
        lam[2, y] = cot[2, y] - dz(p[y])

    flat, upright = {}, {}
    for y in range(-1, 5):
        grad_ref, inverse_ref, rows = (
            (inner_grad_ref, inner_inverse_ref, INNER)
            if y in INNER
            else (outer_grad_ref, outer_inverse_ref, OUTER)
        )
        at = rows.index(y)
        grad = [[grad_ref[at, 3 * i + j] for j in range(3)] for i in range(3)]
        pull = [[dx(lam[i, y]), 0.5 * (lam[i, y + 1] - lam[i, y - 1]), dz(lam[i, y])] for i in range(3)]
        strain, ebb = {}, {}
        for i in range(3):
            for j in range(i + 1):
                strain[i, j] = grad[i][i] if i == j else 0.5 * (grad[i][j] + grad[j][i])
                ebb[i, j] = pull[i][i] if i == j else 0.5 * (pull[i][j] + pull[j][i])
        work = strain[0, 0] * ebb[0, 0] + strain[1, 1] * ebb[1, 1] + strain[2, 2] * ebb[2, 2]
        off_work = strain[1, 0] * ebb[1, 0] + strain[2, 0] * ebb[2, 0] + strain[2, 1] * ebb[2, 1]
        inverse = inverse_ref[at]
        twice = (2.0 * smag_coef) / inverse
        factor = (4.0 * smag_coef) * inverse * (work + 2.0 * off_work)
        stress = {key: twice * ebb[key] + factor * strain[key] for key in strain}

        def both(i, j):
            return stress[max(i, j), min(i, j)] + lam[i, y] * vel[j, y]

        for i in range(3):
            upright[i, y] = both(i, 1)[:TILE]
        if 0 <= y < ROWS:
            for i in range(3):
                carried = lam[0, y] * grad[0][i] + lam[1, y] * grad[1][i] + lam[2, y] * grad[2][i]
                level = dx(both(i, 0)) + dz(both(i, 2))
                flat[i, y] = (lam[i, y] + time_step * (level - carried))[:TILE]
    for i in range(3):
        for y in range(ROWS):
            out_ref[i, y] = flat[i, y] + (0.5 * time_step) * (upright[i, y + 1] - upright[i, y - 1])


def call(kernel, outs, scalars, arrays, cost=None):
    vmem = pl.BlockSpec(memory_space=pltpu.VMEM)
    smem = pl.BlockSpec(memory_space=pltpu.SMEM)
    return pl.pallas_call(
        kernel,
        out_shape=[jax.ShapeDtypeStruct(s, jnp.float32) for s in outs],
        in_specs=[smem] * len(scalars) + [vmem] * len(arrays),
        out_specs=[vmem] * len(outs),
        cost_estimate=cost and pl.CostEstimate(flops=cost, bytes_accessed=2_000_000, transcendentals=100_000),
        compiler_params=pltpu.CompilerParams(vmem_limit_bytes=32 * 1024 * 1024),
    )(*scalars, *arrays)


PY = ("y_low", "z")
PZ = ("y_high", "x", "core")
STEPS = (("z", "core"), ("y_high", "y_low", "x"))


def to_all(rows, axes):
    sizes = [lax.axis_size(axis) for axis in axes]
    order = [0]
    for n in sizes:
        middle = n // 2 if n > 2 else 0
        order = [i * n + (k + middle) % n for i in order for k in range(n)]
    return lax.all_to_all(rows, axes, 0, 0, axis_index_groups=[order])


def size(axes):
    return math.prod(lax.axis_size(axis) for axis in axes)


def swap_across(x, axes):
    n = size(axes)
    return lax.ppermute(x, axes, [(i, (i + 1 if i % 2 else i - 1) % n) for i in range(n)])


def swap_within(x, axes):
    return lax.ppermute(x, axes, [(i, i ^ 1) for i in range(size(axes))])


def body(velocity, cotangent):
    place = lax.axis_index(PY).astype(jnp.int32).reshape(1)
    odd = lax.axis_index("core").astype(jnp.int32).reshape(1)
    block = (3, ROWS, TILE, 256)
    cross, core, cotangent, velocity = call(
        pack_z, [block] * 4, [odd], [jnp.concatenate([cotangent, velocity], axis=0)]
    )
    cross = swap_across(cross, PZ)
    core = swap_within(core, PZ)
    soon, later = (SOON, TILE, 256), (LATE, TILE, 256)
    first, second, zn, zp = call(
        pack_y, [soon, soon, block, block], [odd, place], [cotangent, velocity, cross, core]
    )
    held = [cotangent, velocity, zn, zp, swap_across(first, PY), swap_within(second, PY)]
    lines, b, w, late1, late2 = call(
        moments,
        [(size(STEPS[0]), 1, 128), (8, WIDE, 256), (6, WIDE, 256), later, later],
        [place],
        held,
    )
    got = to_all(lines, STEPS[0])
    late = [swap_across(late1, PY), swap_within(late2, PY)]
    inner = call(inner_slopes, [(2, 9, WIDE, 256), (2, WIDE, 256)], [], held[:4] + [lines], 4_000_000_000)
    outer = call(outer_slopes, [(4, 9, WIDE, 256), (4, WIDE, 256)], [place], held[:4] + late, 4_000_000)
    (lines,) = call(merge, [(size(STEPS[1]), 1, 128)], [], [got])
    sums = to_all(lines, STEPS[1])
    (out,) = call(finish, [block], [place], held + late + [b, w, *inner, *outer, sums])
    return out


def solution(mesh):
    ny, nz = mesh.shape["py"], mesh.shape["pz"]
    x = min(8, nz // 2)
    shape = (2, ny // 2, nz // (2 * x), x, 2)
    names = ("y_low", "z", "y_high", "x", "core")
    fine = jax.sharding.Mesh(mesh.devices.reshape(shape), names)
    placed = P(None, PY, PZ, None)
    return jax.shard_map(body, mesh=fine, in_specs=(placed, placed), out_specs=placed, check_vma=False)
```

```python
import math

import jax
import jax.numpy as jnp
from jax import lax
from jax.experimental import pallas as pl
from jax.experimental.pallas import tpu as pltpu
from jax.sharding import PartitionSpec as P

smag_coef = 0.1156
time_step = 0.2
strain_floor = 0.25

ROWS = 4
TILE = 8
SIDE = 4
WIDE = TILE + 2 * SIDE
SOON = 6
LATE = 14


def rolled(x, shift, axis):
    return pltpu.roll(x, shift % x.shape[axis], axis)


def dx(f):
    n = f.ndim - 1
    return 0.5 * (rolled(f, -1, n) - rolled(f, 1, n))


def dz(f):
    n = f.ndim - 2
    return 0.5 * (rolled(f, -1, n) - rolled(f, 1, n))


def sublane():
    return lax.broadcasted_iota(jnp.int32, (TILE, 256), 0)


def pack_z(odd_ref, both_ref, cross_ref, core_ref, cot_ref, vel_ref):
    row = sublane()
    even = odd_ref[0] == 0
    for c in range(3):
        for y in range(ROWS):
            cot, vel = both_ref[c, y], both_ref[3 + c, y]
            cot_ref[c, y], vel_ref[c, y] = cot, vel
            to_prev = jnp.where(row < 5, cot, rolled(vel, 5, 0))
            to_next = jnp.where(row >= 3, cot, rolled(vel, 3, 0))
            cross_ref[c, y] = jnp.where(even, to_prev, to_next)
            core_ref[c, y] = jnp.where(even, to_next, to_prev)


def side_cot(row, zn, zp):
    return jnp.where(row < SIDE, zn, zp)


def side_vel(row, zn, zp):
    return jnp.where(row < SIDE, rolled(zn, 3, 0), rolled(zp, 5, 0))


def put(row, tile, k):
    return jnp.where(row < SIDE, rolled(tile, k, 0), rolled(tile, -k, 0))


def take(row, tile, k):
    return jnp.where(row < SIDE, rolled(tile, -k, 0), rolled(tile, k, 0))


def mixed(row, base, inner):
    for k, tile in inner:
        base = jnp.where((row == k) | (row == TILE - 1 - k), put(row, tile, k), base)
    return base


def joined(a, b):
    return jnp.concatenate([a, b], axis=0)


def own_parts(refs, row):
    flat, cot_y = {}, {}
    for y in range(ROWS):
        flat[y] = -(dx(cot_frame(refs, row, 0, y)) + along_z_cot(refs, row, cot_frame(refs, row, 2, y), y))
        cot_y[y] = cot_frame(refs, row, 1, y)
    return flat, cot_y


def paired(place_ref, to_prev, to_next, first_ref, second_ref):
    even = lax.rem(place_ref[0], 2) == 0
    for k in range(first_ref.shape[0]):
        first_ref[k] = jnp.where(even, to_prev[k], to_next[k])
        second_ref[k] = jnp.where(even, to_next[k], to_prev[k])


def unpaired(place_ref, first_ref, second_ref):
    even = lax.rem(place_ref[0], 2) == 0
    tiles = range(first_ref.shape[0])
    after = [jnp.where(even, second_ref[k], first_ref[k]) for k in tiles]
    before = [jnp.where(even, first_ref[k], second_ref[k]) for k in tiles]
    return after, before


def pack_y(odd_ref, place_ref, cot_ref, vel_ref, cross_ref, core_ref, first_ref, second_ref, zn_ref, zp_ref):
    even = odd_ref[0] == 0
    for c in range(3):
        for y in range(ROWS):
            cross, core = cross_ref[c, y], core_ref[c, y]
            zn_ref[c, y] = jnp.where(even, core, cross)
            zp_ref[c, y] = jnp.where(even, cross, core)
    refs = (cot_ref, vel_ref, zn_ref, zp_ref)
    row = sublane()
    flat, cot_y = own_parts(refs, row)
    low = flat[0] - 0.5 * cot_y[1]
    high = flat[3] + 0.5 * cot_y[2]
    one = flat[1] - 0.5 * (cot_y[2] - cot_y[0])
    two = flat[2] - 0.5 * (cot_y[3] - cot_y[1])
    to_prev, to_next = [], []
    for out, part, edge in ((to_prev, (low, one, two), 0), (to_next, (high, two, one), 3)):
        side_x = side_cot(row, zn_ref[0, edge], zp_ref[0, edge])
        side_z = side_cot(row, zn_ref[2, edge], zp_ref[2, edge])
        out.append(part[0][:TILE])
        out.append(part[1][:TILE])
        out.append(cot_y[edge][:TILE])
        out.append(mixed(row, part[0][TILE:], [(3, part[2][TILE:])]))
        out.append(mixed(row, part[1][TILE:], [(2, side_x), (3, side_z)]))
        out.append(cot_y[edge][TILE:])
    paired(place_ref, to_prev, to_next, first_ref, second_ref)


def pack_late(place_ref, refs, row, b, first_ref, second_ref):
    cot_ref, vel_ref, zn_ref, zp_ref = refs
    to_prev, to_next = [], []
    for out, d1, d2, d3, d4 in ((to_prev, 0, 1, 2, 3), (to_next, 3, 2, 1, 0)):
        out += [b[d3][:TILE], b[d4][:TILE], cot_ref[0, d1], cot_ref[2, d1]]
        out += [cot_ref[c, d2] for c in range(3)]
        out += [vel_ref[c, d1] for c in range(3)]
        out += [vel_ref[c, d2] for c in range(3)]
        vel = [side_vel(row, zn_ref[c, d1], zp_ref[c, d1]) for c in range(3)]
        out.append(mixed(row, vel[0], [(1, vel[1]), (2, vel[2])]))
    paired(place_ref, to_prev, to_next, first_ref, second_ref)


def cot_frame(refs, row, c, y):
    cot_ref, _, zn_ref, zp_ref = refs
    return joined(cot_ref[c, y], side_cot(row, zn_ref[c, y], zp_ref[c, y]))


def vel_frame(refs, row, c, y):
    _, vel_ref, zn_ref, zp_ref = refs
    return joined(vel_ref[c, y], side_vel(row, zn_ref[c, y], zp_ref[c, y]))


def along_z_cot(refs, row, frame, y):
    if not 0 <= y < ROWS:
        return dz(frame)
    zn_ref, zp_ref = refs[2], refs[3]
    ends = jnp.where(row < SIDE, zp_ref[2, y], zn_ref[2, y])
    wide = lax.broadcasted_iota(jnp.int32, (WIDE, 256), 0)
    both = joined(ends, ends)
    after = jnp.where(wide == TILE + 3, rolled(both, -1, 0), rolled(frame, -1, 0))
    before = jnp.where(wide == TILE + 4, rolled(both, 1, 0), rolled(frame, 1, 0))
    return 0.5 * (after - before)


def laplace(here, below, above):
    beside = rolled(here, 1, 1) + rolled(here, -1, 1)
    beside = beside + above + below
    beside = beside + rolled(here, 1, 0) + rolled(here, -1, 0)
    return 6.0 * here - beside


def ratio(top, bottom):
    safe = bottom > 0.0
    return jnp.where(safe, top / jnp.where(safe, bottom, 1.0), 0.0)


def total(x):
    return jnp.sum(jnp.sum(x, axis=0, keepdims=True), axis=1, keepdims=True)


def moments(
    place_ref,
    cot_ref,
    vel_ref,
    zn_ref,
    zp_ref,
    first_ref,
    second_ref,
    out_ref,
    b_ref,
    w_ref,
    late1_ref,
    late2_ref,
):
    refs = (cot_ref, vel_ref, zn_ref, zp_ref)
    row = sublane()
    after, before = unpaired(place_ref, first_ref, second_ref)
    flat, cot_y = own_parts(refs, row)
    cot_y[-1], cot_y[4] = joined(before[2], before[5]), joined(after[2], after[5])
    b = {y: flat[y] - 0.5 * (cot_y[y + 1] - cot_y[y - 1]) for y in range(ROWS)}
    b[-1] = joined(before[0], before[3]) - 0.5 * cot_y[0]
    b[4] = joined(after[0], after[3]) + 0.5 * cot_y[3]
    b[-2] = joined(before[1], before[4])
    b[5] = joined(after[1], after[4])
    w = {y: laplace(b[y], b[y - 1], b[y + 1]) for y in range(-1, 5)}
    m0 = m1 = None
    for y in range(ROWS):
        bc, wc = b[y][:TILE], w[y][:TILE]
        m0 = bc * bc if m0 is None else m0 + bc * bc
        m1 = bc * wc if m1 is None else m1 + bc * wc
    m0, m1 = total(m0), total(m1)
    sigma = ratio(m1, m0)
    spread = third = cross = None
    for y in range(ROWS):
        bc, wc = b[y][:TILE], w[y][:TILE]
        x = laplace(w[y], w[y - 1], w[y + 1])[:TILE]
        v = wc - sigma * bc
        u = x - sigma * wc
        spread = v * v if spread is None else spread + v * v
        third = v * u if third is None else third + v * u
        cross = bc * u if cross is None else cross + bc * u
    spread, third, cross = total(spread), total(third), total(cross)
    spread_out((m0, m1, spread, third, cross), out_ref)
    for y in range(-2, 6):
        b_ref[y + 2] = b[y]
    for y in range(-1, 5):
        w_ref[y + 1] = w[y]
    pack_late(place_ref, refs, row, b, late1_ref, late2_ref)


def spread_out(parts, out_ref):
    lane = lax.broadcasted_iota(jnp.int32, (1, 128), 1)
    line = jnp.zeros((1, 128), jnp.float32)
    for k, value in enumerate(parts):
        line = jnp.where(lane == k, value, line)
    for j in range(out_ref.shape[0]):
        out_ref[j] = line


def gathered(got_ref):
    lines = got_ref[...].reshape(got_ref.shape[0], 128)
    return [x[:, :1] for x in merged(*[rolled(lines, -k, 1) for k in range(5)])]


def merged(m0, m1, spread, third, cross):
    own = ratio(m1, m0)

    def over(x):
        return jnp.sum(x, axis=0, keepdims=True)

    all0, all1 = over(m0), over(m1)
    delta = ratio(all1, all0) - own
    all_spread = over(spread + delta * delta * m0)
    all_third = over(third - delta * (spread + cross) + delta * delta * m1)
    all_cross = over(cross - delta * m1)
    return all0, all1, all_spread, all_third, all_cross


def merge(got_ref, out_ref):
    spread_out(gathered(got_ref), out_ref)


def slope(vel, y, grad_ref, inverse_ref, at):
    grad = [[dx(vel[i, y]), 0.5 * (vel[i, y + 1] - vel[i, y - 1]), dz(vel[i, y])] for i in range(3)]
    inside = None
    for i in range(3):
        for j in range(3):
            grad_ref[at, 3 * i + j] = grad[i][j]
        for j in range(i + 1):
            strain = grad[i][i] if i == j else 0.5 * (grad[i][j] + grad[j][i])
            square = (1.0 if i == j else 2.0) * (strain * strain)
            inside = square if inside is None else inside + square
    inverse_ref[at] = lax.rsqrt(2.0 * inside + strain_floor)


INNER = (1, 2)
OUTER = (-1, 0, 3, 4)


def inner_slopes(cot_ref, vel_ref, zn_ref, zp_ref, lines_ref, grad_ref, inverse_ref):
    refs = (cot_ref, vel_ref, zn_ref, zp_ref)
    row = sublane()
    vel = {(c, y): vel_frame(refs, row, c, y) for c in range(3) for y in range(ROWS)}
    for at, y in enumerate(INNER):
        slope(vel, y, grad_ref, inverse_ref, at)


def outer_slopes(place_ref, cot_ref, vel_ref, zn_ref, zp_ref, late1_ref, late2_ref, grad_ref, inverse_ref):
    refs = (cot_ref, vel_ref, zn_ref, zp_ref)
    row = sublane()
    vel = {(c, y): vel_frame(refs, row, c, y) for c in range(3) for y in range(ROWS)}
    late = unpaired(place_ref, late1_ref, late2_ref)
    for got, edge, step in ((late[0], ROWS - 1, 1), (late[1], 0, -1)):
        for c in range(3):
            vel[c, edge + step] = joined(got[7 + c], take(row, got[13], c))
            vel[c, edge + 2 * step] = joined(got[10 + c], got[10 + c])
    for at, y in enumerate(OUTER):
        slope(vel, y, grad_ref, inverse_ref, at)


def finish(
    place_ref,
    cot_ref,
    vel_ref,
    zn_ref,
    zp_ref,
    first_ref,
    second_ref,
    late1_ref,
    late2_ref,
    b_ref,
    w_ref,
    inner_grad_ref,
    inner_inverse_ref,
    outer_grad_ref,
    outer_inverse_ref,
    sums_ref,
    out_ref,
):
    refs = (cot_ref, vel_ref, zn_ref, zp_ref)
    row = sublane()
    m0, m1, spread, third, _ = gathered(sums_ref)
    step0 = m0 / m1
    norm1 = step0 * step0 * spread
    beta = norm1 / m0
    bend = step0 * step0 * third - 2.0 * step0 * beta * spread + beta * beta * m1
    step1 = norm1 / bend
    coef_b = step0 + step1 * (1.0 + beta)
    coef_w = -(step1 * step0)

    b = {y: b_ref[y + 2] for y in range(-2, 6)}
    w = {y: w_ref[y + 1] for y in range(-1, 5)}
    cot = {(c, y): cot_frame(refs, row, c, y) for c in range(3) for y in range(ROWS)}
    vel = {(c, y): vel_frame(refs, row, c, y) for c in range(3) for y in range(ROWS)}
    soon = unpaired(place_ref, first_ref, second_ref)
    late = unpaired(place_ref, late1_ref, late2_ref)
    for side, edge, step in ((0, ROWS - 1, 1), (1, 0, -1)):
        near, got = soon[side], late[side]
        y1, y2, y3, y4 = [edge + step * d for d in range(1, 5)]
        b[y3] = joined(got[0], take(row, near[3], 3))
        b[y4] = joined(got[1], got[1])
        cot[0, y1] = joined(got[2], take(row, near[4], 2))
        cot[1, y1] = joined(near[2], near[5])
        cot[2, y1] = joined(got[3], take(row, near[4], 3))
        for c in range(3):
            cot[c, y2] = joined(got[4 + c], got[4 + c])
            vel[c, y1] = joined(got[7 + c], take(row, got[13], c))
            vel[c, y2] = joined(got[10 + c], got[10 + c])
    for y in (-3, -2, 5, 6):
        w[y] = laplace(b[y], b[y - 1], b[y + 1])
    p = {y: coef_b * b[y] + coef_w * w[y] for y in range(-3, 7)}
    lam = {}
    for y in range(-2, 6):
        lam[0, y] = cot[0, y] - dx(p[y])
        lam[1, y] = cot[1, y] - 0.5 * (p[y + 1] - p[y - 1])
        lam[2, y] = cot[2, y] - dz(p[y])

    flat, upright = {}, {}
    for y in range(-1, 5):
        grad_ref, inverse_ref, rows = (
            (inner_grad_ref, inner_inverse_ref, INNER)
            if y in INNER
            else (outer_grad_ref, outer_inverse_ref, OUTER)
        )
        at = rows.index(y)
        grad = [[grad_ref[at, 3 * i + j] for j in range(3)] for i in range(3)]
        pull = [[dx(lam[i, y]), 0.5 * (lam[i, y + 1] - lam[i, y - 1]), dz(lam[i, y])] for i in range(3)]
        strain, ebb = {}, {}
        for i in range(3):
            for j in range(i + 1):
                strain[i, j] = grad[i][i] if i == j else 0.5 * (grad[i][j] + grad[j][i])
                ebb[i, j] = pull[i][i] if i == j else 0.5 * (pull[i][j] + pull[j][i])
        work = strain[0, 0] * ebb[0, 0] + strain[1, 1] * ebb[1, 1] + strain[2, 2] * ebb[2, 2]
        off_work = strain[1, 0] * ebb[1, 0] + strain[2, 0] * ebb[2, 0] + strain[2, 1] * ebb[2, 1]
        inverse = inverse_ref[at]
        twice = (2.0 * smag_coef) / inverse
        factor = (4.0 * smag_coef) * inverse * (work + 2.0 * off_work)
        stress = {key: twice * ebb[key] + factor * strain[key] for key in strain}

        def both(i, j):
            return stress[max(i, j), min(i, j)] + lam[i, y] * vel[j, y]

        for i in range(3):
            upright[i, y] = both(i, 1)[:TILE]
        if 0 <= y < ROWS:
            for i in range(3):
                carried = lam[0, y] * grad[0][i] + lam[1, y] * grad[1][i] + lam[2, y] * grad[2][i]
                level = dx(both(i, 0)) + dz(both(i, 2))
                flat[i, y] = (lam[i, y] + time_step * (level - carried))[:TILE]
    for i in range(3):
        for y in range(ROWS):
            out_ref[i, y] = flat[i, y] + (0.5 * time_step) * (upright[i, y + 1] - upright[i, y - 1])


def call(kernel, outs, scalars, arrays, cost=None):
    vmem = pl.BlockSpec(memory_space=pltpu.VMEM)
    smem = pl.BlockSpec(memory_space=pltpu.SMEM)
    return pl.pallas_call(
        kernel,
        out_shape=[jax.ShapeDtypeStruct(s, jnp.float32) for s in outs],
        in_specs=[smem] * len(scalars) + [vmem] * len(arrays),
        out_specs=[vmem] * len(outs),
        cost_estimate=cost and pl.CostEstimate(flops=cost, bytes_accessed=2_000_000, transcendentals=100_000),
        compiler_params=pltpu.CompilerParams(vmem_limit_bytes=32 * 1024 * 1024),
    )(*scalars, *arrays)


PY = ("y_low", "z")
PZ = ("y_high", "x", "core")
STEPS = (("z", "core"), ("y_high", "y_low", "x"))


def to_all(rows, axes):
    sizes = [lax.axis_size(axis) for axis in axes]
    order = [0]
    for n in sizes:
        middle = n // 2 if n > 2 else 0
        order = [i * n + (k + middle) % n for i in order for k in range(n)]
    return lax.all_to_all(rows, axes, 0, 0, axis_index_groups=[order])


def size(axes):
    return math.prod(lax.axis_size(axis) for axis in axes)


def swap_across(x, axes):
    n = size(axes)
    return lax.ppermute(x, axes, [(i, (i + 1 if i % 2 else i - 1) % n) for i in range(n)])


def swap_within(x, axes):
    return lax.ppermute(x, axes, [(i, i ^ 1) for i in range(size(axes))])


def body(velocity, cotangent):
    place = lax.axis_index(PY).astype(jnp.int32).reshape(1)
    odd = lax.axis_index("core").astype(jnp.int32).reshape(1)
    block = (3, ROWS, TILE, 256)
    cross, core, cotangent, velocity = call(
        pack_z, [block] * 4, [odd], [jnp.concatenate([cotangent, velocity], axis=0)]
    )
    cross = swap_across(cross, PZ)
    core = swap_within(core, PZ)
    soon, later = (SOON, TILE, 256), (LATE, TILE, 256)
    first, second, zn, zp = call(
        pack_y, [soon, soon, block, block], [odd, place], [cotangent, velocity, cross, core]
    )
    held = [cotangent, velocity, zn, zp, swap_across(first, PY), swap_within(second, PY)]
    lines, b, w, late1, late2 = call(
        moments,
        [(size(STEPS[0]), 1, 128), (8, WIDE, 256), (6, WIDE, 256), later, later],
        [place],
        held,
    )
    got = lax.all_to_all(lines, STEPS[0], 0, 0)
    late = [swap_across(late1, PY), swap_within(late2, PY)]
    inner = call(inner_slopes, [(2, 9, WIDE, 256), (2, WIDE, 256)], [], held[:4] + [lines], 4_000_000_000)
    outer = call(outer_slopes, [(4, 9, WIDE, 256), (4, WIDE, 256)], [place], held[:4] + late, 4_000_000)
    (lines,) = call(merge, [(size(STEPS[1]), 1, 128)], [], [got])
    sums = to_all(lines, STEPS[1])
    (out,) = call(finish, [block], [place], held + late + [b, w, *inner, *outer, sums])
    return out


def solution(mesh):
    ny, nz = mesh.shape["py"], mesh.shape["pz"]
    x = min(8, nz // 2)
    shape = (2, ny // 2, nz // (2 * x), x, 2)
    names = ("y_low", "z", "y_high", "x", "core")
    fine = jax.sharding.Mesh(mesh.devices.reshape(shape), names)
    placed = P(None, PY, PZ, None)
    return jax.shard_map(body, mesh=fine, in_specs=(placed, placed), out_specs=placed, check_vma=False)
```

```python
import math

import jax
import jax.numpy as jnp
from jax import lax
from jax.experimental import pallas as pl
from jax.experimental.pallas import tpu as pltpu
from jax.sharding import PartitionSpec as P

smag_coef = 0.1156
time_step = 0.2
strain_floor = 0.25

ROWS = 4
TILE = 8
SIDE = 4
WIDE = TILE + 2 * SIDE
SOON = 6
LATE = 14


def rolled(x, shift, axis):
    return pltpu.roll(x, shift % x.shape[axis], axis)


def dx(f):
    n = f.ndim - 1
    return 0.5 * (rolled(f, -1, n) - rolled(f, 1, n))


def dz(f):
    n = f.ndim - 2
    return 0.5 * (rolled(f, -1, n) - rolled(f, 1, n))


def sublane():
    return lax.broadcasted_iota(jnp.int32, (TILE, 256), 0)


def pack_z(odd_ref, both_ref, cross_ref, core_ref, cot_ref, vel_ref):
    row = sublane()
    even = odd_ref[0] == 0
    for c in range(3):
        for y in range(ROWS):
            cot, vel = both_ref[c, y], both_ref[3 + c, y]
            cot_ref[c, y], vel_ref[c, y] = cot, vel
            to_prev = jnp.where(row < 5, cot, rolled(vel, 5, 0))
            to_next = jnp.where(row >= 3, cot, rolled(vel, 3, 0))
            cross_ref[c, y] = jnp.where(even, to_prev, to_next)
            core_ref[c, y] = jnp.where(even, to_next, to_prev)


def side_cot(row, zn, zp):
    return jnp.where(row < SIDE, zn, zp)


def side_vel(row, zn, zp):
    return jnp.where(row < SIDE, rolled(zn, 3, 0), rolled(zp, 5, 0))


def put(row, tile, k):
    return jnp.where(row < SIDE, rolled(tile, k, 0), rolled(tile, -k, 0))


def take(row, tile, k):
    return jnp.where(row < SIDE, rolled(tile, -k, 0), rolled(tile, k, 0))


def mixed(row, base, inner):
    for k, tile in inner:
        base = jnp.where((row == k) | (row == TILE - 1 - k), put(row, tile, k), base)
    return base


def joined(a, b):
    return jnp.concatenate([a, b], axis=0)


def own_parts(refs, row):
    flat, cot_y = {}, {}
    for y in range(ROWS):
        flat[y] = -(dx(cot_frame(refs, row, 0, y)) + along_z_cot(refs, row, cot_frame(refs, row, 2, y), y))
        cot_y[y] = cot_frame(refs, row, 1, y)
    return flat, cot_y


def paired(place_ref, to_prev, to_next, first_ref, second_ref):
    even = lax.rem(place_ref[0], 2) == 0
    for k in range(first_ref.shape[0]):
        first_ref[k] = jnp.where(even, to_prev[k], to_next[k])
        second_ref[k] = jnp.where(even, to_next[k], to_prev[k])


def unpaired(place_ref, first_ref, second_ref):
    even = lax.rem(place_ref[0], 2) == 0
    tiles = range(first_ref.shape[0])
    after = [jnp.where(even, second_ref[k], first_ref[k]) for k in tiles]
    before = [jnp.where(even, first_ref[k], second_ref[k]) for k in tiles]
    return after, before


def pack_y(odd_ref, place_ref, cot_ref, vel_ref, cross_ref, core_ref, first_ref, second_ref, zn_ref, zp_ref):
    even = odd_ref[0] == 0
    for c in range(3):
        for y in range(ROWS):
            cross, core = cross_ref[c, y], core_ref[c, y]
            zn_ref[c, y] = jnp.where(even, core, cross)
            zp_ref[c, y] = jnp.where(even, cross, core)
    refs = (cot_ref, vel_ref, zn_ref, zp_ref)
    row = sublane()
    flat, cot_y = own_parts(refs, row)
    low = flat[0] - 0.5 * cot_y[1]
    high = flat[3] + 0.5 * cot_y[2]
    one = flat[1] - 0.5 * (cot_y[2] - cot_y[0])
    two = flat[2] - 0.5 * (cot_y[3] - cot_y[1])
    to_prev, to_next = [], []
    for out, part, edge in ((to_prev, (low, one, two), 0), (to_next, (high, two, one), 3)):
        side_x = side_cot(row, zn_ref[0, edge], zp_ref[0, edge])
        side_z = side_cot(row, zn_ref[2, edge], zp_ref[2, edge])
        out.append(part[0][:TILE])
        out.append(part[1][:TILE])
        out.append(cot_y[edge][:TILE])
        out.append(mixed(row, part[0][TILE:], [(3, part[2][TILE:])]))
        out.append(mixed(row, part[1][TILE:], [(2, side_x), (3, side_z)]))
        out.append(cot_y[edge][TILE:])
    paired(place_ref, to_prev, to_next, first_ref, second_ref)


def pack_late(place_ref, refs, row, b, first_ref, second_ref):
    cot_ref, vel_ref, zn_ref, zp_ref = refs
    to_prev, to_next = [], []
    for out, d1, d2, d3, d4 in ((to_prev, 0, 1, 2, 3), (to_next, 3, 2, 1, 0)):
        out += [b[d3][:TILE], b[d4][:TILE], cot_ref[0, d1], cot_ref[2, d1]]
        out += [cot_ref[c, d2] for c in range(3)]
        out += [vel_ref[c, d1] for c in range(3)]
        out += [vel_ref[c, d2] for c in range(3)]
        vel = [side_vel(row, zn_ref[c, d1], zp_ref[c, d1]) for c in range(3)]
        out.append(mixed(row, vel[0], [(1, vel[1]), (2, vel[2])]))
    paired(place_ref, to_prev, to_next, first_ref, second_ref)


def cot_frame(refs, row, c, y):
    cot_ref, _, zn_ref, zp_ref = refs
    return joined(cot_ref[c, y], side_cot(row, zn_ref[c, y], zp_ref[c, y]))


def vel_frame(refs, row, c, y):
    _, vel_ref, zn_ref, zp_ref = refs
    return joined(vel_ref[c, y], side_vel(row, zn_ref[c, y], zp_ref[c, y]))


def along_z_cot(refs, row, frame, y):
    if not 0 <= y < ROWS:
        return dz(frame)
    zn_ref, zp_ref = refs[2], refs[3]
    ends = jnp.where(row < SIDE, zp_ref[2, y], zn_ref[2, y])
    wide = lax.broadcasted_iota(jnp.int32, (WIDE, 256), 0)
    both = joined(ends, ends)
    after = jnp.where(wide == TILE + 3, rolled(both, -1, 0), rolled(frame, -1, 0))
    before = jnp.where(wide == TILE + 4, rolled(both, 1, 0), rolled(frame, 1, 0))
    return 0.5 * (after - before)


def laplace(here, below, above):
    beside = rolled(here, 1, 1) + rolled(here, -1, 1)
    beside = beside + above + below
    beside = beside + rolled(here, 1, 0) + rolled(here, -1, 0)
    return 6.0 * here - beside


def ratio(top, bottom):
    safe = bottom > 0.0
    return jnp.where(safe, top / jnp.where(safe, bottom, 1.0), 0.0)


def total(x):
    return jnp.sum(jnp.sum(x, axis=0, keepdims=True), axis=1, keepdims=True)


def moments(
    place_ref,
    cot_ref,
    vel_ref,
    zn_ref,
    zp_ref,
    first_ref,
    second_ref,
    out_ref,
    b_ref,
    w_ref,
    late1_ref,
    late2_ref,
):
    refs = (cot_ref, vel_ref, zn_ref, zp_ref)
    row = sublane()
    after, before = unpaired(place_ref, first_ref, second_ref)
    flat, cot_y = own_parts(refs, row)
    cot_y[-1], cot_y[4] = joined(before[2], before[5]), joined(after[2], after[5])
    b = {y: flat[y] - 0.5 * (cot_y[y + 1] - cot_y[y - 1]) for y in range(ROWS)}
    b[-1] = joined(before[0], before[3]) - 0.5 * cot_y[0]
    b[4] = joined(after[0], after[3]) + 0.5 * cot_y[3]
    b[-2] = joined(before[1], before[4])
    b[5] = joined(after[1], after[4])
    w = {y: laplace(b[y], b[y - 1], b[y + 1]) for y in range(-1, 5)}
    m0 = m1 = None
    for y in range(ROWS):
        bc, wc = b[y][:TILE], w[y][:TILE]
        m0 = bc * bc if m0 is None else m0 + bc * bc
        m1 = bc * wc if m1 is None else m1 + bc * wc
    m0, m1 = total(m0), total(m1)
    sigma = ratio(m1, m0)
    spread = third = cross = None
    for y in range(ROWS):
        bc, wc = b[y][:TILE], w[y][:TILE]
        x = laplace(w[y], w[y - 1], w[y + 1])[:TILE]
        v = wc - sigma * bc
        u = x - sigma * wc
        spread = v * v if spread is None else spread + v * v
        third = v * u if third is None else third + v * u
        cross = bc * u if cross is None else cross + bc * u
    spread, third, cross = total(spread), total(third), total(cross)
    spread_out((m0, m1, spread, third, cross), out_ref)
    for y in range(-2, 6):
        b_ref[y + 2] = b[y]
    for y in range(-1, 5):
        w_ref[y + 1] = w[y]
    pack_late(place_ref, refs, row, b, late1_ref, late2_ref)


def spread_out(parts, out_ref):
    lane = lax.broadcasted_iota(jnp.int32, (1, 128), 1)
    line = jnp.zeros((1, 128), jnp.float32)
    for k, value in enumerate(parts):
        line = jnp.where(lane == k, value, line)
    for j in range(out_ref.shape[0]):
        out_ref[j] = line


def gathered(got_ref):
    lines = got_ref[...].reshape(got_ref.shape[0], 128)
    return [x[:, :1] for x in merged(*[rolled(lines, -k, 1) for k in range(5)])]


def merged(m0, m1, spread, third, cross):
    own = ratio(m1, m0)

    def over(x):
        return jnp.sum(x, axis=0, keepdims=True)

    all0, all1 = over(m0), over(m1)
    delta = ratio(all1, all0) - own
    all_spread = over(spread + delta * delta * m0)
    all_third = over(third - delta * (spread + cross) + delta * delta * m1)
    all_cross = over(cross - delta * m1)
    return all0, all1, all_spread, all_third, all_cross


def merge(got_ref, out_ref):
    spread_out(gathered(got_ref), out_ref)


def slope(vel, y, grad_ref, inverse_ref, at):
    grad = [[dx(vel[i, y]), 0.5 * (vel[i, y + 1] - vel[i, y - 1]), dz(vel[i, y])] for i in range(3)]
    inside = None
    for i in range(3):
        for j in range(3):
            grad_ref[at, 3 * i + j] = grad[i][j]
        for j in range(i + 1):
            strain = grad[i][i] if i == j else 0.5 * (grad[i][j] + grad[j][i])
            square = (1.0 if i == j else 2.0) * (strain * strain)
            inside = square if inside is None else inside + square
    inverse_ref[at] = lax.rsqrt(2.0 * inside + strain_floor)


INNER = (1, 2)
OUTER = (-1, 0, 3, 4)


def inner_slopes(cot_ref, vel_ref, zn_ref, zp_ref, lines_ref, grad_ref, inverse_ref):
    refs = (cot_ref, vel_ref, zn_ref, zp_ref)
    row = sublane()
    vel = {(c, y): vel_frame(refs, row, c, y) for c in range(3) for y in range(ROWS)}
    for at, y in enumerate(INNER):
        slope(vel, y, grad_ref, inverse_ref, at)


def outer_slopes(place_ref, cot_ref, vel_ref, zn_ref, zp_ref, late1_ref, late2_ref, grad_ref, inverse_ref):
    refs = (cot_ref, vel_ref, zn_ref, zp_ref)
    row = sublane()
    vel = {(c, y): vel_frame(refs, row, c, y) for c in range(3) for y in range(ROWS)}
    late = unpaired(place_ref, late1_ref, late2_ref)
    for got, edge, step in ((late[0], ROWS - 1, 1), (late[1], 0, -1)):
        for c in range(3):
            vel[c, edge + step] = joined(got[7 + c], take(row, got[13], c))
            vel[c, edge + 2 * step] = joined(got[10 + c], got[10 + c])
    for at, y in enumerate(OUTER):
        slope(vel, y, grad_ref, inverse_ref, at)


def finish(
    place_ref,
    cot_ref,
    vel_ref,
    zn_ref,
    zp_ref,
    first_ref,
    second_ref,
    late1_ref,
    late2_ref,
    b_ref,
    w_ref,
    inner_grad_ref,
    inner_inverse_ref,
    outer_grad_ref,
    outer_inverse_ref,
    sums_ref,
    out_ref,
):
    refs = (cot_ref, vel_ref, zn_ref, zp_ref)
    row = sublane()
    m0, m1, spread, third, _ = gathered(sums_ref)
    step0 = m0 / m1
    norm1 = step0 * step0 * spread
    beta = norm1 / m0
    bend = step0 * step0 * third - 2.0 * step0 * beta * spread + beta * beta * m1
    step1 = norm1 / bend
    coef_b = step0 + step1 * (1.0 + beta)
    coef_w = -(step1 * step0)

    b = {y: b_ref[y + 2] for y in range(-2, 6)}
    w = {y: w_ref[y + 1] for y in range(-1, 5)}
    cot = {(c, y): cot_frame(refs, row, c, y) for c in range(3) for y in range(ROWS)}
    vel = {(c, y): vel_frame(refs, row, c, y) for c in range(3) for y in range(ROWS)}
    soon = unpaired(place_ref, first_ref, second_ref)
    late = unpaired(place_ref, late1_ref, late2_ref)
    for side, edge, step in ((0, ROWS - 1, 1), (1, 0, -1)):
        near, got = soon[side], late[side]
        y1, y2, y3, y4 = [edge + step * d for d in range(1, 5)]
        b[y3] = joined(got[0], take(row, near[3], 3))
        b[y4] = joined(got[1], got[1])
        cot[0, y1] = joined(got[2], take(row, near[4], 2))
        cot[1, y1] = joined(near[2], near[5])
        cot[2, y1] = joined(got[3], take(row, near[4], 3))
        for c in range(3):
            cot[c, y2] = joined(got[4 + c], got[4 + c])
            vel[c, y1] = joined(got[7 + c], take(row, got[13], c))
            vel[c, y2] = joined(got[10 + c], got[10 + c])
    for y in (-3, -2, 5, 6):
        w[y] = laplace(b[y], b[y - 1], b[y + 1])
    p = {y: coef_b * b[y] + coef_w * w[y] for y in range(-3, 7)}
    lam = {}
    for y in range(-2, 6):
        lam[0, y] = cot[0, y] - dx(p[y])
        lam[1, y] = cot[1, y] - 0.5 * (p[y + 1] - p[y - 1])
        lam[2, y] = cot[2, y] - dz(p[y])

    flat, upright = {}, {}
    for y in range(-1, 5):
        grad_ref, inverse_ref, rows = (
            (inner_grad_ref, inner_inverse_ref, INNER)
            if y in INNER
            else (outer_grad_ref, outer_inverse_ref, OUTER)
        )
        at = rows.index(y)
        grad = [[grad_ref[at, 3 * i + j] for j in range(3)] for i in range(3)]
        pull = [[dx(lam[i, y]), 0.5 * (lam[i, y + 1] - lam[i, y - 1]), dz(lam[i, y])] for i in range(3)]
        strain, ebb = {}, {}
        for i in range(3):
            for j in range(i + 1):
                strain[i, j] = grad[i][i] if i == j else 0.5 * (grad[i][j] + grad[j][i])
                ebb[i, j] = pull[i][i] if i == j else 0.5 * (pull[i][j] + pull[j][i])
        work = strain[0, 0] * ebb[0, 0] + strain[1, 1] * ebb[1, 1] + strain[2, 2] * ebb[2, 2]
        off_work = strain[1, 0] * ebb[1, 0] + strain[2, 0] * ebb[2, 0] + strain[2, 1] * ebb[2, 1]
        inverse = inverse_ref[at]
        twice = (2.0 * smag_coef) / inverse
        factor = (4.0 * smag_coef) * inverse * (work + 2.0 * off_work)
        stress = {key: twice * ebb[key] + factor * strain[key] for key in strain}

        def both(i, j):
            return stress[max(i, j), min(i, j)] + lam[i, y] * vel[j, y]

        for i in range(3):
            upright[i, y] = both(i, 1)[:TILE]
        if 0 <= y < ROWS:
            for i in range(3):
                carried = lam[0, y] * grad[0][i] + lam[1, y] * grad[1][i] + lam[2, y] * grad[2][i]
                level = dx(both(i, 0)) + dz(both(i, 2))
                flat[i, y] = (lam[i, y] + time_step * (level - carried))[:TILE]
    for i in range(3):
        for y in range(ROWS):
            out_ref[i, y] = flat[i, y] + (0.5 * time_step) * (upright[i, y + 1] - upright[i, y - 1])


def call(kernel, outs, scalars, arrays, cost=None):
    vmem = pl.BlockSpec(memory_space=pltpu.VMEM)
    smem = pl.BlockSpec(memory_space=pltpu.SMEM)
    return pl.pallas_call(
        kernel,
        out_shape=[jax.ShapeDtypeStruct(s, jnp.float32) for s in outs],
        in_specs=[smem] * len(scalars) + [vmem] * len(arrays),
        out_specs=[vmem] * len(outs),
        cost_estimate=cost and pl.CostEstimate(flops=cost, bytes_accessed=2_000_000, transcendentals=100_000),
        compiler_params=pltpu.CompilerParams(vmem_limit_bytes=32 * 1024 * 1024),
    )(*scalars, *arrays)


PY = ("y_low", "z")
PZ = ("y_high", "x", "core")
STEPS = (("z", "core"), ("y_high", "y_low", "x"))


def to_all(rows, axes):
    sizes = [lax.axis_size(axis) for axis in axes]
    order = [0]
    for at, n in enumerate(sizes):
        middle = 0 if at else n // 2
        order = [i * n + (k + middle) % n for i in order for k in range(n)]
    return lax.all_to_all(rows, axes, 0, 0, axis_index_groups=[order])


def size(axes):
    return math.prod(lax.axis_size(axis) for axis in axes)


def swap_across(x, axes):
    n = size(axes)
    return lax.ppermute(x, axes, [(i, (i + 1 if i % 2 else i - 1) % n) for i in range(n)])


def swap_within(x, axes):
    return lax.ppermute(x, axes, [(i, i ^ 1) for i in range(size(axes))])


def body(velocity, cotangent):
    place = lax.axis_index(PY).astype(jnp.int32).reshape(1)
    odd = lax.axis_index("core").astype(jnp.int32).reshape(1)
    block = (3, ROWS, TILE, 256)
    cross, core, cotangent, velocity = call(
        pack_z, [block] * 4, [odd], [jnp.concatenate([cotangent, velocity], axis=0)]
    )
    cross = swap_across(cross, PZ)
    core = swap_within(core, PZ)
    soon, later = (SOON, TILE, 256), (LATE, TILE, 256)
    first, second, zn, zp = call(
        pack_y, [soon, soon, block, block], [odd, place], [cotangent, velocity, cross, core]
    )
    held = [cotangent, velocity, zn, zp, swap_across(first, PY), swap_within(second, PY)]
    lines, b, w, late1, late2 = call(
        moments,
        [(size(STEPS[0]), 1, 128), (8, WIDE, 256), (6, WIDE, 256), later, later],
        [place],
        held,
    )
    got = lax.all_to_all(lines, STEPS[0], 0, 0)
    late = [swap_across(late1, PY), swap_within(late2, PY)]
    inner = call(inner_slopes, [(2, 9, WIDE, 256), (2, WIDE, 256)], [], held[:4] + [lines], 4_000_000_000)
    outer = call(outer_slopes, [(4, 9, WIDE, 256), (4, WIDE, 256)], [place], held[:4] + late, 4_000_000)
    (lines,) = call(merge, [(size(STEPS[1]), 1, 128)], [], [got])
    sums = to_all(lines, STEPS[1])
    (out,) = call(finish, [block], [place], held + late + [b, w, *inner, *outer, sums])
    return out


def solution(mesh):
    ny, nz = mesh.shape["py"], mesh.shape["pz"]
    x = min(8, nz // 2)
    shape = (2, ny // 2, nz // (2 * x), x, 2)
    names = ("y_low", "z", "y_high", "x", "core")
    fine = jax.sharding.Mesh(mesh.devices.reshape(shape), names)
    placed = P(None, PY, PZ, None)
    return jax.shard_map(body, mesh=fine, in_specs=(placed, placed), out_specs=placed, check_vma=False)
```

```python
import math

import jax
import jax.numpy as jnp
from jax import lax
from jax.experimental import pallas as pl
from jax.experimental.pallas import tpu as pltpu
from jax.sharding import PartitionSpec as P

smag_coef = 0.1156
time_step = 0.2
strain_floor = 0.25

ROWS = 4
TILE = 8
SIDE = 4
WIDE = TILE + 2 * SIDE
SOON = 6
LATE = 14


def rolled(x, shift, axis):
    return pltpu.roll(x, shift % x.shape[axis], axis)


def dx(f):
    n = f.ndim - 1
    return 0.5 * (rolled(f, -1, n) - rolled(f, 1, n))


def dz(f):
    n = f.ndim - 2
    return 0.5 * (rolled(f, -1, n) - rolled(f, 1, n))


def sublane():
    return lax.broadcasted_iota(jnp.int32, (TILE, 256), 0)


def pack_z(odd_ref, both_ref, cross_ref, core_ref, cot_ref, vel_ref):
    row = sublane()
    even = odd_ref[0] == 0
    for c in range(3):
        for y in range(ROWS):
            cot, vel = both_ref[c, y], both_ref[3 + c, y]
            cot_ref[c, y], vel_ref[c, y] = cot, vel
            to_prev = jnp.where(row < 5, cot, rolled(vel, 5, 0))
            to_next = jnp.where(row >= 3, cot, rolled(vel, 3, 0))
            cross_ref[c, y] = jnp.where(even, to_prev, to_next)
            core_ref[c, y] = jnp.where(even, to_next, to_prev)


def side_cot(row, zn, zp):
    return jnp.where(row < SIDE, zn, zp)


def side_vel(row, zn, zp):
    return jnp.where(row < SIDE, rolled(zn, 3, 0), rolled(zp, 5, 0))


def put(row, tile, k):
    return jnp.where(row < SIDE, rolled(tile, k, 0), rolled(tile, -k, 0))


def take(row, tile, k):
    return jnp.where(row < SIDE, rolled(tile, -k, 0), rolled(tile, k, 0))


def mixed(row, base, inner):
    for k, tile in inner:
        base = jnp.where((row == k) | (row == TILE - 1 - k), put(row, tile, k), base)
    return base


def joined(a, b):
    return jnp.concatenate([a, b], axis=0)


def own_parts(refs, row):
    flat, cot_y = {}, {}
    for y in range(ROWS):
        flat[y] = -(dx(cot_frame(refs, row, 0, y)) + along_z_cot(refs, row, cot_frame(refs, row, 2, y), y))
        cot_y[y] = cot_frame(refs, row, 1, y)
    return flat, cot_y


def paired(place_ref, to_prev, to_next, first_ref, second_ref):
    even = lax.rem(place_ref[0], 2) == 0
    for k in range(first_ref.shape[0]):
        first_ref[k] = jnp.where(even, to_prev[k], to_next[k])
        second_ref[k] = jnp.where(even, to_next[k], to_prev[k])


def unpaired(place_ref, first_ref, second_ref):
    even = lax.rem(place_ref[0], 2) == 0
    tiles = range(first_ref.shape[0])
    after = [jnp.where(even, second_ref[k], first_ref[k]) for k in tiles]
    before = [jnp.where(even, first_ref[k], second_ref[k]) for k in tiles]
    return after, before


def pack_y(odd_ref, place_ref, cot_ref, vel_ref, cross_ref, core_ref, first_ref, second_ref, zn_ref, zp_ref):
    even = odd_ref[0] == 0
    for c in range(3):
        for y in range(ROWS):
            cross, core = cross_ref[c, y], core_ref[c, y]
            zn_ref[c, y] = jnp.where(even, core, cross)
            zp_ref[c, y] = jnp.where(even, cross, core)
    refs = (cot_ref, vel_ref, zn_ref, zp_ref)
    row = sublane()
    flat, cot_y = own_parts(refs, row)
    low = flat[0] - 0.5 * cot_y[1]
    high = flat[3] + 0.5 * cot_y[2]
    one = flat[1] - 0.5 * (cot_y[2] - cot_y[0])
    two = flat[2] - 0.5 * (cot_y[3] - cot_y[1])
    to_prev, to_next = [], []
    for out, part, edge in ((to_prev, (low, one, two), 0), (to_next, (high, two, one), 3)):
        side_x = side_cot(row, zn_ref[0, edge], zp_ref[0, edge])
        side_z = side_cot(row, zn_ref[2, edge], zp_ref[2, edge])
        out.append(part[0][:TILE])
        out.append(part[1][:TILE])
        out.append(cot_y[edge][:TILE])
        out.append(mixed(row, part[0][TILE:], [(3, part[2][TILE:])]))
        out.append(mixed(row, part[1][TILE:], [(2, side_x), (3, side_z)]))
        out.append(cot_y[edge][TILE:])
    paired(place_ref, to_prev, to_next, first_ref, second_ref)


def pack_late(place_ref, refs, row, b, first_ref, second_ref):
    cot_ref, vel_ref, zn_ref, zp_ref = refs
    to_prev, to_next = [], []
    for out, d1, d2, d3, d4 in ((to_prev, 0, 1, 2, 3), (to_next, 3, 2, 1, 0)):
        out += [b[d3][:TILE], b[d4][:TILE], cot_ref[0, d1], cot_ref[2, d1]]
        out += [cot_ref[c, d2] for c in range(3)]
        out += [vel_ref[c, d1] for c in range(3)]
        out += [vel_ref[c, d2] for c in range(3)]
        vel = [side_vel(row, zn_ref[c, d1], zp_ref[c, d1]) for c in range(3)]
        out.append(mixed(row, vel[0], [(1, vel[1]), (2, vel[2])]))
    paired(place_ref, to_prev, to_next, first_ref, second_ref)


def cot_frame(refs, row, c, y):
    cot_ref, _, zn_ref, zp_ref = refs
    return joined(cot_ref[c, y], side_cot(row, zn_ref[c, y], zp_ref[c, y]))


def vel_frame(refs, row, c, y):
    _, vel_ref, zn_ref, zp_ref = refs
    return joined(vel_ref[c, y], side_vel(row, zn_ref[c, y], zp_ref[c, y]))


def along_z_cot(refs, row, frame, y):
    if not 0 <= y < ROWS:
        return dz(frame)
    zn_ref, zp_ref = refs[2], refs[3]
    ends = jnp.where(row < SIDE, zp_ref[2, y], zn_ref[2, y])
    wide = lax.broadcasted_iota(jnp.int32, (WIDE, 256), 0)
    both = joined(ends, ends)
    after = jnp.where(wide == TILE + 3, rolled(both, -1, 0), rolled(frame, -1, 0))
    before = jnp.where(wide == TILE + 4, rolled(both, 1, 0), rolled(frame, 1, 0))
    return 0.5 * (after - before)


def laplace(here, below, above):
    beside = rolled(here, 1, 1) + rolled(here, -1, 1)
    beside = beside + above + below
    beside = beside + rolled(here, 1, 0) + rolled(here, -1, 0)
    return 6.0 * here - beside


def ratio(top, bottom):
    safe = bottom > 0.0
    return jnp.where(safe, top / jnp.where(safe, bottom, 1.0), 0.0)


def total(x):
    return jnp.sum(jnp.sum(x, axis=0, keepdims=True), axis=1, keepdims=True)


def moments(
    place_ref,
    cot_ref,
    vel_ref,
    zn_ref,
    zp_ref,
    first_ref,
    second_ref,
    out_ref,
    b_ref,
    w_ref,
    late1_ref,
    late2_ref,
):
    refs = (cot_ref, vel_ref, zn_ref, zp_ref)
    row = sublane()
    after, before = unpaired(place_ref, first_ref, second_ref)
    flat, cot_y = own_parts(refs, row)
    cot_y[-1], cot_y[4] = joined(before[2], before[5]), joined(after[2], after[5])
    b = {y: flat[y] - 0.5 * (cot_y[y + 1] - cot_y[y - 1]) for y in range(ROWS)}
    b[-1] = joined(before[0], before[3]) - 0.5 * cot_y[0]
    b[4] = joined(after[0], after[3]) + 0.5 * cot_y[3]
    b[-2] = joined(before[1], before[4])
    b[5] = joined(after[1], after[4])
    w = {y: laplace(b[y], b[y - 1], b[y + 1]) for y in range(-1, 5)}
    m0 = m1 = None
    for y in range(ROWS):
        bc, wc = b[y][:TILE], w[y][:TILE]
        m0 = bc * bc if m0 is None else m0 + bc * bc
        m1 = bc * wc if m1 is None else m1 + bc * wc
    m0, m1 = total(m0), total(m1)
    sigma = ratio(m1, m0)
    spread = third = cross = None
    for y in range(ROWS):
        bc, wc = b[y][:TILE], w[y][:TILE]
        x = laplace(w[y], w[y - 1], w[y + 1])[:TILE]
        v = wc - sigma * bc
        u = x - sigma * wc
        spread = v * v if spread is None else spread + v * v
        third = v * u if third is None else third + v * u
        cross = bc * u if cross is None else cross + bc * u
    spread, third, cross = total(spread), total(third), total(cross)
    spread_out((m0, m1, spread, third, cross), out_ref)
    for y in range(-2, 6):
        b_ref[y + 2] = b[y]
    for y in range(-1, 5):
        w_ref[y + 1] = w[y]
    pack_late(place_ref, refs, row, b, late1_ref, late2_ref)


def spread_out(parts, out_ref):
    lane = lax.broadcasted_iota(jnp.int32, (1, 128), 1)
    line = jnp.zeros((1, 128), jnp.float32)
    for k, value in enumerate(parts):
        line = jnp.where(lane == k, value, line)
    for j in range(out_ref.shape[0]):
        out_ref[j] = line


def gathered(got_ref):
    lines = got_ref[...].reshape(got_ref.shape[0], 128)
    return [x[:, :1] for x in merged(*[rolled(lines, -k, 1) for k in range(5)])]


def merged(m0, m1, spread, third, cross):
    own = ratio(m1, m0)

    def over(x):
        return jnp.sum(x, axis=0, keepdims=True)

    all0, all1 = over(m0), over(m1)
    delta = ratio(all1, all0) - own
    all_spread = over(spread + delta * delta * m0)
    all_third = over(third - delta * (spread + cross) + delta * delta * m1)
    all_cross = over(cross - delta * m1)
    return all0, all1, all_spread, all_third, all_cross


def merge(got_ref, out_ref):
    spread_out(gathered(got_ref), out_ref)


def slope(vel, y, grad_ref, inverse_ref, at):
    grad = [[dx(vel[i, y]), 0.5 * (vel[i, y + 1] - vel[i, y - 1]), dz(vel[i, y])] for i in range(3)]
    inside = None
    for i in range(3):
        for j in range(3):
            grad_ref[at, 3 * i + j] = grad[i][j]
        for j in range(i + 1):
            strain = grad[i][i] if i == j else 0.5 * (grad[i][j] + grad[j][i])
            square = (1.0 if i == j else 2.0) * (strain * strain)
            inside = square if inside is None else inside + square
    inverse_ref[at] = lax.rsqrt(2.0 * inside + strain_floor)


INNER = (1, 2)
OUTER = (-1, 0, 3, 4)


def inner_slopes(cot_ref, vel_ref, zn_ref, zp_ref, lines_ref, grad_ref, inverse_ref):
    refs = (cot_ref, vel_ref, zn_ref, zp_ref)
    row = sublane()
    vel = {(c, y): vel_frame(refs, row, c, y) for c in range(3) for y in range(ROWS)}
    for at, y in enumerate(INNER):
        slope(vel, y, grad_ref, inverse_ref, at)


def outer_slopes(place_ref, cot_ref, vel_ref, zn_ref, zp_ref, late1_ref, late2_ref, grad_ref, inverse_ref):
    refs = (cot_ref, vel_ref, zn_ref, zp_ref)
    row = sublane()
    vel = {(c, y): vel_frame(refs, row, c, y) for c in range(3) for y in range(ROWS)}
    late = unpaired(place_ref, late1_ref, late2_ref)
    for got, edge, step in ((late[0], ROWS - 1, 1), (late[1], 0, -1)):
        for c in range(3):
            vel[c, edge + step] = joined(got[7 + c], take(row, got[13], c))
            vel[c, edge + 2 * step] = joined(got[10 + c], got[10 + c])
    for at, y in enumerate(OUTER):
        slope(vel, y, grad_ref, inverse_ref, at)


def finish(
    place_ref,
    cot_ref,
    vel_ref,
    zn_ref,
    zp_ref,
    first_ref,
    second_ref,
    late1_ref,
    late2_ref,
    b_ref,
    w_ref,
    inner_grad_ref,
    inner_inverse_ref,
    outer_grad_ref,
    outer_inverse_ref,
    sums_ref,
    out_ref,
):
    refs = (cot_ref, vel_ref, zn_ref, zp_ref)
    row = sublane()
    m0, m1, spread, third, _ = gathered(sums_ref)
    step0 = m0 / m1
    norm1 = step0 * step0 * spread
    beta = norm1 / m0
    bend = step0 * step0 * third - 2.0 * step0 * beta * spread + beta * beta * m1
    step1 = norm1 / bend
    coef_b = step0 + step1 * (1.0 + beta)
    coef_w = -(step1 * step0)

    b = {y: b_ref[y + 2] for y in range(-2, 6)}
    w = {y: w_ref[y + 1] for y in range(-1, 5)}
    cot = {(c, y): cot_frame(refs, row, c, y) for c in range(3) for y in range(ROWS)}
    vel = {(c, y): vel_frame(refs, row, c, y) for c in range(3) for y in range(ROWS)}
    soon = unpaired(place_ref, first_ref, second_ref)
    late = unpaired(place_ref, late1_ref, late2_ref)
    for side, edge, step in ((0, ROWS - 1, 1), (1, 0, -1)):
        near, got = soon[side], late[side]
        y1, y2, y3, y4 = [edge + step * d for d in range(1, 5)]
        b[y3] = joined(got[0], take(row, near[3], 3))
        b[y4] = joined(got[1], got[1])
        cot[0, y1] = joined(got[2], take(row, near[4], 2))
        cot[1, y1] = joined(near[2], near[5])
        cot[2, y1] = joined(got[3], take(row, near[4], 3))
        for c in range(3):
            cot[c, y2] = joined(got[4 + c], got[4 + c])
            vel[c, y1] = joined(got[7 + c], take(row, got[13], c))
            vel[c, y2] = joined(got[10 + c], got[10 + c])
    for y in (-3, -2, 5, 6):
        w[y] = laplace(b[y], b[y - 1], b[y + 1])
    p = {y: coef_b * b[y] + coef_w * w[y] for y in range(-3, 7)}
    lam = {}
    for y in range(-2, 6):
        lam[0, y] = cot[0, y] - dx(p[y])
        lam[1, y] = cot[1, y] - 0.5 * (p[y + 1] - p[y - 1])
        lam[2, y] = cot[2, y] - dz(p[y])

    flat, upright = {}, {}
    for y in range(-1, 5):
        grad_ref, inverse_ref, rows = (
            (inner_grad_ref, inner_inverse_ref, INNER)
            if y in INNER
            else (outer_grad_ref, outer_inverse_ref, OUTER)
        )
        at = rows.index(y)
        grad = [[grad_ref[at, 3 * i + j] for j in range(3)] for i in range(3)]
        pull = [[dx(lam[i, y]), 0.5 * (lam[i, y + 1] - lam[i, y - 1]), dz(lam[i, y])] for i in range(3)]
        strain, ebb = {}, {}
        for i in range(3):
            for j in range(i + 1):
                strain[i, j] = grad[i][i] if i == j else 0.5 * (grad[i][j] + grad[j][i])
                ebb[i, j] = pull[i][i] if i == j else 0.5 * (pull[i][j] + pull[j][i])
        work = strain[0, 0] * ebb[0, 0] + strain[1, 1] * ebb[1, 1] + strain[2, 2] * ebb[2, 2]
        off_work = strain[1, 0] * ebb[1, 0] + strain[2, 0] * ebb[2, 0] + strain[2, 1] * ebb[2, 1]
        inverse = inverse_ref[at]
        twice = (2.0 * smag_coef) / inverse
        factor = (4.0 * smag_coef) * inverse * (work + 2.0 * off_work)
        stress = {key: twice * ebb[key] + factor * strain[key] for key in strain}

        def both(i, j):
            return stress[max(i, j), min(i, j)] + lam[i, y] * vel[j, y]

        for i in range(3):
            upright[i, y] = both(i, 1)[:TILE]
        if 0 <= y < ROWS:
            for i in range(3):
                carried = lam[0, y] * grad[0][i] + lam[1, y] * grad[1][i] + lam[2, y] * grad[2][i]
                level = dx(both(i, 0)) + dz(both(i, 2))
                flat[i, y] = (lam[i, y] + time_step * (level - carried))[:TILE]
    for i in range(3):
        for y in range(ROWS):
            out_ref[i, y] = flat[i, y] + (0.5 * time_step) * (upright[i, y + 1] - upright[i, y - 1])


def call(kernel, outs, scalars, arrays, cost=None):
    vmem = pl.BlockSpec(memory_space=pltpu.VMEM)
    smem = pl.BlockSpec(memory_space=pltpu.SMEM)
    return pl.pallas_call(
        kernel,
        out_shape=[jax.ShapeDtypeStruct(s, jnp.float32) for s in outs],
        in_specs=[smem] * len(scalars) + [vmem] * len(arrays),
        out_specs=[vmem] * len(outs),
        cost_estimate=cost and pl.CostEstimate(flops=cost, bytes_accessed=2_000_000, transcendentals=100_000),
        compiler_params=pltpu.CompilerParams(vmem_limit_bytes=32 * 1024 * 1024),
    )(*scalars, *arrays)


PY = ("y_low", "z")
PZ = ("y_high", "x", "core")
STEPS = (("z", "core"), ("y_high", "y_low", "x"))


def to_all(rows, axes):
    sizes = [lax.axis_size(axis) for axis in axes]
    order = [0]
    for at, n in enumerate(sizes):
        middle = n // 2 if at == len(sizes) - 1 else 0
        order = [i * n + (k + middle) % n for i in order for k in range(n)]
    return lax.all_to_all(rows, axes, 0, 0, axis_index_groups=[order])


def size(axes):
    return math.prod(lax.axis_size(axis) for axis in axes)


def swap_across(x, axes):
    n = size(axes)
    return lax.ppermute(x, axes, [(i, (i + 1 if i % 2 else i - 1) % n) for i in range(n)])


def swap_within(x, axes):
    return lax.ppermute(x, axes, [(i, i ^ 1) for i in range(size(axes))])


def body(velocity, cotangent):
    place = lax.axis_index(PY).astype(jnp.int32).reshape(1)
    odd = lax.axis_index("core").astype(jnp.int32).reshape(1)
    block = (3, ROWS, TILE, 256)
    cross, core, cotangent, velocity = call(
        pack_z, [block] * 4, [odd], [jnp.concatenate([cotangent, velocity], axis=0)]
    )
    cross = swap_across(cross, PZ)
    core = swap_within(core, PZ)
    soon, later = (SOON, TILE, 256), (LATE, TILE, 256)
    first, second, zn, zp = call(
        pack_y, [soon, soon, block, block], [odd, place], [cotangent, velocity, cross, core]
    )
    held = [cotangent, velocity, zn, zp, swap_across(first, PY), swap_within(second, PY)]
    lines, b, w, late1, late2 = call(
        moments,
        [(size(STEPS[0]), 1, 128), (8, WIDE, 256), (6, WIDE, 256), later, later],
        [place],
        held,
    )
    got = lax.all_to_all(lines, STEPS[0], 0, 0)
    late = [swap_across(late1, PY), swap_within(late2, PY)]
    inner = call(inner_slopes, [(2, 9, WIDE, 256), (2, WIDE, 256)], [], held[:4] + [lines], 4_000_000_000)
    outer = call(outer_slopes, [(4, 9, WIDE, 256), (4, WIDE, 256)], [place], held[:4] + late, 4_000_000)
    (lines,) = call(merge, [(size(STEPS[1]), 1, 128)], [], [got])
    sums = to_all(lines, STEPS[1])
    (out,) = call(finish, [block], [place], held + late + [b, w, *inner, *outer, sums])
    return out


def solution(mesh):
    ny, nz = mesh.shape["py"], mesh.shape["pz"]
    x = min(8, nz // 2)
    shape = (2, ny // 2, nz // (2 * x), x, 2)
    names = ("y_low", "z", "y_high", "x", "core")
    fine = jax.sharding.Mesh(mesh.devices.reshape(shape), names)
    placed = P(None, PY, PZ, None)
    return jax.shard_map(body, mesh=fine, in_specs=(placed, placed), out_specs=placed, check_vma=False)
```
